128 devices in a mesh: replica: 32 (over x, y, core), section: 4 (over z).
Axes of the slice: x: 4, y: 4, z: 4, core: 2. Of those that a mesh axis runs over, the one named last changes fastest.
Arguments:
- acts_in: bfloat16 [4096, 7168], P('replica'), may hold values from -6 to 6
- cotangent: bfloat16 [4096, 7168], P('replica'), may hold values from -6 to 6
- old_blocks: bfloat16 [128, 112, 128, 256], P(('replica', 'section')), may hold values from -6 to 6
- send_slot: int32 [128, 224], P(('replica', 'section')), may hold values from 0 to 111, as said below
- send_dest: int32 [128, 224], P(('replica', 'section')), may hold values from -1 to 127, as said below
- send_block: int32 [128, 224], P(('replica', 'section')), may hold values from 0 to 111, as said below
- old_first: float32 [128, 4, 128, 256], P(('replica', 'section')), may hold values from -6 to 6
- old_second: float32 [128, 4, 128, 256], P(('replica', 'section')), may hold values from 0.5 to 4
- moment_dest: int32 [128, 4], P(('replica', 'section')), may hold values from 0 to 15, as said below
Outputs:
- new_weight: bfloat16 [4, 128, 128, 256], P('section', 'replica')
- new_first: float32 [4, 128, 128, 256], P('section', 'replica')
- new_second: float32 [4, 128, 128, 256], P('section', 'replica')
The draws below stay inside these ranges and needn't reach their ends.
Inputs may be any that keep to these rules, and one draw needn't show every extreme that they name: `send_dest`: device numbers are replica times 4 plus section; -1 marks an empty entry. Every device is named with each block index 0 to 111 exactly once over all devices' lists. No device has more than 2 entries for one destination, and some device has exactly 2 for some destination. One device has no entries; one has 224. `send_slot`: 0 where the entry is empty. `send_block`: 0 where the entry is empty. `moment_dest`: within each replica the 4 x 4 entries are each value once.
All inputs are finite; a program needn't handle non-finite values.
Results may differ from the reference program's by a relative error of at most 0.022.
Values may be sent and summed in bfloat16 or wider, within the bound.
No kernel may reach another device: no remote copies, remote signals or barrier semaphores. Data moves between devices by JAX's collectives and lax.ppermute only.
A program may use at most 192 MiB of HBM per device.

```python
import math
import jax
import jax.numpy as jnp
from jax import lax

D = 7168
FWIN = 256
BLOCK_ROWS = 128
MB_TOK = 64
MICRO = 2
NBLK = 112
GROUP = 1
SENDS = 224
HOLD = 112
OWN_SLOTS = 4
NPAD = 128
TOK_REP = 128
TOKENS = 4096
N_REPLICA = 32
N_SECTION = 4
DEVICES = 128


def route_plan(key):
    key_offsets, key_order, key_lost, key_slot, key_columns = jax.random.split(key, 5)
    group_count = NBLK // GROUP
    half_way = DEVICES // 2
    others = jax.random.permutation(key_offsets, DEVICES - 1).astype(jnp.int32)
    others = jnp.where(others >= half_way, others + 1, others)
    offsets = jnp.concatenate([jnp.full((1,), half_way, jnp.int32), others[:group_count - 1]]).astype(jnp.int32)
    block_order = jax.random.permutation(key_order, NBLK).astype(jnp.int32)
    shift_of = offsets[block_order // GROUP]
    lost_device = jax.random.randint(key_lost, (), 0, DEVICES).astype(jnp.int32)
    offset_gap = (offsets[1] - offsets[0]) % DEVICES
    busiest = (lost_device - offset_gap) % DEVICES
    senders = jnp.arange(DEVICES, dtype=jnp.int32)[:, None]
    own_dest = (senders - shift_of[None, :]) % DEVICES
    own_dest = jnp.where(senders == lost_device, -1, own_dest)
    extra_dest = jnp.broadcast_to(((lost_device - shift_of) % DEVICES)[None, :], (DEVICES, NBLK))
    extra_dest = jnp.where(senders == busiest, extra_dest, -1)
    destinations = jnp.concatenate([own_dest, extra_dest], axis=1).astype(jnp.int32)
    block_ids = jnp.broadcast_to(jnp.concatenate([jnp.arange(NBLK, dtype=jnp.int32), jnp.arange(NBLK, dtype=jnp.int32)])[None, :], (DEVICES, SENDS))
    held_slots = jax.random.randint(key_slot, (DEVICES, SENDS), 0, HOLD).astype(jnp.int32)
    held_slots = jnp.where(destinations >= 0, held_slots, 0)
    block_ids = jnp.where(destinations >= 0, block_ids, 0)
    columns = jax.random.permutation(key_columns, SENDS)
    return (held_slots[:, columns], destinations[:, columns], block_ids[:, columns])


def draw_send_slot(key, part):
    return route_plan(key)[0]


def draw_send_dest(key, part):
    return route_plan(key)[1]


def draw_send_block(key, part):
    return route_plan(key)[2]


def draw_moment_dest(key, part):
    key = jax.random.fold_in(key, 7)
    replica_keys = jax.random.split(key, N_REPLICA)
    shuffled = jax.vmap(lambda one_key: jax.random.permutation(one_key, N_SECTION * OWN_SLOTS))(replica_keys)
    return shuffled.reshape(DEVICES, OWN_SLOTS).astype(jnp.int32)


def shard_levels(key, shape, cuts, least, largest):
    factor_of = 1.0
    for axis_at, shards_of in cuts:
        draws = jax.random.uniform(jax.random.fold_in(jax.random.fold_in(key, 6), axis_at), (shards_of,), jnp.float32, least / len(cuts), largest / len(cuts))
        factor_of = factor_of * jnp.repeat(jnp.exp(draws), shape[axis_at] // shards_of).reshape((-1,) + (1,) * (len(shape) - 1 - axis_at))
    return factor_of


def centred(own_key, shape, deviation, limit, cuts=(), held_as=jnp.bfloat16):
    array = deviation * jax.random.normal(own_key, shape, jnp.float32)
    if cuts:
        array = array * shard_levels(own_key, shape, cuts, -0.22, 0.18)
    return jnp.clip(array, -limit, limit).astype(held_as)


def setup_inputs(seed: int = 0) -> dict:
    keys = jax.random.split(jax.random.key(seed), 10)
    return {
        "acts_in": centred(keys[0], (TOKENS, D), 1.0, 6.0, ((0, 32),)),
        "cotangent": centred(keys[1], (TOKENS, D), 1.0, 6.0, ((0, 32),)),
        "old_blocks": centred(keys[2], (DEVICES, HOLD, BLOCK_ROWS, FWIN), 1.0, 6.0, ((0, 128),)),
        "send_slot": draw_send_slot(jax.random.fold_in(keys[9], 71), 0),
        "send_dest": draw_send_dest(jax.random.fold_in(keys[9], 71), 0),
        "send_block": draw_send_block(jax.random.fold_in(keys[9], 71), 0),
        "old_first": centred(keys[6], (DEVICES, OWN_SLOTS, BLOCK_ROWS, FWIN), 1.0, 6.0, ((0, 128),), jnp.float32),
        "old_second": jnp.clip(jnp.exp(math.log(4.0) - 2.0794415 * jax.random.uniform(keys[7], (DEVICES, OWN_SLOTS, BLOCK_ROWS, FWIN), jnp.float32) ** shard_levels(keys[7], (DEVICES, OWN_SLOTS, BLOCK_ROWS, FWIN), ((0, 128),), -0.2, 0.2)), 0.5, 4.0),
        "moment_dest": draw_moment_dest(jax.random.fold_in(keys[9], 71), 0),
    }


rms_eps = 1e-05
beta_first = 0.9
beta_second = 0.95
step_size = 0.1
adam_eps = 1e-08

def gelu_tanh(values):
    return jax.nn.gelu(values, approximate=True)

def section_forward(layer_in, up_matrix, out_matrix):
    scale_in = up_matrix.shape[0] ** (-0.5)
    scale_out = up_matrix.shape[1] ** (-0.5)
    input_wide = layer_in.astype(jnp.float32)
    root_mean = jnp.sqrt(lax.optimization_barrier(jnp.mean(input_wide * input_wide, axis=-1, keepdims=True)) + rms_eps)
    normed_low = (input_wide / root_mean).astype(jnp.bfloat16)
    pre_act = jnp.dot(normed_low, up_matrix, preferred_element_type=jnp.float32) * scale_in
    activated = gelu_tanh(pre_act).astype(jnp.bfloat16)
    branch = lax.dot_general(activated, out_matrix, (((1,), (1,)), ((), ())), preferred_element_type=jnp.float32)
    return (input_wide + branch * scale_out).astype(jnp.bfloat16)

def section_backward(layer_in, grad_out, up_matrix, out_matrix):
    scale_in = up_matrix.shape[0] ** (-0.5)
    scale_out = up_matrix.shape[1] ** (-0.5)
    input_wide = layer_in.astype(jnp.float32)
    root_mean = jnp.sqrt(lax.optimization_barrier(jnp.mean(input_wide * input_wide, axis=-1, keepdims=True)) + rms_eps)
    normed_wide = input_wide / root_mean
    normed_low = normed_wide.astype(jnp.bfloat16)
    pre_act = jnp.dot(normed_low, up_matrix, preferred_element_type=jnp.float32) * scale_in
    activated = gelu_tanh(pre_act).astype(jnp.bfloat16)
    grad_back = lax.dot_general(grad_out, activated, (((0,), (0,)), ((), ())), preferred_element_type=jnp.float32) * scale_out
    grad_act = jnp.dot(grad_out, out_matrix, preferred_element_type=jnp.float32) * scale_out
    pulled = jax.vjp(gelu_tanh, pre_act)[1](grad_act)[0]
    grad_pre = pulled.astype(jnp.bfloat16)
    grad_up = lax.dot_general(normed_low, grad_pre, (((0,), (0,)), ((), ())), preferred_element_type=jnp.float32) * scale_in
    grad_norm = lax.dot_general(grad_pre, up_matrix, (((1,), (1,)), ((), ())), preferred_element_type=jnp.float32) * scale_in
    correction = lax.optimization_barrier(jnp.mean(grad_norm * normed_wide, axis=-1, keepdims=True))
    grad_in = grad_out.astype(jnp.float32) + (grad_norm - normed_wide * correction) / root_mean
    return (grad_in.astype(jnp.bfloat16), grad_up, grad_back)

def reference(acts_in, cotangent, old_blocks, send_slot, send_dest, send_block, old_first, old_second, moment_dest):
    devices = N_REPLICA * N_SECTION
    flat_dest = send_dest.reshape(-1).astype(jnp.int32)
    flat_block = send_block.reshape(-1).astype(jnp.int32)
    target = jnp.where(flat_dest >= 0, flat_dest * NBLK + flat_block, devices * NBLK).astype(jnp.int32)
    table = jnp.zeros((devices * NBLK + 1,), jnp.int32).at[target].set(jnp.arange(devices * SENDS, dtype=jnp.int32))
    table = table[:devices * NBLK].reshape(devices, NBLK)
    source_dev = (table // SENDS).astype(jnp.int32)
    source_slot = send_slot.reshape(-1)[table].astype(jnp.int32)
    half_count = NBLK // 2

    def per_replica(summed, replica_idx):
        inputs = lax.dynamic_slice_in_dim(acts_in, replica_idx * TOK_REP, TOK_REP, 0).reshape(MICRO, MB_TOK, D)
        cots = lax.dynamic_slice_in_dim(cotangent, replica_idx * TOK_REP, TOK_REP, 0).reshape(MICRO, MB_TOK, D)
        matrices = []
        owned = []
        for section_idx in range(N_SECTION):
            device = replica_idx * N_SECTION + section_idx
            blocks = old_blocks[source_dev[device], source_slot[device]]
            up_matrix = blocks[:half_count].reshape(D, FWIN)
            out_matrix = blocks[half_count:].reshape(D, FWIN)
            matrices.append((up_matrix, out_matrix))
            padded = jnp.concatenate([blocks, jnp.zeros((NPAD - NBLK, BLOCK_ROWS, FWIN), jnp.bfloat16)], axis=0)
            owned.append(lax.dynamic_slice_in_dim(padded, replica_idx * OWN_SLOTS, OWN_SLOTS, 0))
        saved = [[None] * MICRO for section_idx in range(N_SECTION)]
        for micro_index in range(MICRO):
            current = inputs[micro_index]
            for section_idx in range(N_SECTION):
                saved[section_idx][micro_index] = current
                current = section_forward(current, matrices[section_idx][0], matrices[section_idx][1])
        grads_up = [jnp.zeros((D, FWIN), jnp.float32) for section_idx in range(N_SECTION)]
        grads_back = [jnp.zeros((D, FWIN), jnp.float32) for section_idx in range(N_SECTION)]
        for micro_index in range(MICRO):
            grad_y = cots[micro_index]
            for section_idx in reversed(range(N_SECTION)):
                grad_y, grad_up, grad_back = section_backward(saved[section_idx][micro_index], grad_y, matrices[section_idx][0], matrices[section_idx][1])
                grads_up[section_idx] = grads_up[section_idx] + grad_up
                grads_back[section_idx] = grads_back[section_idx] + grad_back
        stacked = []
        for section_idx in range(N_SECTION):
            stacked.append(jnp.concatenate([grads_up[section_idx].reshape(half_count, BLOCK_ROWS, FWIN), grads_back[section_idx].reshape(half_count, BLOCK_ROWS, FWIN), jnp.zeros((NPAD - NBLK, BLOCK_ROWS, FWIN), jnp.float32)], axis=0))
        partial_low = lax.optimization_barrier(jnp.stack(stacked).astype(jnp.bfloat16))
        return (summed + partial_low.astype(jnp.float32), jnp.stack(owned))
    start = jnp.zeros((N_SECTION, NPAD, BLOCK_ROWS, FWIN), jnp.float32)
    gradient, owned_all = lax.scan(per_replica, start, jnp.arange(N_REPLICA, dtype=jnp.int32))
    owned_weight = jnp.transpose(owned_all, (1, 0, 2, 3, 4)).reshape(N_SECTION, NPAD, BLOCK_ROWS, FWIN)
    entries = N_SECTION * OWN_SLOTS
    dest_table = moment_dest.reshape(N_REPLICA, entries).astype(jnp.int32)

    def invert(values):
        return jnp.zeros((entries,), jnp.int32).at[values].set(jnp.arange(entries, dtype=jnp.int32))
    inverse = jax.vmap(invert)(dest_table)
    first_held = old_first.reshape(N_REPLICA, entries, BLOCK_ROWS, FWIN)
    second_held = old_second.reshape(N_REPLICA, entries, BLOCK_ROWS, FWIN)
    first = jnp.take_along_axis(first_held, inverse[:, :, None, None], axis=1)
    second = jnp.take_along_axis(second_held, inverse[:, :, None, None], axis=1)
    first = jnp.transpose(first.reshape(N_REPLICA, N_SECTION, OWN_SLOTS, BLOCK_ROWS, FWIN), (1, 0, 2, 3, 4)).reshape(N_SECTION, NPAD, BLOCK_ROWS, FWIN)
    second = jnp.transpose(second.reshape(N_REPLICA, N_SECTION, OWN_SLOTS, BLOCK_ROWS, FWIN), (1, 0, 2, 3, 4)).reshape(N_SECTION, NPAD, BLOCK_ROWS, FWIN)
    new_first = beta_first * first + (1.0 - beta_first) * gradient
    new_second = beta_second * second + (1.0 - beta_second) * gradient * gradient
    new_weight = (owned_weight.astype(jnp.float32) - step_size * new_first / (jnp.sqrt(new_second) + adam_eps)).astype(jnp.bfloat16)
    return (new_weight, new_first, new_second)
```

```python
import functools

import jax
import jax.numpy as jnp
from jax import lax
from jax.experimental import pallas as pl
from jax.experimental.pallas import tpu as pltpu
from jax.sharding import PartitionSpec as P


D = 7168
HID = 256
TOK = 128
NBLK = 112
HALF = 56
PIECE = 32
LOCAL = HALF * PIECE
GROUPS = LOCAL // 128
SECTIONS = 4
REPLICAS = 32
DEVICES = 128
OWN = 4
REAL_OWNERS = NBLK // OWN
BIG = 1 << 20
EVERY = ("replica", "section")

rms_eps = 1e-05
beta_first = 0.9
beta_second = 0.95
step_size = 0.1
adam_eps = 1e-08
SCALE_IN = D ** (-0.5)
SCALE_OUT = HID ** (-0.5)

f32 = jnp.float32
bf16 = jnp.bfloat16
ANY = pl.BlockSpec(memory_space=pl.ANY)
SMEM = pl.BlockSpec(memory_space=pltpu.SMEM)
VMEM = pl.BlockSpec(memory_space=pltpu.VMEM)
LIMIT = 12 * 1024 * 1024


def struct(shape, dtype):
    return jax.ShapeDtypeStruct(shape, dtype)


def call(kernel, out_shape, in_specs, out_specs, scratch=(), after=()):
    waits = len(after)

    def body(*refs):
        kernel(*refs[waits:])

    run = pl.pallas_call(
        body,
        out_shape=out_shape,
        in_specs=[ANY] * waits + in_specs,
        out_specs=out_specs,
        scratch_shapes=list(scratch),
        compiler_params=pltpu.CompilerParams(vmem_limit_bytes=LIMIT),
    )
    return lambda *arrays: run(*after, *arrays)


def replica_at(x, y, core):
    return ((x % 4) * 4 + (y % 4)) * 2 + core


def shift_xy(block, step_x, step_y):
    route = [
        (replica_at(x, y, c), replica_at(x + step_x, y + step_y, c))
        for x in range(4)
        for y in range(4)
        for c in range(2)
    ]
    return lax.ppermute(block, "replica", route)


def shift_z(block, step):
    return lax.ppermute(block, "section", [(i, (i + step) % 4) for i in range(4)])


def from_sibling(block):
    return lax.ppermute(block, "replica", [(i, i ^ 1) for i in range(REPLICAS)])


def pack_kernel(slots, blocks, out, room, came, went):
    def start(d, carry):
        r = d // 4
        pltpu.make_async_copy(
            blocks.at[slots[d]], room.at[r, :, d % 4], came.at[r // 4]
        ).start()
        return carry

    lax.fori_loop(0, DEVICES, start, 0)
    for part in range(8):
        rows = pl.ds(part * 4, 4)
        pltpu.make_async_copy(room.at[rows], room.at[rows], came.at[part]).wait()
        pltpu.make_async_copy(room.at[rows], out.at[rows], went.at[part]).start()
    for part in range(8):
        rows = pl.ds(part * 4, 4)
        pltpu.make_async_copy(room.at[rows], out.at[rows], went.at[part]).wait()


def pack(slots, blocks):
    shape = (REPLICAS, 4, SECTIONS, PIECE, HID)
    return call(
        pack_kernel,
        struct(shape, bf16),
        [SMEM, ANY],
        ANY,
        [
            pltpu.VMEM(shape, bf16),
            pltpu.SemaphoreType.DMA((8,)),
            pltpu.SemaphoreType.DMA((8,)),
        ],
    )(slots, blocks)


def pack_second_kernel(flag, slots, blocks, out_0, out_1, out_2, out_3, room, came, went):
    outs = (out_0, out_1, out_2, out_3)

    @pl.when(flag[0] == 1)
    def _():
        for s in range(SECTIONS):

            def start(r, carry):
                pltpu.make_async_copy(
                    blocks.at[slots[r * 4 + s]], room.at[s, r], came.at[s]
                ).start()
                return carry

            lax.fori_loop(0, REPLICAS, start, 0)
        for s in range(SECTIONS):
            pltpu.make_async_copy(room.at[s], room.at[s], came.at[s]).wait()
            pltpu.make_async_copy(room.at[s], outs[s], went.at[s]).start()
        for s in range(SECTIONS):
            pltpu.make_async_copy(room.at[s], outs[s], went.at[s]).wait()


def pack_second(flag, slots, blocks):
    return call(
        pack_second_kernel,
        [struct((REPLICAS, 4, PIECE, HID), bf16)] * 4,
        [SMEM, SMEM, ANY],
        [ANY] * 4,
        [
            pltpu.VMEM((SECTIONS, REPLICAS, 4, PIECE, HID), bf16),
            pltpu.SemaphoreType.DMA((4,)),
            pltpu.SemaphoreType.DMA((4,)),
        ],
    )(flag, slots, blocks)


def choose_kernel(which, in_0, in_1, in_2, in_3, out, room, sem):
    for k, ref in enumerate((in_0, in_1, in_2, in_3)):

        @pl.when(which[0] == k)
        def _():
            come = pltpu.make_async_copy(ref, room, sem.at[0])
            come.start()
            come.wait()
            go = pltpu.make_async_copy(room, out, sem.at[1])
            go.start()
            go.wait()


def choose(which, arrays):
    return call(
        choose_kernel,
        struct((REPLICAS, 4, PIECE, HID), bf16),
        [SMEM] + [ANY] * 4,
        ANY,
        [pltpu.VMEM((REPLICAS, 4, PIECE, HID), bf16), pltpu.SemaphoreType.DMA((2,))],
    )(which, *arrays)


def blank_kernel(flag, out):
    pass


def blank(flag):
    return call(blank_kernel, struct((DEVICES * 4, PIECE, HID), bf16), [SMEM], ANY)(flag)


def gather_kernel(places, first, relayed, second, out, sem):
    def start(b, carry):
        place = places[b]

        @pl.when(place < 512)
        def _():
            pltpu.make_async_copy(first.at[place], out.at[b], sem).start()

        @pl.when((place >= 512) & (place < 640))
        def _():
            pltpu.make_async_copy(relayed.at[place - 512], out.at[b], sem).start()

        @pl.when(place >= 640)
        def _():
            pltpu.make_async_copy(second.at[place - 640], out.at[b], sem).start()

        return carry

    lax.fori_loop(0, NBLK, start, 0)
    pltpu.make_async_copy(out, out, sem).wait()


def gather(places, first, relayed, second):
    return call(
        gather_kernel,
        struct((NBLK, PIECE, HID), bf16),
        [SMEM, ANY, ANY, ANY],
        ANY,
        [pltpu.SemaphoreType.DMA],
    )(places, first, relayed, second)


def send_tables(send_slot, send_dest, send_block):
    code = send_slot.reshape(1, -1) * 128 + send_block.reshape(1, -1)
    match = send_dest.reshape(1, -1) == jnp.arange(DEVICES, dtype=jnp.int32)[:, None]
    low = jnp.min(jnp.where(match, code, BIG), axis=1)
    high = jnp.max(jnp.where(match, code, -1), axis=1)
    first = jnp.where(low < BIG, low, -1)
    second = jnp.where(high > low, high, -1)
    return first, second


def route_blocks(old_blocks, send_slot, send_dest, send_block, moment_dest):
    me_r = lax.axis_index("replica")
    me_z = lax.axis_index("section")
    blocks = old_blocks.reshape(NBLK, 4, PIECE, HID)
    first, second = send_tables(send_slot, send_dest, send_block)
    has_second = jnp.any(second >= 0).astype(jnp.int32)
    first_slots = jnp.maximum(first, 0) // 128
    second_slots = jnp.maximum(second, 0) // 128

    def labels_of(codes):
        return jnp.where(codes >= 0, codes % 128 + 1, 0).reshape(REPLICAS, 1, SECTIONS)

    note = jnp.concatenate([has_second.reshape(1), moment_dest.reshape(-1), jnp.zeros((3,), jnp.int32)])
    labels = jnp.concatenate(
        [
            labels_of(first),
            labels_of(second),
            jnp.broadcast_to(note, (REPLICAS, 1, 8)),
        ],
        axis=2,
    )
    labels = jnp.broadcast_to(labels, (REPLICAS, 4, 16)).reshape(DEVICES, 16)

    got = lax.all_to_all(labels, EVERY, 0, 0, tiled=True)
    buffer = pack(first_slots, blocks).reshape(DEVICES, 4 * PIECE, HID)
    buffer, got, flag = lax.optimization_barrier((buffer, got, has_second.reshape(1)))
    parts = pack_second(flag, second_slots, blocks)
    relays = (parts[0], from_sibling(parts[1]), shift_xy(parts[2], 1, 0), shift_xy(parts[3], 0, 1))
    arrived = lax.all_to_all(buffer, EVERY, 0, 0, tiled=True).reshape(DEVICES * 4, PIECE, HID)

    holders = got[:, 8]
    alone = jnp.sum(holders) == 1
    numbers = jnp.arange(DEVICES, dtype=jnp.int32)
    busy = jnp.sum(jnp.where(holders > 0, numbers, 0))
    busy = jnp.where(alone, busy, 0)
    busy_r, busy_z = busy // 4, busy % 4
    busy_x, busy_y, busy_c = busy_r // 8, (busy_r // 2) % 4, busy_r % 2

    def relay(k):
        r = (
            busy_r,
            busy_r + 1 - 2 * busy_c,
            ((busy_x + 1) % 4) * 8 + busy_y * 2 + busy_c,
            busy_x * 8 + ((busy_y + 1) % 4) * 2 + busy_c,
        )[k]
        return r * 4 + busy_z

    me = me_r * 4 + me_z
    which = jnp.int32(0)
    for k in range(1, 4):
        which = jnp.where(relay(k) == me, k, which)
    relayed = choose(which.reshape(1).astype(jnp.int32), relays)
    relayed, arrived = lax.optimization_barrier((relayed, arrived))
    relayed = lax.all_to_all(
        relayed.reshape(DEVICES, PIECE, HID), EVERY, 0, 0, tiled=True
    )

    def second_round():
        again = pack(second_slots, blocks).reshape(DEVICES, 4 * PIECE, HID)
        return lax.all_to_all(again, EVERY, 0, 0, tiled=True).reshape(DEVICES * 4, PIECE, HID)

    spare = lax.cond(alone, lambda: blank(has_second.reshape(1)), second_round)

    wanted = jnp.arange(1, NBLK + 1, dtype=jnp.int32)[None, None, :]
    in_first = got[:, 0:4, None] == wanted
    in_second = got[:, 4:8, None] == wanted
    sections = jnp.arange(SECTIONS, dtype=jnp.int32)[None, :, None]
    flat = numbers[:, None, None] * 4 + sections
    via = jnp.stack([relay(k) for k in range(4)])[None, :, None] + 512
    later = jnp.where(alone, via, flat + 640)
    places = jnp.sum(jnp.where(in_first, flat, 0) + jnp.where(in_second, later, 0), axis=0)
    places = jnp.clip(places, 0, 1151)
    weights = [gather(places[s], arrived, relayed, spare) for s in range(SECTIONS)]
    return weights, got


def quarter_kernel(pick, acts, cots, acts_out, cots_out):
    chosen = pick[...]
    for j in range(GROUPS):
        wide = slice(j * 512, (j + 1) * 512)
        narrow = slice(j * 128, (j + 1) * 128)
        acts_out[:, narrow] = jnp.dot(
            acts[:, wide], chosen, preferred_element_type=f32
        ).astype(bf16)
        cots_out[:, narrow] = jnp.dot(
            cots[:, wide], chosen, preferred_element_type=f32
        ).astype(bf16)


def quarter(acts, cots, q):
    rows = jnp.arange(512, dtype=jnp.int32)[:, None]
    columns = jnp.arange(128, dtype=jnp.int32)[None, :]
    pick = (rows == (columns // 32) * 128 + q * 32 + columns % 32).astype(bf16)
    return call(
        quarter_kernel,
        [struct((TOK, LOCAL), bf16)] * 2,
        [VMEM] * 3,
        [VMEM] * 2,
    )(pick, acts, cots)


def up_of(weight):
    return weight[:HALF].reshape(LOCAL, HID)


def out_of(weight):
    return weight[HALF:].reshape(LOCAL, HID)


def put_forward(message, layer_in, up_matrix):
    wide = layer_in.astype(f32)
    squares = jnp.sum(wide * wide, axis=1, keepdims=True)
    high = squares.astype(bf16)
    low = (squares - high.astype(f32)).astype(bf16)
    lane = lax.broadcasted_iota(jnp.int32, (TOK, 128), 1)
    message[:, 0:HID] = jnp.dot(layer_in, up_matrix, preferred_element_type=f32).astype(bf16)
    message[:, HID : HID + 128] = jnp.where(
        lane == 0, high.astype(f32), jnp.where(lane == 1, low.astype(f32), 0.0)
    ).astype(bf16)


def take_forward(total):
    squares = total[:, HID : HID + 1] + total[:, HID + 1 : HID + 2]
    inverse = lax.rsqrt(squares * (1.0 / D) + rms_eps)
    pre = total[:, 0:HID] * inverse * SCALE_IN
    return pre, jax.nn.gelu(pre, approximate=True).astype(bf16), inverse


def gelu_slope(v):
    root = 0.7978845608028654
    t = jnp.tanh(root * (v + 0.044715 * v * v * v))
    return 0.5 * (1.0 + t) + 0.5 * v * (1.0 - t * t) * root * (1.0 + 0.134145 * v * v)


def times_t(a, b):
    return lax.dot_general(a, b, (((1,), (1,)), ((), ())), preferred_element_type=f32)


def summed(refs):
    return sum([ref[...].astype(f32) for ref in refs[1:]], refs[0][...].astype(f32))


def open_kernel(layer_in, weight, message):
    put_forward(message, layer_in[...], up_of(weight))


def forward_kernel(last, *refs):
    messages, refs = refs[:4], refs[4:]
    if last:
        layer_in, weight, weight_next, cots, pair, pre, inverse, layer_out, message = refs
    else:
        layer_in, weight, weight_next, pair, pre, inverse, layer_out, message = refs
    pre_value, act_value, inverse_value = take_forward(summed(messages))
    pair[:, 0:LOCAL] = layer_in[...]
    pair[:, LOCAL:] = act_value
    pre[...] = pre_value
    inverse[...] = jnp.broadcast_to(inverse_value, (TOK, 128))
    branch = times_t(act_value, out_of(weight))
    result = (layer_in[...].astype(f32) + branch * SCALE_OUT).astype(bf16)
    layer_out[...] = result
    put_forward(message, result, up_of(weight_next))
    if last:
        message[:, HID + 128 :] = jnp.dot(
            cots[...], out_of(weight_next), preferred_element_type=f32
        ).astype(bf16)


def backward_kernel(from_forward, *refs):
    messages, refs = refs[:4], refs[4:]
    total = summed(messages)
    if from_forward:
        grad_out, layer_in, weight, weight_next, pair, back, grad_in, message = refs
        pre_value, act_value, inverse_value = take_forward(total)
        pair[:, 0:LOCAL] = layer_in[...]
        pair[:, LOCAL:] = act_value
        grad_act = total[:, HID + 128 :] * SCALE_OUT
    else:
        pre, inverse, grad_out, layer_in, weight, weight_next, back, grad_in, message = refs
        pre_value = pre[...]
        inverse_value = inverse[:, 0:1]
        grad_act = total * SCALE_OUT
    pulled = (grad_act * gelu_slope(pre_value)).astype(bf16)
    back[:, 0:LOCAL] = grad_out[...]
    back[:, LOCAL:] = (pulled.astype(f32) * inverse_value).astype(bf16)
    correction = jnp.sum(pulled.astype(f32) * pre_value, axis=1, keepdims=True) * (1.0 / D)
    grad_norm = times_t(pulled, up_of(weight)) * SCALE_IN
    normed = layer_in[...].astype(f32) * inverse_value
    result = grad_out[...].astype(f32) + (grad_norm - normed * correction) * inverse_value
    result = result.astype(bf16)
    grad_in[...] = result
    message[...] = jnp.dot(result, out_of(weight_next), preferred_element_type=f32).astype(bf16)


def close_kernel(*refs):
    messages, (pre, inverse, grad_out, back) = refs[:4], refs[4:]
    grad_act = summed(messages) * SCALE_OUT
    pulled = (grad_act * gelu_slope(pre[...])).astype(bf16)
    back[:, 0:LOCAL] = grad_out[...]
    back[:, LOCAL:] = (pulled.astype(f32) * inverse[:, 0:1]).astype(bf16)


def all_of(message):
    return [message] + [shift_z(message, k) for k in (1, 3, 2)]


def gradient_kernel(x_first, place, pair, back, pair_sib, back_sib, *refs):
    outs, chosen, table = refs[:4], refs[4], refs[5]
    core = place[2]
    small = slice(LOCAL, LOCAL + HID)
    half = GROUPS // 2

    def product(left, left_sib, right, right_sib, scale, start):
        both = jnp.concatenate([left[:, small], left_sib[:, small]], axis=0)
        turned = both.astype(f32).T.astype(bf16)
        for g in range(half):
            columns = pl.ds(pl.multiple_of((2 * g + core) * 128, 128), 128)
            chosen[0:TOK, g * 128 : (g + 1) * 128] = right[:, columns]
            chosen[TOK:, g * 128 : (g + 1) * 128] = right_sib[:, columns]
        result = jnp.dot(turned, chosen[...], preferred_element_type=f32) * scale
        for g in range(half):
            table[start + g] = result[:, g * 128 : (g + 1) * 128].astype(bf16)

    product(back, back_sib, pair, pair_sib, SCALE_IN, 0)
    product(pair, pair_sib, back, back_sib, SCALE_OUT, half)
    table[2 * half] = jnp.zeros((HID, 128), bf16)
    table[2 * half + 1] = jnp.zeros((HID, 128), bf16)
    for k in range(4):
        for j in range(4):
            if x_first:
                owner = lax.rem(place[0] + k, 4) * 4 + j
            else:
                owner = j * 4 + lax.rem(place[1] + k, 4)
            outs[k][j] = table[owner]


def halve_kernel(x_first, count, place, *refs):
    mine = place[1] if x_first else place[0]
    outs = refs[4 * count :]
    for k in range(4):
        chunk = lax.rem(mine + k, 4)
        for n in range(count):
            four = refs[4 * n : 4 * n + 4]
            total = sum([ref[chunk].astype(f32) for ref in four[1:]], four[0][chunk].astype(f32))
            outs[k][n] = total.astype(outs[k].dtype)


def section_gradient(s, place, own, sib):
    x_first = s % 2 == 1
    chunks = call(
        functools.partial(gradient_kernel, x_first),
        [struct((4, HID, 128), bf16)] * 4,
        [SMEM] + [VMEM] * 4,
        [VMEM] * 4,
        [pltpu.VMEM((2 * TOK, LOCAL // 2), bf16), pltpu.VMEM((16, HID, 128), bf16)],
    )(place, *own, *sib)
    step = (1, 0) if x_first else (0, 1)
    moved = [shift_xy(chunks[k], k * step[0], k * step[1]) for k in (1, 2, 3)]
    return [chunks[0]] + moved, chunks[0]


def second_half(x_first, place, sections):
    count = len(sections)
    kept, *sends = call(
        functools.partial(halve_kernel, x_first, count),
        [struct((count, HID, 128), f32)] + [struct((count, HID, 128), bf16)] * 3,
        [SMEM] + [VMEM] * (4 * count),
        [VMEM] * 4,
    )(place, *[v for section in sections for v in section])
    step = (0, 1) if x_first else (1, 0)
    return [kept] + [shift_xy(sends[k - 1], k * step[0], k * step[1]) for k in (1, 2, 3)]


def finish_kernel(place, *refs):
    odd, even, refs = refs[:4], refs[4:8], refs[8:]
    kept, sends, table = refs[0], refs[1:4], refs[4]
    for n in range(2):
        table[2 * n + 1] = sum([ref[n].astype(f32) for ref in odd[1:]], odd[0][n])
        table[2 * n] = sum([ref[n].astype(f32) for ref in even[1:]], even[0][n])
    for k in range(4):
        value = table[lax.rem(place[3] + k, 4)]
        if k == 0:
            kept[...] = value
        else:
            sends[k - 1][...] = value.astype(bf16)


def split_moments_kernel(place, first, second, *outs):
    for k in range(4):
        rows = pl.ds(pl.multiple_of(lax.rem(place[3] + k, 4) * PIECE, PIECE), PIECE)
        for a in range(OWN):
            outs[k][0, a] = first[a, rows, :].astype(bf16)
            outs[k][1, a] = second[a, rows, :].astype(bf16)


def order_kernel(place, source, *refs):
    moments, outs, table = refs[:4], refs[4:8], refs[8]
    for k in range(4):
        table[k] = moments[k][...]
    for k in range(4):
        section = lax.rem(place[3] + k, 4)
        for i in range(OWN):
            held = source[section * OWN + i]
            outs[k][0, i] = table[held // OWN, 0, lax.rem(held, OWN)]
            outs[k][1, i] = table[held // OWN, 1, lax.rem(held, OWN)]


def owned_kernel(place, *refs):
    weights, outs = refs[:4], refs[4:8]
    start = jnp.minimum(place[4], REAL_OWNERS - 1) * OWN
    for k in range(4):
        section = lax.rem(place[3] + k, 4)
        for s in range(SECTIONS):

            @pl.when(section == s)
            def _():
                outs[k][...] = weights[s][pl.ds(start, OWN)]


def adam_kernel(place, *refs):
    gradients, held, weights = refs[:4], refs[4:8], refs[8:12]
    weight_out, first_out, second_out = refs[12:]
    real = place[4] < REAL_OWNERS
    for k in range(4):
        q = lax.rem(place[3] + 4 - k, 4)
        rows = pl.ds(pl.multiple_of(q * PIECE, PIECE), PIECE)
        turned = jnp.where(real, gradients[k][...].astype(f32).T, 0.0)
        for i in range(OWN):
            gradient = turned[i * PIECE : (i + 1) * PIECE, :]
            weight = jnp.where(real, weights[k][i].astype(f32), 0.0)
            first = beta_first * held[k][0, i].astype(f32) + (1.0 - beta_first) * gradient
            second = beta_second * held[k][1, i].astype(f32) + (
                (1.0 - beta_second) * gradient * gradient
            )
            first_out[i, rows, :] = first
            second_out[i, rows, :] = second
            weight_out[i, rows, :] = (
                weight - step_size * first / (jnp.sqrt(second) + adam_eps)
            ).astype(bf16)


def on_device(
    acts_in,
    cotangent,
    old_blocks,
    send_slot,
    send_dest,
    send_block,
    old_first,
    old_second,
    moment_dest,
):
    me_r = lax.axis_index("replica")
    me_z = lax.axis_index("section")
    place = jnp.stack([me_r // 8, (me_r // 2) % 4, me_r % 2, me_z, me_r]).astype(jnp.int32)

    split = call(
        split_moments_kernel,
        [struct((2, OWN, PIECE, HID), bf16)] * 4,
        [SMEM, VMEM, VMEM],
        [VMEM] * 4,
    )(place, old_first[0], old_second[0])
    pieces = [split[0]] + [shift_z(split[k], k) for k in (1, 2, 3)]

    weights, labels = route_blocks(old_blocks, send_slot, send_dest, send_block, moment_dest)
    table = lax.dynamic_slice_in_dim(labels, me_r * 4, 4, 0)[:, 9:13]
    distance = (me_z - jnp.arange(SECTIONS, dtype=jnp.int32)) % 4
    held = (distance[:, None] * OWN + jnp.arange(OWN, dtype=jnp.int32)[None, :]).reshape(-1)
    slots = jnp.arange(SECTIONS * OWN, dtype=jnp.int32)
    source = jnp.sum(jnp.where(table.reshape(1, -1) == slots[:, None], held[None, :], 0), axis=1)
    ordered = call(
        order_kernel,
        [struct((2, OWN, PIECE, HID), bf16)] * 4,
        [SMEM, SMEM] + [VMEM] * 4,
        [VMEM] * 4,
        [pltpu.VMEM((4, 2, OWN, PIECE, HID), bf16)],
    )(place, source, *pieces)
    moments = [ordered[0]] + [shift_z(ordered[k], k) for k in (1, 2, 3)]

    layer_0, cots = quarter(acts_in, cotangent, me_z)
    message = call(
        open_kernel, struct((TOK, HID + 128), bf16), [VMEM] * 2, VMEM, after=moments[1:]
    )(layer_0, weights[0])
    layers = [layer_0]
    pairs, pairs_sib, pres, inverses = [], [], [], []
    for s in range(SECTIONS - 1):
        last = s == SECTIONS - 2
        width = 2 * HID + 128 if last else HID + 128
        extra = (cots,) if last else ()
        pair, pre, inverse, layer, message = call(
            functools.partial(forward_kernel, last),
            [
                struct((TOK, LOCAL + HID), bf16),
                struct((TOK, HID), f32),
                struct((TOK, 128), f32),
                struct((TOK, LOCAL), bf16),
                struct((TOK, width), bf16),
            ],
            [VMEM] * (7 + len(extra)),
            [VMEM] * 5,
        )(*all_of(message), layers[s], weights[s], weights[s + 1], *extra)
        layers.append(layer)
        pairs.append(pair)
        pairs_sib.append(from_sibling(pair))
        pres.append(pre)
        inverses.append(inverse)

    owned = call(
        owned_kernel,
        [struct((OWN, PIECE, HID), bf16)] * 4,
        [SMEM] + [VMEM] * 4,
        [VMEM] * 4,
    )(place, *weights)
    owned = [owned[0]] + [shift_z(owned[k], k) for k in (1, 2, 3)]

    grad = cots
    done = []
    parts = [None] * SECTIONS
    for s in reversed(range(SECTIONS)):
        messages = all_of(message)
        wide = struct((TOK, LOCAL + HID), bf16)
        if s == 0:
            back = call(close_kernel, wide, [VMEM] * 7, VMEM, after=done)(
                *messages, pres[0], inverses[0], grad
            )
        elif s == SECTIONS - 1:
            pair, back, grad, message = call(
                functools.partial(backward_kernel, True),
                [wide, wide, struct((TOK, LOCAL), bf16), struct((TOK, HID), bf16)],
                [VMEM] * 8,
                [VMEM] * 4,
            )(*messages, grad, layers[s], weights[s], weights[s - 1])
            pairs.append(pair)
            pairs_sib.append(from_sibling(pair))
        else:
            back, grad, message = call(
                functools.partial(backward_kernel, False),
                [wide, struct((TOK, LOCAL), bf16), struct((TOK, HID), bf16)],
                [VMEM] * 10,
                [VMEM] * 3,
                after=done,
            )(*messages, pres[s], inverses[s], grad, layers[s], weights[s], weights[s - 1])
        own, sib = (pairs[s], back), (pairs_sib[s], from_sibling(back))
        parts[s], chunk = section_gradient(s, place, own, sib)
        done = [chunk]

    odd = second_half(True, place, [parts[1], parts[3]])
    even = second_half(False, place, [parts[0], parts[2]])
    kept, *sends = call(
        finish_kernel,
        [struct((HID, 128), f32)] + [struct((HID, 128), bf16)] * 3,
        [SMEM] + [VMEM] * 8,
        [VMEM] * 4,
        [pltpu.VMEM((SECTIONS, HID, 128), f32)],
    )(place, *odd, *even)
    gradients = [kept] + [shift_z(sends[k - 1], k) for k in (1, 2, 3)]
    new_weight, new_first, new_second = call(
        adam_kernel,
        [
            struct((OWN, 128, HID), bf16),
            struct((OWN, 128, HID), f32),
            struct((OWN, 128, HID), f32),
        ],
        [SMEM] + [VMEM] * 12,
        [VMEM] * 3,
    )(place, *gradients, *moments, *owned)
    return (new_weight[None], new_first[None], new_second[None])


def solution(mesh):
    in_specs = (
        P("replica", None),
        P("replica", None),
        P(("replica", "section"), None, None, None),
        P(("replica", "section"), None),
        P(("replica", "section"), None),
        P(("replica", "section"), None),
        P(("replica", "section"), None, None, None),
        P(("replica", "section"), None, None, None),
        P(("replica", "section"), None),
    )
    out_specs = (
        P("section", "replica", None, None),
        P("section", "replica", None, None),
        P("section", "replica", None, None),
    )
    return jax.shard_map(
        on_device, mesh=mesh, in_specs=in_specs, out_specs=out_specs, check_vma=False
    )
```

```python
import functools

import jax
import jax.numpy as jnp
from jax import lax
from jax.experimental import pallas as pl
from jax.experimental.pallas import tpu as pltpu
from jax.sharding import PartitionSpec as P


D = 7168
HID = 256
TOK = 128
NBLK = 112
HALF = 56
PIECE = 32
LOCAL = HALF * PIECE
GROUPS = LOCAL // 128
SECTIONS = 4
REPLICAS = 32
DEVICES = 128
OWN = 4
REAL_OWNERS = NBLK // OWN
BIG = 1 << 20
CHUNK = SECTIONS * PIECE + 16
EVERY = ("replica", "section")

rms_eps = 1e-05
beta_first = 0.9
beta_second = 0.95
step_size = 0.1
adam_eps = 1e-08
SCALE_IN = D ** (-0.5)
SCALE_OUT = HID ** (-0.5)

f32 = jnp.float32
bf16 = jnp.bfloat16
ANY = pl.BlockSpec(memory_space=pl.ANY)
HBM = pl.BlockSpec(memory_space=pltpu.HBM)
SMEM = pl.BlockSpec(memory_space=pltpu.SMEM)
VMEM = pl.BlockSpec(memory_space=pltpu.VMEM)
LIMIT = 12 * 1024 * 1024
BULK = 62 * 1024 * 1024


def struct(shape, dtype):
    return jax.ShapeDtypeStruct(shape, dtype)


def call(kernel, out_shape, in_specs, out_specs, scratch=(), after=(), aliases=None, limit=LIMIT):
    waits = len(after)

    def body(*refs):
        kernel(*refs[waits:])

    run = pl.pallas_call(
        body,
        out_shape=out_shape,
        in_specs=[ANY] * waits + in_specs,
        out_specs=out_specs,
        scratch_shapes=list(scratch),
        input_output_aliases={waits + i: o for i, o in (aliases or {}).items()},
        compiler_params=pltpu.CompilerParams(vmem_limit_bytes=limit),
    )
    return lambda *arrays: run(*after, *arrays)


def replica_at(x, y, core):
    return ((x % 4) * 4 + (y % 4)) * 2 + core


def shift_xy(block, step_x, step_y):
    route = [
        (replica_at(x, y, c), replica_at(x + step_x, y + step_y, c))
        for x in range(4)
        for y in range(4)
        for c in range(2)
    ]
    return lax.ppermute(block, "replica", route)


def shift_z(block, step):
    return lax.ppermute(block, "section", [(i, (i + step) % 4) for i in range(4)])


def spread(block, axis):
    if axis == "z":
        names = ("replica", "section")
        route = []
        for r in range(REPLICAS):
            step = 1 - 2 * (r % 2)
            route += [(r * 4 + i, r * 4 + (i + step) % 4) for i in range(4)]
        return lax.ppermute(block, names, route)
    route = []
    for x in range(4):
        for y in range(4):
            for c in range(2):
                step = 1 - 2 * c
                to = (x + step, y) if axis == "x" else (x, y + step)
                route.append((replica_at(x, y, c), replica_at(*to, c)))
    return lax.ppermute(block, "replica", route)


def from_sibling(block):
    return lax.ppermute(block, "replica", [(i, i ^ 1) for i in range(REPLICAS)])


def pack_kernel(slots, blocks, out, room, came, went):
    for part in range(8):
        for s in range(SECTIONS):

            def start(i, carry):
                r = part * 4 + i
                pltpu.make_async_copy(
                    blocks.at[slots[r * 4 + s]],
                    room.at[r, :, pl.ds(s * PIECE, PIECE)],
                    came.at[part],
                ).start()
                return carry

            lax.fori_loop(0, 4, start, 0)

    def go(part):
        rows = pl.ds(part * 4, 4)
        into = out.at[rows, :, pl.ds(0, SECTIONS * PIECE)]
        return pltpu.make_async_copy(room.at[rows], into, went.at[part])

    for part in range(8):
        rows = pl.ds(part * 4, 4)
        pltpu.make_async_copy(room.at[rows], room.at[rows], came.at[part]).wait()
        go(part).start()
    for part in range(8):
        go(part).wait()


def pack(slots, blocks, tall, after=()):
    return call(
        pack_kernel,
        struct((REPLICAS, 4, tall, HID), bf16),
        [SMEM, ANY],
        HBM,
        [
            pltpu.VMEM((REPLICAS, 4, SECTIONS * PIECE, HID), bf16),
            pltpu.SemaphoreType.DMA((8,)),
            pltpu.SemaphoreType.DMA((8,)),
        ],
        after=after,
        limit=BULK,
    )(slots, blocks)


def pack_second_kernel(flag, slots, blocks, *refs):
    outs, (room, came, went) = refs[:5], refs[5:]

    @pl.when(flag[0] == 1)
    def _():
        for s in range(SECTIONS):

            def start(r, carry):
                pltpu.make_async_copy(
                    blocks.at[slots[r * 4 + s]], room.at[s, r], came.at[s]
                ).start()
                return carry

            lax.fori_loop(0, REPLICAS, start, 0)

        def go(s, h):
            rows = room.at[s, :, :, pl.ds(h * 16, 16)]
            return pltpu.make_async_copy(
                rows, outs[4].at[s] if h else outs[s], went.at[s + 4 * h]
            )

        for s in range(SECTIONS):
            pltpu.make_async_copy(room.at[s], room.at[s], came.at[s]).wait()
            go(s, 1).start()
            go(s, 0).start()
        for s in range(SECTIONS):
            go(s, 1).wait()
            go(s, 0).wait()


def pack_second(flag, slots, blocks):
    return call(
        pack_second_kernel,
        [struct((REPLICAS, 4, 16, HID), bf16)] * 4
        + [struct((SECTIONS, REPLICAS, 4, 16, HID), bf16)],
        [SMEM, SMEM, ANY],
        [HBM] * 5,
        [
            pltpu.VMEM((SECTIONS, REPLICAS, 4, PIECE, HID), bf16),
            pltpu.SemaphoreType.DMA((4,)),
            pltpu.SemaphoreType.DMA((8,)),
        ],
        limit=BULK,
    )(flag, slots, blocks)


def take_over_kernel(flag, got, in_0, in_1, in_2, in_3, out_0, out_1, out_2, out_3, room, came, went):
    outs = (out_0, out_1, out_2, out_3)

    @pl.when(flag[0] == 1)
    def _():
        def come(s):
            return pltpu.make_async_copy(got.at[s], room.at[s], came.at[s])

        def go(s):
            return pltpu.make_async_copy(room.at[s], outs[s], went.at[s])

        for s in range(SECTIONS):
            come(s).start()
        for s in range(SECTIONS):
            come(s).wait()
            go(s).start()
        for s in range(SECTIONS):
            go(s).wait()


def take_over(flag, got, own, after):
    return call(
        take_over_kernel,
        [struct((REPLICAS, 4, 16, HID), bf16)] * 4,
        [SMEM] + [HBM] * 5,
        [HBM] * 4,
        [
            pltpu.VMEM((SECTIONS, REPLICAS, 4, 16, HID), bf16),
            pltpu.SemaphoreType.DMA((4,)),
            pltpu.SemaphoreType.DMA((4,)),
        ],
        after=after,
        aliases={2: 0, 3: 1, 4: 2, 5: 3},
        limit=BULK,
    )(flag, got, *own)


def add_relayed_kernel(which, in_0, in_1, in_2, in_3, buffer, out, room, sem):
    for k, ref in enumerate((in_0, in_1, in_2, in_3)):

        @pl.when(which[0] == k)
        def _():
            come = pltpu.make_async_copy(ref, room, sem.at[0])
            come.start()
            come.wait()
            go = pltpu.make_async_copy(room, out.at[:, :, pl.ds(SECTIONS * PIECE, 16)], sem.at[1])
            go.start()
            go.wait()


def add_relayed(which, relays, buffer):
    return call(
        add_relayed_kernel,
        struct((REPLICAS, 4, CHUNK, HID), bf16),
        [SMEM] + [HBM] * 5,
        HBM,
        [pltpu.VMEM((REPLICAS, 4, 16, HID), bf16), pltpu.SemaphoreType.DMA((2,))],
        aliases={5: 0},
        limit=BULK,
    )(which, *relays, buffer)


def blank_kernel(flag, out):
    pass


def blank(flag):
    return call(blank_kernel, struct((DEVICES, SECTIONS * PIECE, HID), bf16), [SMEM], HBM)(flag)


def fetch(section, place, relays, first, second, out, sem):
    rows = section * PIECE
    if not isinstance(section, int):
        rows = pl.multiple_of(rows, PIECE)
    rows = pl.ds(rows, PIECE)
    extra = pl.ds(SECTIONS * PIECE, 16)

    @pl.when(place < DEVICES)
    def _():
        pltpu.make_async_copy(first.at[place, rows], out, sem).start()

    @pl.when(place >= DEVICES)
    def _():
        @pl.when(place < 2 * DEVICES)
        def _():
            pltpu.make_async_copy(second.at[place - DEVICES, rows], out, sem).start()

        @pl.when(place == 2 * DEVICES)
        def _():
            low, high = relays[section], relays[section + 4]
            pltpu.make_async_copy(first.at[low, extra], out.at[pl.ds(0, 16)], sem).start()
            pltpu.make_async_copy(first.at[high, extra], out.at[pl.ds(16, 16)], sem).start()


def gather_kernel(section, begin, places, relays, first, second, out, sem):
    def start(b, carry):
        fetch(section, places[begin + b], relays, first, second, out.at[b], sem)
        return carry

    lax.fori_loop(0, HALF, start, 0, unroll=8)
    pltpu.make_async_copy(out, out, sem).wait()


def gather(section, begin, places, relays, first, second):
    return call(
        functools.partial(gather_kernel, section, begin),
        struct((HALF, PIECE, HID), bf16),
        [SMEM, SMEM, ANY, ANY],
        ANY,
        [pltpu.SemaphoreType.DMA],
    )(places, relays, first, second)


def send_tables(send_slot, send_dest, send_block):
    code = send_slot.reshape(1, -1) * 128 + send_block.reshape(1, -1)
    match = send_dest.reshape(1, -1) == jnp.arange(DEVICES, dtype=jnp.int32)[:, None]
    low = jnp.min(jnp.where(match, code, BIG), axis=1)
    high = jnp.max(jnp.where(match, code, -1), axis=1)
    first = jnp.where(low < BIG, low, -1)
    second = jnp.where(high > low, high, -1)
    return first, second


def route_blocks(old_blocks, send_slot, send_dest, send_block, moment_dest):
    me_r = lax.axis_index("replica")
    me_z = lax.axis_index("section")
    blocks = old_blocks.reshape(NBLK, 4, PIECE, HID)
    first, second = send_tables(send_slot, send_dest, send_block)
    has_second = jnp.any(second >= 0).astype(jnp.int32)
    spread_out = jnp.arange(DEVICES, dtype=jnp.int32) % NBLK
    first_slots = jnp.where(first >= 0, first // 128, spread_out)
    second_slots = jnp.where(second >= 0, second // 128, spread_out)

    def labels_of(codes):
        return jnp.where(codes >= 0, codes % 128 + 1, 0).reshape(REPLICAS, 1, SECTIONS)

    note = jnp.concatenate([has_second.reshape(1), moment_dest.reshape(-1), jnp.zeros((3,), jnp.int32)])
    labels = jnp.concatenate(
        [
            labels_of(first),
            labels_of(second),
            jnp.broadcast_to(note, (REPLICAS, 1, 8)),
        ],
        axis=2,
    )
    labels = jnp.broadcast_to(labels, (REPLICAS, 4, 16)).reshape(DEVICES, 16)

    flag = has_second.reshape(1)
    *own, other = pack_second(flag, second_slots, blocks)
    flag_other = from_sibling(jnp.broadcast_to(flag, (128,)))[:1]
    came = from_sibling(other)
    other, labels = lax.optimization_barrier((other, labels))
    got = lax.all_to_all(labels, EVERY, 0, 0, tiled=True)
    mine = take_over(flag_other, came, own, after=[got])
    relays = [mine[0], spread(mine[1], "x"), spread(mine[2], "y"), spread(mine[3], "z")]
    buffer = pack(first_slots, blocks, CHUNK)

    holders = got[:, 8]
    alone = jnp.sum(holders) == 1
    numbers = jnp.arange(DEVICES, dtype=jnp.int32)
    busy = jnp.sum(jnp.where(holders > 0, numbers, 0))
    busy = jnp.where(alone, busy, 0)
    x, y, core, z = busy // 32, (busy // 8) % 4, (busy // 4) % 2, busy % 4
    found = []
    for c in (core, 1 - core):
        step = 1 + 2 * c
        for dx, dy, dz in ((0, 0, 0), (1, 0, 0), (0, 1, 0), (0, 0, 1)):
            chip = (x + dx * step) % 4 * 4 + (y + dy * step) % 4
            found.append((chip * 2 + c) * 4 + (z + dz * step) % 4)
    relay_places = jnp.stack(found).astype(jnp.int32)
    is_me = relay_places == me_r * 4 + me_z
    which = jnp.sum(jnp.where(is_me, jnp.arange(8, dtype=jnp.int32) % 4 + 1, 0)) - 1
    buffer = add_relayed(which.reshape(1).astype(jnp.int32), relays, buffer)
    arrived = lax.all_to_all(buffer.reshape(DEVICES, CHUNK, HID), EVERY, 0, 0, tiled=True)

    def second_round():
        again = pack(second_slots, blocks, SECTIONS * PIECE)
        return lax.all_to_all(
            again.reshape(DEVICES, SECTIONS * PIECE, HID), EVERY, 0, 0, tiled=True
        )

    spare = lax.cond(alone, lambda: blank(flag), second_round)

    wanted = jnp.arange(1, NBLK + 1, dtype=jnp.int32)[None, None, :]
    in_first = got[:, 0:4, None] == wanted
    in_second = got[:, 4:8, None] == wanted
    senders = numbers[:, None, None]
    later = jnp.where(alone, 2 * DEVICES, senders + DEVICES)
    places = jnp.sum(jnp.where(in_first, senders, 0) + jnp.where(in_second, later, 0), axis=0)
    places = jnp.clip(places, 0, 2 * DEVICES)
    weights = [
        [gather(s, begin, places[s], relay_places, arrived, spare) for begin in (0, HALF)]
        for s in range(SECTIONS)
    ]
    return weights, got, (places.reshape(-1), relay_places, arrived, spare)


def quarter_kernel(pick, acts, cots, acts_out, cots_out):
    chosen = pick[...]
    for j in range(GROUPS):
        wide = slice(j * 512, (j + 1) * 512)
        narrow = slice(j * 128, (j + 1) * 128)
        acts_out[:, narrow] = jnp.dot(
            acts[:, wide], chosen, preferred_element_type=f32
        ).astype(bf16)
        cots_out[:, narrow] = jnp.dot(
            cots[:, wide], chosen, preferred_element_type=f32
        ).astype(bf16)


def quarter(acts, cots, q):
    rows = jnp.arange(512, dtype=jnp.int32)[:, None]
    columns = jnp.arange(128, dtype=jnp.int32)[None, :]
    pick = (rows == (columns // 32) * 128 + q * 32 + columns % 32).astype(bf16)
    return call(
        quarter_kernel,
        [struct((TOK, LOCAL), bf16)] * 2,
        [VMEM] * 3,
        [VMEM] * 2,
    )(pick, acts, cots)


def flat(weight):
    return weight[...].reshape(LOCAL, HID)


def put_forward(message, layer_in, up_matrix):
    wide = layer_in.astype(f32)
    squares = jnp.sum(wide * wide, axis=1, keepdims=True)
    high = squares.astype(bf16)
    low = (squares - high.astype(f32)).astype(bf16)
    lane = lax.broadcasted_iota(jnp.int32, (TOK, 128), 1)
    message[:, 0:HID] = jnp.dot(layer_in, up_matrix, preferred_element_type=f32).astype(bf16)
    message[:, HID : HID + 128] = jnp.where(
        lane == 0, high.astype(f32), jnp.where(lane == 1, low.astype(f32), 0.0)
    ).astype(bf16)


def take_forward(total):
    squares = total[:, HID : HID + 1] + total[:, HID + 1 : HID + 2]
    inverse = lax.rsqrt(squares * (1.0 / D) + rms_eps)
    pre = total[:, 0:HID] * inverse * SCALE_IN
    return pre, jax.nn.gelu(pre, approximate=True).astype(bf16), inverse


def gelu_slope(v):
    root = 0.7978845608028654
    t = jnp.tanh(root * (v + 0.044715 * v * v * v))
    return 0.5 * (1.0 + t) + 0.5 * v * (1.0 - t * t) * root * (1.0 + 0.134145 * v * v)


def times_t(a, b):
    return lax.dot_general(a, b, (((1,), (1,)), ((), ())), preferred_element_type=f32)


def summed(refs):
    return sum([ref[...].astype(f32) for ref in refs[1:]], refs[0][...].astype(f32))


def open_kernel(layer_in, weight, message):
    put_forward(message, layer_in[...], flat(weight))


def forward_kernel(layer_in, out_matrix, up_next, *refs):
    messages, (pair, pre, inverse, layer_out, message) = refs[:4], refs[4:]
    result = forward_step(messages, layer_in, out_matrix, pair, pre, inverse, layer_out)
    put_forward(message, result, flat(up_next))


def forward_step(messages, layer_in, out_matrix, pair, pre, inverse, layer_out):
    pre_value, act_value, inverse_value = take_forward(summed(messages))
    pair[:, 0:LOCAL] = layer_in[...]
    pair[:, LOCAL:] = act_value
    pre[...] = pre_value
    inverse[...] = jnp.broadcast_to(inverse_value, (TOK, 128))
    branch = times_t(act_value, flat(out_matrix))
    result = (layer_in[...].astype(f32) + branch * SCALE_OUT).astype(bf16)
    layer_out[...] = result
    return result


def turn_kernel(layer_in, out_matrix, up_next, out_next, cots, *refs):
    messages, (pair, pre, inverse, layer_out, message) = refs[:4], refs[4:]
    result = forward_step(messages, layer_in, out_matrix, pair, pre, inverse, layer_out)
    put_forward(message, result, flat(up_next))
    message[:, HID + 128 :] = jnp.dot(
        cots[...], flat(out_next), preferred_element_type=f32
    ).astype(bf16)


def backward_kernel(from_forward, *refs):
    messages, refs = refs[:4], refs[4:]
    total = summed(messages)
    if from_forward:
        grad_out, layer_in, up_matrix, out_next, pair, back, grad_in, message = refs
        pre_value, act_value, inverse_value = take_forward(total)
        pair[:, 0:LOCAL] = layer_in[...]
        pair[:, LOCAL:] = act_value
        grad_act = total[:, HID + 128 :] * SCALE_OUT
    else:
        pre, inverse, grad_out, layer_in, up_matrix, out_next, back, grad_in, message = refs
        pre_value = pre[...]
        inverse_value = inverse[:, 0:1]
        grad_act = total * SCALE_OUT
    pulled = (grad_act * gelu_slope(pre_value)).astype(bf16)
    back[:, 0:LOCAL] = grad_out[...]
    back[:, LOCAL:] = (pulled.astype(f32) * inverse_value).astype(bf16)
    correction = jnp.sum(pulled.astype(f32) * pre_value, axis=1, keepdims=True) * (1.0 / D)
    grad_norm = times_t(pulled, flat(up_matrix)) * SCALE_IN
    normed = layer_in[...].astype(f32) * inverse_value
    result = grad_out[...].astype(f32) + (grad_norm - normed * correction) * inverse_value
    result = result.astype(bf16)
    grad_in[...] = result
    message[...] = jnp.dot(result, flat(out_next), preferred_element_type=f32).astype(bf16)


def close_kernel(*refs):
    messages, (pre, inverse, grad_out, back) = refs[:4], refs[4:]
    grad_act = summed(messages) * SCALE_OUT
    pulled = (grad_act * gelu_slope(pre[...])).astype(bf16)
    back[:, 0:LOCAL] = grad_out[...]
    back[:, LOCAL:] = (pulled.astype(f32) * inverse[:, 0:1]).astype(bf16)


def all_of(message):
    return [message] + [shift_z(message, k) for k in (1, 3, 2)]


def products(core, pair, back, pair_sib, back_sib, chosen, store):
    small = slice(LOCAL, LOCAL + HID)
    half = GROUPS // 2

    def product(left, left_sib, right, right_sib, scale, start):
        both = jnp.concatenate([left[:, small], left_sib[:, small]], axis=0)
        turned = both.astype(f32).T.astype(bf16)
        for g in range(half):
            columns = pl.ds(pl.multiple_of((2 * g + core) * 128, 128), 128)
            chosen[0:TOK, g * 128 : (g + 1) * 128] = right[:, columns]
            chosen[TOK:, g * 128 : (g + 1) * 128] = right_sib[:, columns]
        result = jnp.dot(turned, chosen[...], preferred_element_type=f32) * scale
        for g in range(half):
            store(start + g, result[:, g * 128 : (g + 1) * 128].astype(bf16))

    product(back, back_sib, pair, pair_sib, SCALE_IN, 0)
    product(pair, pair_sib, back, back_sib, SCALE_OUT, half)
    for owner in range(2 * half, 16):
        store(owner, jnp.zeros((HID, 128), bf16))


def gradient_kernel(x_first, count, place, *refs):
    ins, outs, (chosen, table) = refs[: 4 * count], refs[4 * count : 4 * count + 4], refs[-2:]
    for n in range(count):

        def store(owner, value):
            table[owner, n] = value

        products(place[2], *ins[4 * n : 4 * n + 4], chosen, store)
    for k in range(4):
        for j in range(4):
            if x_first:
                owner = lax.rem(place[0] + k, 4) * 4 + j
            else:
                owner = j * 4 + lax.rem(place[1] + k, 4)
            outs[k][j] = table[owner]


def halve_kernel(x_first, counts, place, *refs):
    mine = place[1] if x_first else place[0]
    outs = refs[4 * len(counts) :]
    for k in range(4):
        chunk = lax.rem(mine + k, 4)
        start = 0
        for n, count in enumerate(counts):
            four = refs[4 * n : 4 * n + 4]
            total = sum([ref[chunk].astype(f32) for ref in four[1:]], four[0][chunk].astype(f32))
            outs[k][start : start + count] = total.astype(outs[k].dtype)
            start += count


def first_half(x_first, place, sections, after=()):
    count = len(sections)
    chunks = call(
        functools.partial(gradient_kernel, x_first, count),
        [struct((4, count, HID, 128), bf16)] * 4,
        [SMEM] + [VMEM] * (4 * count),
        [VMEM] * 4,
        [pltpu.VMEM((2 * TOK, LOCAL // 2), bf16), pltpu.VMEM((16, count, HID, 128), bf16)],
        after=after,
    )(place, *[v for section in sections for v in section])
    step = (1, 0) if x_first else (0, 1)
    return [chunks[0]] + [shift_xy(chunks[k], k * step[0], k * step[1]) for k in (1, 2, 3)]


def second_half(x_first, place, parts, after):
    counts = [part[0].shape[1] for part in parts]
    count = sum(counts)
    kept, *sends = call(
        functools.partial(halve_kernel, x_first, counts),
        [struct((count, HID, 128), f32)] + [struct((count, HID, 128), bf16)] * 3,
        [SMEM] + [VMEM] * (4 * len(parts)),
        [VMEM] * 4,
        after=after,
    )(place, *[v for part in parts for v in part])
    step = (0, 1) if x_first else (1, 0)
    return [kept] + [shift_xy(sends[k - 1], k * step[0], k * step[1]) for k in (1, 2, 3)]


def finish_kernel(places_in, place, *refs):
    groups, refs = refs[: 4 * len(places_in)], refs[4 * len(places_in) :]
    kept, sends, table = refs[0], refs[1:4], refs[4]
    for m, sections in enumerate(places_in):
        four = groups[4 * m : 4 * m + 4]
        for n, section in enumerate(sections):
            table[section] = sum([ref[n].astype(f32) for ref in four[1:]], four[0][n])
    for k in range(4):
        value = table[lax.rem(place[3] + k, 4)]
        if k == 0:
            kept[...] = value
        else:
            sends[k - 1][...] = value.astype(bf16)


def split_moments_kernel(place, first, second, *outs):
    for k in range(4):
        rows = pl.ds(pl.multiple_of(lax.rem(place[3] + k, 4) * PIECE, PIECE), PIECE)
        for a in range(OWN):
            outs[k][0, a] = first[a, rows, :].astype(bf16)
            outs[k][1, a] = second[a, rows, :].astype(bf16)


def order_kernel(place, source, places, relays, first, second, *refs):
    moments, outs, (table, came, sem) = refs[:4], refs[4:8], refs[8:]
    start = jnp.minimum(place[4], REAL_OWNERS - 1) * OWN
    for k in range(4):
        section = lax.rem(place[3] + k, 4)
        for i in range(OWN):
            held = places[section * NBLK + start + i]
            fetch(section, held, relays, first, second, came.at[k, i], sem)
    for k in range(4):
        table[k] = moments[k][...]
    for k in range(4):
        section = lax.rem(place[3] + k, 4)
        for i in range(OWN):
            held = source[section * OWN + i]
            outs[k][1, i] = table[held // OWN, 0, lax.rem(held, OWN)]
            outs[k][2, i] = table[held // OWN, 1, lax.rem(held, OWN)]
    pltpu.make_async_copy(came, came, sem).wait()
    for k in range(4):
        outs[k][0] = came[k]


def adam_kernel(place, *refs):
    gradients, held = refs[:4], refs[4:8]
    weight_out, first_out, second_out = refs[8:]
    real = place[4] < REAL_OWNERS
    for k in range(4):
        q = lax.rem(place[3] + 4 - k, 4)
        rows = pl.ds(pl.multiple_of(q * PIECE, PIECE), PIECE)
        turned = jnp.where(real, gradients[k][...].astype(f32).T, 0.0)
        for i in range(OWN):
            gradient = turned[i * PIECE : (i + 1) * PIECE, :]
            weight = jnp.where(real, held[k][0, i].astype(f32), 0.0)
            first = beta_first * held[k][1, i].astype(f32) + (1.0 - beta_first) * gradient
            second = beta_second * held[k][2, i].astype(f32) + (
                (1.0 - beta_second) * gradient * gradient
            )
            first_out[i, rows, :] = first
            second_out[i, rows, :] = second
            weight_out[i, rows, :] = (
                weight - step_size * first / (jnp.sqrt(second) + adam_eps)
            ).astype(bf16)


def on_device(
    acts_in,
    cotangent,
    old_blocks,
    send_slot,
    send_dest,
    send_block,
    old_first,
    old_second,
    moment_dest,
):
    me_r = lax.axis_index("replica")
    me_z = lax.axis_index("section")
    place = jnp.stack([me_r // 8, (me_r // 2) % 4, me_r % 2, me_z, me_r]).astype(jnp.int32)

    split = call(
        split_moments_kernel,
        [struct((2, OWN, PIECE, HID), bf16)] * 4,
        [SMEM, VMEM, VMEM],
        [VMEM] * 4,
    )(place, old_first[0], old_second[0])
    pieces = [split[0]] + [shift_z(split[k], k) for k in (1, 2, 3)]

    weights, labels, arrivals = route_blocks(
        old_blocks, send_slot, send_dest, send_block, moment_dest
    )
    table = lax.dynamic_slice_in_dim(labels, me_r * 4, 4, 0)[:, 9:13]
    distance = (me_z - jnp.arange(SECTIONS, dtype=jnp.int32)) % 4
    held = (distance[:, None] * OWN + jnp.arange(OWN, dtype=jnp.int32)[None, :]).reshape(-1)
    slots = jnp.arange(SECTIONS * OWN, dtype=jnp.int32)
    source = jnp.sum(jnp.where(table.reshape(1, -1) == slots[:, None], held[None, :], 0), axis=1)
    layer_0, cots = quarter(acts_in, cotangent, me_z)
    message = call(
        open_kernel, struct((TOK, HID + 128), bf16), [VMEM] * 2, VMEM
    )(layer_0, weights[0][0])
    layers = [layer_0]
    pairs, pairs_sib, pres, inverses = [], [], [], []
    wide = struct((TOK, LOCAL + HID), bf16)
    narrow = struct((TOK, LOCAL), bf16)
    for s in range(SECTIONS - 1):
        messages = all_of(message)
        turn = s == SECTIONS - 2
        extra = (weights[s + 1][1], cots) if turn else ()
        pair, pre, inverse, layer, message = call(
            turn_kernel if turn else forward_kernel,
            [
                wide,
                struct((TOK, HID), f32),
                struct((TOK, 128), f32),
                narrow,
                struct((TOK, 2 * HID + 128 if turn else HID + 128), bf16),
            ],
            [VMEM] * (7 + len(extra)),
            [VMEM] * 5,
            after=pairs_sib[-1:] if s else pieces[1:],
        )(layers[s], weights[s][1], weights[s + 1][0], *extra, *messages)
        layers.append(layer)
        pairs.append(pair)
        pairs_sib.append(from_sibling(pair))
        pres.append(pre)
        inverses.append(inverse)

    ordered = call(
        order_kernel,
        [struct((3, OWN, PIECE, HID), bf16)] * 4,
        [SMEM] * 4 + [ANY] * 2 + [VMEM] * 4,
        [VMEM] * 4,
        [
            pltpu.VMEM((4, 2, OWN, PIECE, HID), bf16),
            pltpu.VMEM((4, OWN, PIECE, HID), bf16),
            pltpu.SemaphoreType.DMA,
        ],
    )(place, source, *arrivals, *pieces)
    owned = [ordered[0]] + [shift_z(ordered[k], k) for k in (1, 2, 3)]

    grad = cots
    ready, parts = [None] * SECTIONS, [None] * SECTIONS
    after = pairs_sib[-1:]
    for s in reversed(range(SECTIONS)):
        messages = all_of(message)
        if s == SECTIONS - 1:
            pair, back, grad, message = call(
                functools.partial(backward_kernel, True),
                [wide, wide, narrow, struct((TOK, HID), bf16)],
                [VMEM] * 8,
                [VMEM] * 4,
                after=after,
            )(*messages, grad, layers[s], weights[s][0], weights[s - 1][1])
            pairs.append(pair)
            pairs_sib.append(from_sibling(pair))
        elif s > 0:
            back, grad, message = call(
                functools.partial(backward_kernel, False),
                [wide, narrow, struct((TOK, HID), bf16)],
                [VMEM] * 10,
                [VMEM] * 3,
                after=after,
            )(*messages, pres[s], inverses[s], grad, layers[s], weights[s][0], weights[s - 1][1])
        else:
            back = call(close_kernel, wide, [VMEM] * 7, VMEM, after=after)(
                *messages, pres[0], inverses[0], grad
            )
        ready[s] = (pairs[s], back, pairs_sib[s], from_sibling(back))
        if s == 3:
            after = []
        elif s == 2:
            after = [ready[2][3], ready[3][3]]
        elif s == 1:
            odd = first_half(True, place, [ready[3], ready[1]])
            after = odd[:1]
        else:
            even = first_half(False, place, [ready[2], ready[0]])
            after = even[:1]
    across = second_half(True, place, [odd], after)
    along = second_half(False, place, [even], after)
    kept, *sends = call(
        functools.partial(finish_kernel, ((3, 1), (2, 0))),
        [struct((HID, 128), f32)] + [struct((HID, 128), bf16)] * 3,
        [SMEM] + [VMEM] * 8,
        [VMEM] * 4,
        [pltpu.VMEM((SECTIONS, HID, 128), f32)],
    )(place, *across, *along)
    gradients = [kept] + [shift_z(sends[k - 1], k) for k in (1, 2, 3)]
    new_weight, new_first, new_second = call(
        adam_kernel,
        [
            struct((OWN, 128, HID), bf16),
            struct((OWN, 128, HID), f32),
            struct((OWN, 128, HID), f32),
        ],
        [SMEM] + [VMEM] * 8,
        [VMEM] * 3,
    )(place, *gradients, *owned)
    return (new_weight[None], new_first[None], new_second[None])


def solution(mesh):
    in_specs = (
        P("replica", None),
        P("replica", None),
        P(("replica", "section"), None, None, None),
        P(("replica", "section"), None),
        P(("replica", "section"), None),
        P(("replica", "section"), None),
        P(("replica", "section"), None, None, None),
        P(("replica", "section"), None, None, None),
        P(("replica", "section"), None),
    )
    out_specs = (
        P("section", "replica", None, None),
        P("section", "replica", None, None),
        P("section", "replica", None, None),
    )
    return jax.shard_map(
        on_device, mesh=mesh, in_specs=in_specs, out_specs=out_specs, check_vma=False
    )
```

```python
import functools

import jax
import jax.numpy as jnp
from jax import lax
from jax.experimental import pallas as pl
from jax.experimental.pallas import tpu as pltpu
from jax.sharding import PartitionSpec as P


D = 7168
HID = 256
TOK = 128
NBLK = 112
HALF = 56
PIECE = 32
LOCAL = HALF * PIECE
GROUPS = LOCAL // 128
LEFT = 2 * LOCAL + HID
SECTIONS = 4
REPLICAS = 32
DEVICES = 128
OWN = 4
REAL_OWNERS = NBLK // OWN
BIG = 1e6
CHUNK = SECTIONS * PIECE + 16
EVERY = ("replica", "section")

rms_eps = 1e-05
beta_first = 0.9
beta_second = 0.95
step_size = 0.1
adam_eps = 1e-08
SCALE_IN = D ** (-0.5)
SCALE_OUT = HID ** (-0.5)

f32 = jnp.float32
bf16 = jnp.bfloat16
ANY = pl.BlockSpec(memory_space=pl.ANY)
HBM = pl.BlockSpec(memory_space=pltpu.HBM)
SMEM = pl.BlockSpec(memory_space=pltpu.SMEM)
VMEM = pl.BlockSpec(memory_space=pltpu.VMEM)
LIMIT = 12 * 1024 * 1024
BULK = 62 * 1024 * 1024
BYTES_PER_US = 3.4e6


def struct(shape, dtype):
    return jax.ShapeDtypeStruct(shape, dtype)


def call(kernel, out_shape, in_specs, out_specs, scratch=(), after=(), aliases=None, limit=LIMIT, us=1.0):
    waits = len(after)

    def body(*refs):
        kernel(*refs[waits:])

    run = pl.pallas_call(
        body,
        out_shape=out_shape,
        in_specs=[ANY] * waits + in_specs,
        out_specs=out_specs,
        scratch_shapes=list(scratch),
        input_output_aliases={waits + i: o for i, o in (aliases or {}).items()},
        compiler_params=pltpu.CompilerParams(vmem_limit_bytes=limit),
        cost_estimate=pl.CostEstimate(
            flops=0, bytes_accessed=int(us * BYTES_PER_US), transcendentals=0
        ),
    )
    return lambda *arrays: run(*after, *arrays)


def replica_at(x, y, core):
    return ((x % 4) * 4 + (y % 4)) * 2 + core


def shift_xy(block, step_x, step_y):
    route = [
        (replica_at(x, y, c), replica_at(x + step_x, y + step_y, c))
        for x in range(4)
        for y in range(4)
        for c in range(2)
    ]
    return lax.ppermute(block, "replica", route)


def shift_z(block, step):
    return lax.ppermute(block, "section", [(i, (i + step) % 4) for i in range(4)])


def spread(block, axis):
    if axis == "z":
        names = ("replica", "section")
        route = []
        for r in range(REPLICAS):
            step = 1 - 2 * (r % 2)
            route += [(r * 4 + i, r * 4 + (i + step) % 4) for i in range(4)]
        return lax.ppermute(block, names, route)
    route = []
    for x in range(4):
        for y in range(4):
            for c in range(2):
                step = 1 - 2 * c
                to = (x + step, y) if axis == "x" else (x, y + step)
                route.append((replica_at(x, y, c), replica_at(*to, c)))
    return lax.ppermute(block, "replica", route)


def from_sibling(block):
    return lax.ppermute(block, "replica", [(i, i ^ 1) for i in range(REPLICAS)])


def pack_kernel(which, table, blocks, out, room, came, went):
    for part in range(8):
        for s in range(SECTIONS):

            def start(i, carry):
                r = part * 4 + i
                pltpu.make_async_copy(
                    blocks.at[table[which, r * 4 + s]],
                    room.at[r, :, pl.ds(s * PIECE, PIECE)],
                    came.at[part],
                ).start()
                return carry

            lax.fori_loop(0, 4, start, 0)

    def go(part):
        rows = pl.ds(part * 4, 4)
        into = out.at[rows, :, pl.ds(0, SECTIONS * PIECE)]
        return pltpu.make_async_copy(room.at[rows], into, went.at[part])

    for part in range(8):
        rows = pl.ds(part * 4, 4)
        pltpu.make_async_copy(room.at[rows], room.at[rows], came.at[part]).wait()
        go(part).start()
    for part in range(8):
        go(part).wait()


def pack(which, table, blocks, tall, after=()):
    return call(
        functools.partial(pack_kernel, which),
        struct((REPLICAS, 4, tall, HID), bf16),
        [SMEM, ANY],
        HBM,
        [
            pltpu.VMEM((REPLICAS, 4, SECTIONS * PIECE, HID), bf16),
            pltpu.SemaphoreType.DMA((8,)),
            pltpu.SemaphoreType.DMA((8,)),
        ],
        after=after,
        limit=BULK, us=7.4)(table, blocks)


def pack_second_kernel(half, table, blocks, *refs):
    outs, (room, came, went) = refs[:-3], refs[-3:]

    @pl.when(table[2, 0] == 1)
    def _():
        for s in range(SECTIONS):

            def start(r, carry):
                rows = blocks.at[table[1, r * 4 + s], :, pl.ds(half * 16, 16)]
                pltpu.make_async_copy(rows, room.at[s, r], came.at[s]).start()
                return carry

            lax.fori_loop(0, REPLICAS, start, 0, unroll=4)

        def go(s):
            out = outs[0].at[s] if len(outs) == 1 else outs[s]
            return pltpu.make_async_copy(room.at[s], out, went.at[s])

        for s in range(SECTIONS):
            pltpu.make_async_copy(room.at[s], room.at[s], came.at[s]).wait()
            go(s).start()
        for s in range(SECTIONS):
            go(s).wait()


def pack_second(half, table, blocks, after=()):
    shape = (REPLICAS, 4, 16, HID)
    split = [struct(shape, bf16)] * SECTIONS
    whole = [struct((SECTIONS, *shape), bf16)]
    outs = whole if half else split
    return call(
        functools.partial(pack_second_kernel, half),
        outs,
        [SMEM, ANY],
        [HBM] * len(outs),
        [
            pltpu.VMEM((SECTIONS, *shape), bf16),
            pltpu.SemaphoreType.DMA((4,)),
            pltpu.SemaphoreType.DMA((4,)),
        ],
        after=after,
        limit=BULK, us=4.0)(table, blocks)


def take_over_kernel(table, got, in_0, in_1, in_2, in_3, out_0, out_1, out_2, out_3, room, came, went):
    outs = (out_0, out_1, out_2, out_3)

    @pl.when(table[2, 0] == 1)
    def _():
        def come(s):
            return pltpu.make_async_copy(got.at[s], room.at[s], came.at[s])

        def go(s):
            return pltpu.make_async_copy(room.at[s], outs[s], went.at[s])

        for s in range(SECTIONS):
            come(s).start()
        for s in range(SECTIONS):
            come(s).wait()
            go(s).start()
        for s in range(SECTIONS):
            go(s).wait()


def take_over(flag, got, own):
    return call(
        take_over_kernel,
        [struct((REPLICAS, 4, 16, HID), bf16)] * 4,
        [SMEM] + [HBM] * 5,
        [HBM] * 4,
        [
            pltpu.VMEM((SECTIONS, REPLICAS, 4, 16, HID), bf16),
            pltpu.SemaphoreType.DMA((4,)),
            pltpu.SemaphoreType.DMA((4,)),
        ],
        aliases={2: 0, 3: 1, 4: 2, 5: 3},
        limit=BULK, us=4.0)(flag, got, *own)


def relay_places(busy):
    x, y, core, z = busy // 32, (busy // 8) % 4, (busy // 4) % 2, busy % 4
    found = []
    for c in (core, 1 - core):
        step = 1 + 2 * c
        for dx, dy, dz in ((0, 0, 0), (1, 0, 0), (0, 1, 0), (0, 0, 1)):
            chip = (x + dx * step) % 4 * 4 + (y + dy * step) % 4
            found.append((chip * 2 + c) * 4 + (z + dz * step) % 4)
    return found


def add_relayed_kernel(got, place, in_0, in_1, in_2, in_3, buffer, out, room, sem):
    numbers = lax.broadcasted_iota(jnp.int32, (DEVICES, 16), 0)
    lanes = lax.broadcasted_iota(jnp.int32, (DEVICES, 16), 1)
    holds = (lanes == 8) & (got[...] == 1)
    busy = jnp.max(jnp.where(holds, numbers.astype(f32), 0.0)).astype(jnp.int32)
    places = relay_places(busy)
    me = place[4] * 4 + place[3]
    for k, ref in enumerate((in_0, in_1, in_2, in_3)):

        @pl.when((places[k] == me) | (places[4 + k] == me))
        def _():
            come = pltpu.make_async_copy(ref, room, sem.at[0])
            come.start()
            come.wait()
            go = pltpu.make_async_copy(room, out.at[:, :, pl.ds(SECTIONS * PIECE, 16)], sem.at[1])
            go.start()
            go.wait()


def add_relayed(got, place, relays, buffer):
    return call(
        add_relayed_kernel,
        struct((REPLICAS, 4, CHUNK, HID), bf16),
        [VMEM, SMEM] + [HBM] * 5,
        HBM,
        [pltpu.VMEM((REPLICAS, 4, 16, HID), bf16), pltpu.SemaphoreType.DMA((2,))],
        aliases={6: 0},
        limit=BULK, us=2.2)(got, place, *relays, buffer)


def blank_kernel(flag, out):
    pass


def blank(flag):
    return call(blank_kernel, struct((DEVICES, SECTIONS * PIECE, HID), bf16), [SMEM], HBM)(flag)


def fetch(section, place, relays, first, second, out, sem):
    rows = section * PIECE
    if not isinstance(section, int):
        rows = pl.multiple_of(rows, PIECE)
    rows = pl.ds(rows, PIECE)
    extra = pl.ds(SECTIONS * PIECE, 16)

    @pl.when(place < DEVICES)
    def _():
        pltpu.make_async_copy(first.at[place, rows], out, sem).start()

    @pl.when(place >= DEVICES)
    def _():
        @pl.when(place < 2 * DEVICES)
        def _():
            pltpu.make_async_copy(second.at[place - DEVICES, rows], out, sem).start()

        @pl.when(place == 2 * DEVICES)
        def _():
            low, high = relays[section], relays[section + 4]
            pltpu.make_async_copy(first.at[low, extra], out.at[pl.ds(0, 16)], sem).start()
            pltpu.make_async_copy(first.at[high, extra], out.at[pl.ds(16, 16)], sem).start()


def gather_kernel(section, begin, places, relays, first, second, out, sem):
    def start(b, carry):
        fetch(section, places[begin + b], relays, first, second, out.at[b], sem)
        return carry

    lax.fori_loop(0, HALF, start, 0, unroll=8)
    pltpu.make_async_copy(out, out, sem).wait()


def gather(section, begin, places, relays, first, second):
    return call(
        functools.partial(gather_kernel, section, begin),
        struct((HALF, PIECE, HID), bf16),
        [SMEM, SMEM, ANY, ANY],
        ANY,
        [pltpu.SemaphoreType.DMA], us=1.9)(places, relays, first, second)


def tables_kernel(lists, table, labels):
    send_slot, send_dest, send_block = lists[0:1], lists[1:2], lists[2:3]
    code = (send_slot * 128 + send_block).astype(f32)
    lanes = lax.broadcasted_iota(jnp.int32, (DEVICES, 128), 1)
    rows = lax.broadcasted_iota(jnp.int32, (DEVICES, 128), 0)
    entries = (DEVICES, lists.shape[1])
    match = send_dest == lax.broadcasted_iota(jnp.int32, entries, 0)
    low = jnp.min(jnp.where(match, code, BIG), axis=1, keepdims=True)
    high = jnp.max(jnp.where(match, code, -1.0), axis=1, keepdims=True)
    first = jnp.where(low < BIG, low, -1.0)
    second = jnp.where(high > low, high, -1.0)
    any_second = jnp.max(second, axis=0, keepdims=True) >= 0.0
    flag = jnp.broadcast_to(jnp.where(any_second, 1.0, 0.0), (8, 128))
    spare_slot = jnp.where(lanes >= NBLK, lanes - NBLK, lanes).astype(f32)
    slots, named = [], []
    for codes in (first, second):
        along = jnp.broadcast_to(codes, (DEVICES, 128)).T
        slot = jnp.floor(along * (1.0 / 128))
        slots.append(jnp.where(along >= 0.0, slot, spare_slot)[0:8])
        block = jnp.where(along >= 0.0, along - 128.0 * slot + 1.0, 0.0)
        named.append(jnp.where(rows // 4 == lanes // 4, block, 0.0).astype(bf16))
    short = lax.broadcasted_iota(jnp.int32, (8, 128), 0)
    table[...] = jnp.where(
        short == 0, slots[0], jnp.where(short == 1, slots[1], flag)
    ).astype(jnp.int32)
    d = lax.broadcasted_iota(jnp.int32, (DEVICES, 16), 0)
    j = lax.broadcasted_iota(jnp.int32, (DEVICES, 16), 1)
    total = jnp.where(j == 8, jnp.broadcast_to(flag[0:1, 0:16], (DEVICES, 16)), 0.0)
    for n, names in enumerate(named):
        pick = jnp.where(d % 4 == j - 4 * n, 1.0, 0.0).astype(bf16)
        total = total + jnp.dot(names, pick, preferred_element_type=f32)
    result = total.astype(jnp.int32)
    for k in range(OWN):
        own = jnp.broadcast_to(lists[3:4, k : k + 1], (DEVICES, 16))
        result = jnp.where(j == 9 + k, own, result)
    labels[...] = result


def send_tables(moment_dest, send_slot, send_dest, send_block):
    moments = jnp.pad(moment_dest, ((0, 0), (0, send_dest.shape[1] - moment_dest.shape[1])))
    return call(
        tables_kernel,
        [struct((8, 128), jnp.int32), struct((DEVICES, 16), jnp.int32)],
        [VMEM],
        [VMEM] * 2,
        us=1.0,
    )(jnp.concatenate([send_slot, send_dest, send_block, moments], axis=0))


def route_blocks(
    place, acts_in, cotangent, old_blocks, send_slot, send_dest, send_block, moment_dest
):
    blocks = old_blocks.reshape(NBLK, 4, PIECE, HID)
    table, labels = send_tables(moment_dest, send_slot, send_dest, send_block)

    (other,) = pack_second(1, table, blocks)
    table_other = from_sibling(table)
    came = from_sibling(other)
    other, labels = lax.optimization_barrier((other, labels))
    got = lax.all_to_all(labels, EVERY, 0, 0, tiled=True)
    own = pack_second(0, table, blocks, after=[other])
    mine = take_over(table_other, came, own)
    relays = [mine[0], spread(mine[1], "x"), spread(mine[2], "y"), spread(mine[3], "z")]
    buffer = pack(0, table, blocks, CHUNK)

    buffer = add_relayed(got, place, relays, buffer)
    layer_0, cots = quarter(acts_in, cotangent, place[3])
    buffer, got = lax.optimization_barrier((buffer, got))
    holders = got[:, 8]
    alone = jnp.sum(holders) == 1
    numbers = jnp.arange(DEVICES, dtype=jnp.int32)
    busy = jnp.sum(jnp.where(holders > 0, numbers, 0))
    busy = jnp.where(alone, busy, 0)
    relayed_by = jnp.stack(relay_places(busy)).astype(jnp.int32)
    arrived = lax.all_to_all(buffer.reshape(DEVICES, CHUNK, HID), EVERY, 0, 0, tiled=True)

    def second_round():
        again = pack(1, table, blocks, SECTIONS * PIECE)
        return lax.all_to_all(
            again.reshape(DEVICES, SECTIONS * PIECE, HID), EVERY, 0, 0, tiled=True
        )

    arrived, table, alone_now = lax.optimization_barrier((arrived, table, alone))
    spare = lax.cond(alone_now, lambda: blank(table), second_round)

    wanted = jnp.arange(1, NBLK + 1, dtype=jnp.int32)[None, None, :]
    in_first = got[:, 0:4, None] == wanted
    in_second = got[:, 4:8, None] == wanted
    senders = numbers[:, None, None]
    later = jnp.where(alone, 2 * DEVICES, senders + DEVICES)
    places = jnp.sum(jnp.where(in_first, senders, 0) + jnp.where(in_second, later, 0), axis=0)
    places = jnp.clip(places, 0, 2 * DEVICES)
    weights = [
        [gather(s, begin, places[s], relayed_by, arrived, spare) for begin in (0, HALF)]
        for s in range(SECTIONS)
    ]
    return weights, got, (places.reshape(-1), relayed_by, arrived, spare), layer_0, cots


def quarter_kernel(pick, acts, cots, acts_out, cots_out):
    chosen = pick[...]
    for j in range(GROUPS):
        wide = slice(j * 512, (j + 1) * 512)
        narrow = slice(j * 128, (j + 1) * 128)
        acts_out[:, narrow] = jnp.dot(
            acts[:, wide], chosen, preferred_element_type=f32
        ).astype(bf16)
        cots_out[:, narrow] = jnp.dot(
            cots[:, wide], chosen, preferred_element_type=f32
        ).astype(bf16)


def quarter(acts, cots, q):
    rows = jnp.arange(512, dtype=jnp.int32)[:, None]
    columns = jnp.arange(128, dtype=jnp.int32)[None, :]
    pick = (rows == (columns // 32) * 128 + q * 32 + columns % 32).astype(bf16)
    return call(
        quarter_kernel,
        [struct((TOK, LOCAL), bf16)] * 2,
        [VMEM] * 3,
        [VMEM] * 2, us=1.1)(pick, acts, cots)


def flat(weight):
    return weight[...].reshape(LOCAL, HID)


def put_forward(message, layer_in, up_matrix):
    wide = layer_in.astype(f32)
    squares = jnp.sum(wide * wide, axis=1, keepdims=True)
    high = squares.astype(bf16)
    low = (squares - high.astype(f32)).astype(bf16)
    lane = lax.broadcasted_iota(jnp.int32, (TOK, 128), 1)
    message[:, 0:HID] = jnp.dot(layer_in, up_matrix, preferred_element_type=f32).astype(bf16)
    message[:, HID : HID + 128] = jnp.where(
        lane == 0, high.astype(f32), jnp.where(lane == 1, low.astype(f32), 0.0)
    ).astype(bf16)


def take_forward(total):
    squares = total[:, HID : HID + 1] + total[:, HID + 1 : HID + 2]
    inverse = lax.rsqrt(squares * (1.0 / D) + rms_eps)
    pre = total[:, 0:HID] * inverse * SCALE_IN
    return pre, jax.nn.gelu(pre, approximate=True).astype(bf16), inverse


def gelu_slope(v):
    root = 0.7978845608028654
    t = jnp.tanh(root * (v + 0.044715 * v * v * v))
    return 0.5 * (1.0 + t) + 0.5 * v * (1.0 - t * t) * root * (1.0 + 0.134145 * v * v)


def times_t(a, b):
    return lax.dot_general(a, b, (((1,), (1,)), ((), ())), preferred_element_type=f32)


def summed(refs):
    return sum([ref[...].astype(f32) for ref in refs[1:]], refs[0][...].astype(f32))


def open_kernel(layer_in, weight, message):
    put_forward(message, layer_in[...], flat(weight))


def forward_kernel(layer_in, out_matrix, up_next, *refs):
    messages, (act, pre, inverse, layer_out, message) = refs[:4], refs[4:]
    result = forward_step(messages, layer_in, out_matrix, act, pre, inverse, layer_out)
    put_forward(message, result, flat(up_next))


def forward_step(messages, layer_in, out_matrix, act, pre, inverse, layer_out):
    pre_value, act_value, inverse_value = take_forward(summed(messages))
    act[...] = act_value
    pre[...] = pre_value
    inverse[...] = jnp.broadcast_to(inverse_value, (TOK, 128))
    branch = times_t(act_value, flat(out_matrix))
    result = (layer_in[...].astype(f32) + branch * SCALE_OUT).astype(bf16)
    layer_out[...] = result
    return result


def turn_kernel(layer_in, out_matrix, up_next, out_next, cots, *refs):
    messages, (act, pre, inverse, layer_out, message) = refs[:4], refs[4:]
    result = forward_step(messages, layer_in, out_matrix, act, pre, inverse, layer_out)
    put_forward(message, result, flat(up_next))
    message[:, HID + 128 :] = jnp.dot(
        cots[...], flat(out_next), preferred_element_type=f32
    ).astype(bf16)


def backward_kernel(from_forward, *refs):
    messages, refs = refs[:4], refs[4:]
    total = summed(messages)
    if from_forward:
        grad_out, layer_in, up_matrix, out_next, back, grad_in, message = refs
        pre_value, act_value, inverse_value = take_forward(total)
        back[:, LEFT:] = act_value
        grad_act = total[:, HID + 128 :] * SCALE_OUT
    else:
        act, pre, inverse, grad_out, layer_in, up_matrix, out_next, back, grad_in, message = refs
        back[:, LEFT:] = act[...]
        pre_value = pre[...]
        inverse_value = inverse[:, 0:1]
        grad_act = total * SCALE_OUT
    pulled = (grad_act * gelu_slope(pre_value)).astype(bf16)
    back[:, 0:LOCAL] = layer_in[...]
    back[:, LOCAL : 2 * LOCAL] = grad_out[...]
    back[:, 2 * LOCAL : LEFT] = (pulled.astype(f32) * inverse_value).astype(bf16)
    correction = jnp.sum(pulled.astype(f32) * pre_value, axis=1, keepdims=True) * (1.0 / D)
    grad_norm = times_t(pulled, flat(up_matrix)) * SCALE_IN
    normed = layer_in[...].astype(f32) * inverse_value
    result = grad_out[...].astype(f32) + (grad_norm - normed * correction) * inverse_value
    result = result.astype(bf16)
    grad_in[...] = result
    message[...] = jnp.dot(result, flat(out_next), preferred_element_type=f32).astype(bf16)


def close_kernel(*refs):
    messages, (act, pre, inverse, grad_out, layer_in, back) = refs[:4], refs[4:]
    grad_act = summed(messages) * SCALE_OUT
    pulled = (grad_act * gelu_slope(pre[...])).astype(bf16)
    back[:, 0:LOCAL] = layer_in[...]
    back[:, LOCAL : 2 * LOCAL] = grad_out[...]
    back[:, 2 * LOCAL : LEFT] = (pulled.astype(f32) * inverse[:, 0:1]).astype(bf16)
    back[:, LEFT:] = act[...]


def all_of(message):
    return [message] + [shift_z(message, k) for k in (1, 3, 2)]


def products(core, mine, other, chosen, store):
    half = GROUPS // 2

    def product(left, right, scale, start):
        both = jnp.concatenate([mine[:, left], other[:, left]], axis=0)
        turned = both.astype(f32).T.astype(bf16)
        for g in range(half):
            columns = pl.ds(pl.multiple_of(right + (2 * g + core) * 128, 128), 128)
            chosen[0:TOK, g * 128 : (g + 1) * 128] = mine[:, columns]
            chosen[TOK:, g * 128 : (g + 1) * 128] = other[:, columns]
        result = jnp.dot(turned, chosen[...], preferred_element_type=f32) * scale
        for g in range(half):
            store(start + g, result[:, g * 128 : (g + 1) * 128].astype(bf16))

    product(slice(2 * LOCAL, LEFT), 0, SCALE_IN, 0)
    product(slice(LEFT, LEFT + HID), LOCAL, SCALE_OUT, half)
    for owner in range(2 * half, 16):
        store(owner, jnp.zeros((HID, 128), bf16))


def gradient_kernel(x_first, count, place, *refs):
    ins, outs, (chosen, table) = refs[: 2 * count], refs[2 * count : 2 * count + 4], refs[-2:]
    for n in range(count):

        def store(owner, value):
            table[owner, n] = value

        products(place[2], *ins[2 * n : 2 * n + 2], chosen, store)
    for k in range(4):
        for j in range(4):
            if x_first:
                owner = lax.rem(place[0] + k, 4) * 4 + j
            else:
                owner = j * 4 + lax.rem(place[1] + k, 4)
            outs[k][j] = table[owner]


def halve_kernel(x_first, counts, place, *refs):
    mine = place[1] if x_first else place[0]
    outs = refs[4 * len(counts) :]
    for k in range(4):
        chunk = lax.rem(mine + k, 4)
        start = 0
        for n, count in enumerate(counts):
            four = refs[4 * n : 4 * n + 4]
            total = sum([ref[chunk].astype(f32) for ref in four[1:]], four[0][chunk].astype(f32))
            outs[k][start : start + count] = total.astype(outs[k].dtype)
            start += count


def first_half(x_first, place, sections, after=()):
    count = len(sections)
    chunks = call(
        functools.partial(gradient_kernel, x_first, count),
        [struct((4, count, HID, 128), bf16)] * 4,
        [SMEM] + [VMEM] * (2 * count),
        [VMEM] * 4,
        [pltpu.VMEM((2 * TOK, LOCAL // 2), bf16), pltpu.VMEM((16, count, HID, 128), bf16)],
        after=after, us=3.3)(place, *[v for section in sections for v in section])
    step = (1, 0) if x_first else (0, 1)
    return [chunks[0]] + [shift_xy(chunks[k], k * step[0], k * step[1]) for k in (1, 2, 3)]


def second_half(x_first, place, parts, after):
    counts = [part[0].shape[1] for part in parts]
    count = sum(counts)
    kept, *sends = call(
        functools.partial(halve_kernel, x_first, counts),
        [struct((count, HID, 128), f32)] + [struct((count, HID, 128), bf16)] * 3,
        [SMEM] + [VMEM] * (4 * len(parts)),
        [VMEM] * 4,
        after=after, us=1.4)(place, *[v for part in parts for v in part])
    step = (0, 1) if x_first else (1, 0)
    return [kept] + [shift_xy(sends[k - 1], k * step[0], k * step[1]) for k in (1, 2, 3)]


def finish_kernel(places_in, place, *refs):
    groups, refs = refs[: 4 * len(places_in)], refs[4 * len(places_in) :]
    kept, sends, table = refs[0], refs[1:4], refs[4]
    for m, sections in enumerate(places_in):
        four = groups[4 * m : 4 * m + 4]
        for n, section in enumerate(sections):
            table[section] = sum([ref[n].astype(f32) for ref in four[1:]], four[0][n])
    for k in range(4):
        value = table[lax.rem(place[3] + k, 4)]
        if k == 0:
            kept[...] = value
        else:
            sends[k - 1][...] = value.astype(bf16)


def split_moments_kernel(place, first, second, *outs):
    for k in range(4):
        rows = pl.ds(pl.multiple_of(lax.rem(place[3] + k, 4) * PIECE, PIECE), PIECE)
        for a in range(OWN):
            outs[k][0, a] = first[a, rows, :].astype(bf16)
            outs[k][1, a] = second[a, rows, :].astype(bf16)


def order_kernel(place, source, places, relays, first, second, *refs):
    moments, outs, (table, came, sem) = refs[:4], refs[4:8], refs[8:]
    start = jnp.minimum(place[4], REAL_OWNERS - 1) * OWN
    for k in range(4):
        section = lax.rem(place[3] + k, 4)
        for i in range(OWN):
            held = places[section * NBLK + start + i]
            fetch(section, held, relays, first, second, came.at[k, i], sem)
    for k in range(4):
        table[k] = moments[k][...]
    for k in range(4):
        section = lax.rem(place[3] + k, 4)
        for i in range(OWN):
            held = source[section * OWN + i]
            outs[k][1, i] = table[held // OWN, 0, lax.rem(held, OWN)]
            outs[k][2, i] = table[held // OWN, 1, lax.rem(held, OWN)]
    pltpu.make_async_copy(came, came, sem).wait()
    for k in range(4):
        outs[k][0] = came[k]


def adam_kernel(place, *refs):
    gradients, held = refs[:4], refs[4:8]
    weight_out, first_out, second_out = refs[8:]
    real = place[4] < REAL_OWNERS
    for k in range(4):
        q = lax.rem(place[3] + 4 - k, 4)
        rows = pl.ds(pl.multiple_of(q * PIECE, PIECE), PIECE)
        turned = jnp.where(real, gradients[k][...].astype(f32).T, 0.0)
        for i in range(OWN):
            gradient = turned[i * PIECE : (i + 1) * PIECE, :]
            weight = jnp.where(real, held[k][0, i].astype(f32), 0.0)
            first = beta_first * held[k][1, i].astype(f32) + (1.0 - beta_first) * gradient
            second = beta_second * held[k][2, i].astype(f32) + (
                (1.0 - beta_second) * gradient * gradient
            )
            first_out[i, rows, :] = first
            second_out[i, rows, :] = second
            weight_out[i, rows, :] = (
                weight - step_size * first / (jnp.sqrt(second) + adam_eps)
            ).astype(bf16)


def on_device(
    acts_in,
    cotangent,
    old_blocks,
    send_slot,
    send_dest,
    send_block,
    old_first,
    old_second,
    moment_dest,
):
    me_r = lax.axis_index("replica")
    me_z = lax.axis_index("section")
    place = jnp.stack([me_r // 8, (me_r // 2) % 4, me_r % 2, me_z, me_r]).astype(jnp.int32)

    split = call(
        split_moments_kernel,
        [struct((2, OWN, PIECE, HID), bf16)] * 4,
        [SMEM, VMEM, VMEM],
        [VMEM] * 4, us=1.3)(place, old_first[0], old_second[0])
    pieces = [split[0]] + [shift_z(split[k], k) for k in (1, 2, 3)]

    weights, labels, arrivals, layer_0, cots = route_blocks(
        place, acts_in, cotangent, old_blocks, send_slot, send_dest, send_block, moment_dest
    )
    table = lax.dynamic_slice_in_dim(labels, me_r * 4, 4, 0)[:, 9:13]
    distance = (me_z - jnp.arange(SECTIONS, dtype=jnp.int32)) % 4
    held = (distance[:, None] * OWN + jnp.arange(OWN, dtype=jnp.int32)[None, :]).reshape(-1)
    slots = jnp.arange(SECTIONS * OWN, dtype=jnp.int32)
    source = jnp.sum(jnp.where(table.reshape(1, -1) == slots[:, None], held[None, :], 0), axis=1)
    message = call(
        open_kernel, struct((TOK, HID + 128), bf16), [VMEM] * 2, VMEM, us=0.3)(layer_0, weights[0][0])
    layers = [layer_0]
    acts, pres, inverses = [], [], []
    wide = struct((TOK, LEFT + HID), bf16)
    short = struct((TOK, HID), bf16)
    narrow = struct((TOK, LOCAL), bf16)
    for s in range(SECTIONS - 1):
        messages = all_of(message)
        turn = s == SECTIONS - 2
        extra = (weights[s + 1][1], cots) if turn else ()
        act, pre, inverse, layer, message = call(
            turn_kernel if turn else forward_kernel,
            [
                short,
                struct((TOK, HID), f32),
                struct((TOK, 128), f32),
                narrow,
                struct((TOK, 2 * HID + 128 if turn else HID + 128), bf16),
            ],
            [VMEM] * (7 + len(extra)),
            [VMEM] * 5,
            after=() if s else pieces[1:],
        )(layers[s], weights[s][1], weights[s + 1][0], *extra, *messages)
        layers.append(layer)
        acts.append(act)
        pres.append(pre)
        inverses.append(inverse)

    ordered = call(
        order_kernel,
        [struct((3, OWN, PIECE, HID), bf16)] * 4,
        [SMEM] * 4 + [ANY] * 2 + [VMEM] * 4,
        [VMEM] * 4,
        [
            pltpu.VMEM((4, 2, OWN, PIECE, HID), bf16),
            pltpu.VMEM((4, OWN, PIECE, HID), bf16),
            pltpu.SemaphoreType.DMA,
        ], us=1.6)(place, source, *arrivals, *pieces)
    owned = [ordered[0]] + [shift_z(ordered[k], k) for k in (1, 2, 3)]

    grad = cots
    ready = [None] * SECTIONS
    after = []
    for s in reversed(range(SECTIONS)):
        messages = all_of(message)
        if s == SECTIONS - 1:
            back, grad, message = call(
                functools.partial(backward_kernel, True),
                [wide, narrow, short],
                [VMEM] * 8,
                [VMEM] * 3,
                after=after,
            )(*messages, grad, layers[s], weights[s][0], weights[s - 1][1])
        elif s > 0:
            back, grad, message = call(
                functools.partial(backward_kernel, False),
                [wide, narrow, short],
                [VMEM] * 11,
                [VMEM] * 3,
                after=after,
            )(
                *messages, acts[s], pres[s], inverses[s], grad, layers[s], weights[s][0],
                weights[s - 1][1]
            )
        else:
            back = call(close_kernel, wide, [VMEM] * 9, VMEM, after=after)(
                *messages, acts[0], pres[0], inverses[0], grad, layers[0]
            )
        ready[s] = (back, from_sibling(back))
        if s == 3:
            after = []
        elif s == 2:
            after = [ready[2][1], ready[3][1]]
        elif s == 1:
            odd = first_half(True, place, [ready[3], ready[1]])
            after = odd[:1]
        else:
            even = first_half(False, place, [ready[2], ready[0]])
            after = even[:1]
    across = second_half(True, place, [odd], after)
    along = second_half(False, place, [even], after)
    kept, *sends = call(
        functools.partial(finish_kernel, ((3, 1), (2, 0))),
        [struct((HID, 128), f32)] + [struct((HID, 128), bf16)] * 3,
        [SMEM] + [VMEM] * 8,
        [VMEM] * 4,
        [pltpu.VMEM((SECTIONS, HID, 128), f32)], us=0.7)(place, *across, *along)
    gradients = [kept] + [shift_z(sends[k - 1], k) for k in (1, 2, 3)]
    new_weight, new_first, new_second = call(
        adam_kernel,
        [
            struct((OWN, 128, HID), bf16),
            struct((OWN, 128, HID), f32),
            struct((OWN, 128, HID), f32),
        ],
        [SMEM] + [VMEM] * 8,
        [VMEM] * 3, us=2.1)(place, *gradients, *owned)
    return (new_weight[None], new_first[None], new_second[None])


def solution(mesh):
    in_specs = (
        P("replica", None),
        P("replica", None),
        P(("replica", "section"), None, None, None),
        P(("replica", "section"), None),
        P(("replica", "section"), None),
        P(("replica", "section"), None),
        P(("replica", "section"), None, None, None),
        P(("replica", "section"), None, None, None),
        P(("replica", "section"), None),
    )
    out_specs = (
        P("section", "replica", None, None),
        P("section", "replica", None, None),
        P("section", "replica", None, None),
    )
    return jax.shard_map(
        on_device, mesh=mesh, in_specs=in_specs, out_specs=out_specs, check_vma=False
    )
```

```python
import functools

import jax
import jax.numpy as jnp
from jax import lax
from jax.experimental import pallas as pl
from jax.experimental.pallas import tpu as pltpu
from jax.sharding import PartitionSpec as P


D = 7168
HID = 256
TOK = 128
NBLK = 112
HALF = 56
PIECE = 32
LOCAL = HALF * PIECE
GROUPS = LOCAL // 128
LEFT = 2 * LOCAL + HID
SECTIONS = 4
REPLICAS = 32
DEVICES = 128
OWN = 4
REAL_OWNERS = NBLK // OWN
BIG = 1e6
EXTRA = 2 * PIECE
EVERY = ("replica", "section")

rms_eps = 1e-05
beta_first = 0.9
beta_second = 0.95
step_size = 0.1
adam_eps = 1e-08
SCALE_IN = D ** (-0.5)
SCALE_OUT = HID ** (-0.5)

f32 = jnp.float32
bf16 = jnp.bfloat16
ANY = pl.BlockSpec(memory_space=pl.ANY)
HBM = pl.BlockSpec(memory_space=pltpu.HBM)
SMEM = pl.BlockSpec(memory_space=pltpu.SMEM)
VMEM = pl.BlockSpec(memory_space=pltpu.VMEM)
LIMIT = 12 * 1024 * 1024
BULK = 62 * 1024 * 1024
BYTES_PER_US = 3.4e6


def struct(shape, dtype):
    return jax.ShapeDtypeStruct(shape, dtype)


def call(kernel, out_shape, in_specs, out_specs, scratch=(), after=(), aliases=None, limit=LIMIT, us=1.0):
    waits = len(after)

    def body(*refs):
        kernel(*refs[waits:])

    run = pl.pallas_call(
        body,
        out_shape=out_shape,
        in_specs=[ANY] * waits + in_specs,
        out_specs=out_specs,
        scratch_shapes=list(scratch),
        input_output_aliases={waits + i: o for i, o in (aliases or {}).items()},
        compiler_params=pltpu.CompilerParams(vmem_limit_bytes=limit),
        cost_estimate=pl.CostEstimate(
            flops=0, bytes_accessed=int(us * BYTES_PER_US), transcendentals=0
        ),
    )
    return lambda *arrays: run(*after, *arrays)


def replica_at(x, y, core):
    return ((x % 4) * 4 + (y % 4)) * 2 + core


def shift_xy(block, step_x, step_y):
    route = [
        (replica_at(x, y, c), replica_at(x + step_x, y + step_y, c))
        for x in range(4)
        for y in range(4)
        for c in range(2)
    ]
    return lax.ppermute(block, "replica", route)


def shift_z(block, step):
    return lax.ppermute(block, "section", [(i, (i + step) % 4) for i in range(4)])


def spread(block, axis):
    if axis == "z":
        names = ("replica", "section")
        route = []
        for r in range(REPLICAS):
            step = 1 - 2 * (r % 2)
            route += [(r * 4 + i, r * 4 + (i + step) % 4) for i in range(4)]
        return lax.ppermute(block, names, route)
    route = []
    for x in range(4):
        for y in range(4):
            for c in range(2):
                step = 1 - 2 * c
                to = (x + step, y) if axis == "x" else (x, y + step)
                route.append((replica_at(x, y, c), replica_at(*to, c)))
    return lax.ppermute(block, "replica", route)


def from_sibling(block):
    return lax.ppermute(block, "replica", [(i, i ^ 1) for i in range(REPLICAS)])


def pack_kernel(which, sections, table, blocks, out, room, came, went):
    tall = len(sections) * PIECE
    for part in range(8):
        for n, s in enumerate(sections):

            def start(i, carry):
                r = part * 4 + i
                pltpu.make_async_copy(
                    blocks.at[table[which, r * 4 + s]],
                    room.at[r, :, pl.ds(n * PIECE, PIECE)],
                    came.at[part],
                ).start()
                return carry

            lax.fori_loop(0, 4, start, 0)

    def go(part):
        rows = pl.ds(part * 4, 4)
        into = out.at[rows, :, pl.ds(0, tall)]
        return pltpu.make_async_copy(room.at[rows], into, went.at[part])

    for part in range(8):
        rows = pl.ds(part * 4, 4)
        pltpu.make_async_copy(room.at[rows], room.at[rows], came.at[part]).wait()
        go(part).start()
    for part in range(8):
        go(part).wait()


def pack(which, sections, table, blocks, extra=0, after=()):
    tall = len(sections) * PIECE
    return call(
        functools.partial(pack_kernel, which, sections),
        struct((REPLICAS, 4, tall + extra, HID), bf16),
        [SMEM, ANY],
        HBM,
        [
            pltpu.VMEM((REPLICAS, 4, tall, HID), bf16),
            pltpu.SemaphoreType.DMA((8,)),
            pltpu.SemaphoreType.DMA((8,)),
        ],
        after=after,
        limit=BULK,
        us=1.85 * len(sections),
    )(table, blocks)


def pack_second_kernel(half, table, blocks, *refs):
    outs, (room, came, went) = refs[:-3], refs[-3:]

    @pl.when(table[2, 0] == 1)
    def _():
        for s in range(SECTIONS):

            def start(r, carry):
                rows = blocks.at[table[1, r * 4 + s], :, pl.ds(half * 16, 16)]
                pltpu.make_async_copy(rows, room.at[s, r], came.at[s]).start()
                return carry

            lax.fori_loop(0, REPLICAS, start, 0, unroll=4)

        def go(s):
            out = outs[0].at[s] if len(outs) == 1 else outs[s]
            return pltpu.make_async_copy(room.at[s], out, went.at[s])

        for s in range(SECTIONS):
            pltpu.make_async_copy(room.at[s], room.at[s], came.at[s]).wait()
            go(s).start()
        for s in range(SECTIONS):
            go(s).wait()


def pack_second(half, table, blocks, after=()):
    shape = (REPLICAS, 4, 16, HID)
    split = [struct(shape, bf16)] * SECTIONS
    whole = [struct((SECTIONS, *shape), bf16)]
    outs = whole if half else split
    return call(
        functools.partial(pack_second_kernel, half),
        outs,
        [SMEM, ANY],
        [HBM] * len(outs),
        [
            pltpu.VMEM((SECTIONS, *shape), bf16),
            pltpu.SemaphoreType.DMA((4,)),
            pltpu.SemaphoreType.DMA((4,)),
        ],
        after=after,
        limit=BULK, us=4.0)(table, blocks)


def take_over_kernel(table, got, in_0, in_1, in_2, in_3, out_0, out_1, out_2, out_3, room, came, went):
    outs = (out_0, out_1, out_2, out_3)

    @pl.when(table[2, 0] == 1)
    def _():
        def come(s):
            return pltpu.make_async_copy(got.at[s], room.at[s], came.at[s])

        def go(s):
            return pltpu.make_async_copy(room.at[s], outs[s], went.at[s])

        for s in range(SECTIONS):
            come(s).start()
        for s in range(SECTIONS):
            come(s).wait()
            go(s).start()
        for s in range(SECTIONS):
            go(s).wait()


def take_over(flag, got, own):
    return call(
        take_over_kernel,
        [struct((REPLICAS, 4, 16, HID), bf16)] * 4,
        [SMEM] + [HBM] * 5,
        [HBM] * 4,
        [
            pltpu.VMEM((SECTIONS, REPLICAS, 4, 16, HID), bf16),
            pltpu.SemaphoreType.DMA((4,)),
            pltpu.SemaphoreType.DMA((4,)),
        ],
        aliases={2: 0, 3: 1, 4: 2, 5: 3},
        limit=BULK, us=4.0)(flag, got, *own)


def relay_places(busy):
    x, y, core, z = busy // 32, (busy // 8) % 4, (busy // 4) % 2, busy % 4
    found = []
    for c in (core, 1 - core):
        step = 1 + 2 * c
        for dx, dy, dz in ((0, 0, 0), (1, 0, 0), (0, 1, 0), (0, 0, 1)):
            chip = (x + dx * step) % 4 * 4 + (y + dy * step) % 4
            found.append((chip * 2 + c) * 4 + (z + dz * step) % 4)
    return found


def add_relayed_kernel(got, place, in_0, in_1, in_2, in_3, buffer, out, room, sem):
    numbers = lax.broadcasted_iota(jnp.int32, (DEVICES, 16), 0)
    lanes = lax.broadcasted_iota(jnp.int32, (DEVICES, 16), 1)
    holds = (lanes == 8) & (got[...] == 1)
    busy = jnp.max(jnp.where(holds, numbers.astype(f32), 0.0)).astype(jnp.int32)
    places = relay_places(busy)
    me = place[4] * 4 + place[3]
    for k, ref in enumerate((in_0, in_1, in_2, in_3)):

        @pl.when((places[k] == me) | (places[4 + k] == me))
        def _():
            come = pltpu.make_async_copy(ref, room, sem.at[0])
            come.start()
            come.wait()
            go = pltpu.make_async_copy(room, out.at[:, :, pl.ds(EXTRA, 16)], sem.at[1])
            go.start()
            go.wait()


def add_relayed(got, place, relays, buffer):
    return call(
        add_relayed_kernel,
        struct((REPLICAS, 4, EXTRA + 16, HID), bf16),
        [VMEM, SMEM] + [HBM] * 5,
        HBM,
        [pltpu.VMEM((REPLICAS, 4, 16, HID), bf16), pltpu.SemaphoreType.DMA((2,))],
        aliases={6: 0},
        limit=BULK, us=2.2)(got, place, *relays, buffer)


def blank_kernel(flag, out):
    pass


def blank(flag):
    return call(blank_kernel, struct((DEVICES, SECTIONS * PIECE, HID), bf16), [SMEM], HBM)(flag)


def fetch(section, place, relays, firsts, second, out, sem):
    def copy(source, target):
        pltpu.make_async_copy(source, target, sem).start()

    def rows(start):
        if not isinstance(start, int):
            start = pl.multiple_of(start, PIECE)
        return pl.ds(start, PIECE)

    for half in range(2):
        here = section // 2 == half

        def direct():
            @pl.when(place < DEVICES)
            def _():
                copy(firsts[half].at[place, rows((section - 2 * half) * PIECE)], out)

        if not isinstance(section, int):
            pl.when(here)(direct)
        elif here:
            direct()

    @pl.when(place >= DEVICES)
    def _():
        @pl.when(place < 2 * DEVICES)
        def _():
            copy(second.at[place - DEVICES, rows(section * PIECE)], out)

        @pl.when(place == 2 * DEVICES)
        def _():
            extra = pl.ds(EXTRA, 16)
            copy(firsts[1].at[relays[section], extra], out.at[pl.ds(0, 16)])
            copy(firsts[1].at[relays[section + 4], extra], out.at[pl.ds(16, 16)])


def gather_kernel(section, begin, places, relays, early, late, second, out, sem):
    def start(b, carry):
        fetch(section, places[begin + b], relays, (early, late), second, out.at[b], sem)
        return carry

    lax.fori_loop(0, HALF, start, 0, unroll=8)
    pltpu.make_async_copy(out, out, sem).wait()


def gather(section, begin, places, relays, early, late, second):
    return call(
        functools.partial(gather_kernel, section, begin),
        struct((HALF, PIECE, HID), bf16),
        [SMEM, SMEM, ANY, ANY, ANY],
        ANY,
        [pltpu.SemaphoreType.DMA], us=1.9)(places, relays, early, late, second)


def tables_kernel(lists, table, labels):
    send_slot, send_dest, send_block = lists[0:1], lists[1:2], lists[2:3]
    code = (send_slot * 128 + send_block).astype(f32)
    lanes = lax.broadcasted_iota(jnp.int32, (DEVICES, 128), 1)
    rows = lax.broadcasted_iota(jnp.int32, (DEVICES, 128), 0)
    entries = (DEVICES, lists.shape[1])
    match = send_dest == lax.broadcasted_iota(jnp.int32, entries, 0)
    low = jnp.min(jnp.where(match, code, BIG), axis=1, keepdims=True)
    high = jnp.max(jnp.where(match, code, -1.0), axis=1, keepdims=True)
    first = jnp.where(low < BIG, low, -1.0)
    second = jnp.where(high > low, high, -1.0)
    any_second = jnp.max(second, axis=0, keepdims=True) >= 0.0
    flag = jnp.broadcast_to(jnp.where(any_second, 1.0, 0.0), (8, 128))
    spare_slot = jnp.where(lanes >= NBLK, lanes - NBLK, lanes).astype(f32)
    slots, named = [], []
    for codes in (first, second):
        along = jnp.broadcast_to(codes, (DEVICES, 128)).T
        slot = jnp.floor(along * (1.0 / 128))
        slots.append(jnp.where(along >= 0.0, slot, spare_slot)[0:8])
        block = jnp.where(along >= 0.0, along - 128.0 * slot + 1.0, 0.0)
        named.append(jnp.where(rows // 4 == lanes // 4, block, 0.0).astype(bf16))
    short = lax.broadcasted_iota(jnp.int32, (8, 128), 0)
    table[...] = jnp.where(
        short == 0, slots[0], jnp.where(short == 1, slots[1], flag)
    ).astype(jnp.int32)
    d = lax.broadcasted_iota(jnp.int32, (DEVICES, 16), 0)
    j = lax.broadcasted_iota(jnp.int32, (DEVICES, 16), 1)
    total = jnp.where(j == 8, jnp.broadcast_to(flag[0:1, 0:16], (DEVICES, 16)), 0.0)
    for n, names in enumerate(named):
        pick = jnp.where(d % 4 == j - 4 * n, 1.0, 0.0).astype(bf16)
        total = total + jnp.dot(names, pick, preferred_element_type=f32)
    result = total.astype(jnp.int32)
    for k in range(OWN):
        own = jnp.broadcast_to(lists[3:4, k : k + 1], (DEVICES, 16))
        result = jnp.where(j == 9 + k, own, result)
    labels[...] = result


def send_tables(moment_dest, send_slot, send_dest, send_block):
    moments = jnp.pad(moment_dest, ((0, 0), (0, send_dest.shape[1] - moment_dest.shape[1])))
    return call(
        tables_kernel,
        [struct((8, 128), jnp.int32), struct((DEVICES, 16), jnp.int32)],
        [VMEM],
        [VMEM] * 2,
        us=1.0,
    )(jnp.concatenate([send_slot, send_dest, send_block, moments], axis=0))


def route_blocks(
    place, acts_in, cotangent, old_blocks, send_slot, send_dest, send_block, moment_dest
):
    blocks = old_blocks.reshape(NBLK, 4, PIECE, HID)
    table, labels = send_tables(moment_dest, send_slot, send_dest, send_block)

    early = pack(0, (0, 1), table, blocks)
    early, table = lax.optimization_barrier((early, table))
    (other,) = pack_second(1, table, blocks)
    table_other = from_sibling(table)
    came = from_sibling(other)
    own = pack_second(0, table, blocks, after=[other])
    mine = take_over(table_other, came, own)
    buffer = pack(0, (2, 3), table, blocks, 16)
    early = lax.all_to_all(early.reshape(DEVICES, EXTRA, HID), EVERY, 0, 0, tiled=True)
    early, labels, buffer = lax.optimization_barrier((early, labels, buffer))
    relays = [mine[0], spread(mine[1], "x"), spread(mine[2], "y"), spread(mine[3], "z")]
    got = lax.all_to_all(labels, EVERY, 0, 0, tiled=True)
    buffer = add_relayed(got, place, relays, buffer)
    layer_0, cots = quarter(acts_in, cotangent, place[3])
    buffer, got = lax.optimization_barrier((buffer, got))
    holders = got[:, 8]
    alone = jnp.sum(holders) == 1
    numbers = jnp.arange(DEVICES, dtype=jnp.int32)
    busy = jnp.sum(jnp.where(holders > 0, numbers, 0))
    busy = jnp.where(alone, busy, 0)
    relayed_by = jnp.stack(relay_places(busy)).astype(jnp.int32)
    late = lax.all_to_all(buffer.reshape(DEVICES, EXTRA + 16, HID), EVERY, 0, 0, tiled=True)

    def second_round():
        again = pack(1, tuple(range(SECTIONS)), table, blocks)
        return lax.all_to_all(
            again.reshape(DEVICES, SECTIONS * PIECE, HID), EVERY, 0, 0, tiled=True
        )

    late, table, alone_now = lax.optimization_barrier((late, table, alone))
    spare = lax.cond(alone_now, lambda: blank(table), second_round)

    wanted = jnp.arange(1, NBLK + 1, dtype=jnp.int32)[None, None, :]
    in_first = got[:, 0:4, None] == wanted
    in_second = got[:, 4:8, None] == wanted
    senders = numbers[:, None, None]
    later = jnp.where(alone, 2 * DEVICES, senders + DEVICES)
    places = jnp.sum(jnp.where(in_first, senders, 0) + jnp.where(in_second, later, 0), axis=0)
    places = jnp.clip(places, 0, 2 * DEVICES)
    weights = [
        [gather(s, begin, places[s], relayed_by, early, late, spare) for begin in (0, HALF)]
        for s in range(SECTIONS)
    ]
    return weights, got, (places.reshape(-1), relayed_by, early, late, spare), layer_0, cots


def quarter_kernel(pick, acts, cots, acts_out, cots_out):
    chosen = pick[...]
    for j in range(GROUPS):
        wide = slice(j * 512, (j + 1) * 512)
        narrow = slice(j * 128, (j + 1) * 128)
        acts_out[:, narrow] = jnp.dot(
            acts[:, wide], chosen, preferred_element_type=f32
        ).astype(bf16)
        cots_out[:, narrow] = jnp.dot(
            cots[:, wide], chosen, preferred_element_type=f32
        ).astype(bf16)


def quarter(acts, cots, q):
    rows = jnp.arange(512, dtype=jnp.int32)[:, None]
    columns = jnp.arange(128, dtype=jnp.int32)[None, :]
    pick = (rows == (columns // 32) * 128 + q * 32 + columns % 32).astype(bf16)
    return call(
        quarter_kernel,
        [struct((TOK, LOCAL), bf16)] * 2,
        [VMEM] * 3,
        [VMEM] * 2, us=1.1)(pick, acts, cots)


def flat(weight):
    return weight[...].reshape(LOCAL, HID)


def put_forward(message, layer_in, up_matrix):
    wide = layer_in.astype(f32)
    squares = jnp.sum(wide * wide, axis=1, keepdims=True)
    high = squares.astype(bf16)
    low = (squares - high.astype(f32)).astype(bf16)
    lane = lax.broadcasted_iota(jnp.int32, (TOK, 128), 1)
    message[:, 0:HID] = jnp.dot(layer_in, up_matrix, preferred_element_type=f32).astype(bf16)
    message[:, HID : HID + 128] = jnp.where(
        lane == 0, high.astype(f32), jnp.where(lane == 1, low.astype(f32), 0.0)
    ).astype(bf16)


def take_forward(total):
    squares = total[:, HID : HID + 1] + total[:, HID + 1 : HID + 2]
    inverse = lax.rsqrt(squares * (1.0 / D) + rms_eps)
    pre = total[:, 0:HID] * inverse * SCALE_IN
    return pre, jax.nn.gelu(pre, approximate=True).astype(bf16), inverse


def gelu_slope(v):
    root = 0.7978845608028654
    t = jnp.tanh(root * (v + 0.044715 * v * v * v))
    return 0.5 * (1.0 + t) + 0.5 * v * (1.0 - t * t) * root * (1.0 + 0.134145 * v * v)


def times_t(a, b):
    return lax.dot_general(a, b, (((1,), (1,)), ((), ())), preferred_element_type=f32)


def summed(refs):
    return sum([ref[...].astype(f32) for ref in refs[1:]], refs[0][...].astype(f32))


def open_kernel(layer_in, weight, message):
    put_forward(message, layer_in[...], flat(weight))


def forward_kernel(layer_in, out_matrix, up_next, *refs):
    messages, (act, pre, inverse, layer_out, message) = refs[:4], refs[4:]
    result = forward_step(messages, layer_in, out_matrix, act, pre, inverse, layer_out)
    put_forward(message, result, flat(up_next))


def forward_step(messages, layer_in, out_matrix, act, pre, inverse, layer_out):
    pre_value, act_value, inverse_value = take_forward(summed(messages))
    act[...] = act_value
    pre[...] = pre_value
    inverse[...] = jnp.broadcast_to(inverse_value, (TOK, 128))
    branch = times_t(act_value, flat(out_matrix))
    result = (layer_in[...].astype(f32) + branch * SCALE_OUT).astype(bf16)
    layer_out[...] = result
    return result


def turn_kernel(layer_in, out_matrix, up_next, out_next, cots, *refs):
    messages, (act, pre, inverse, layer_out, message) = refs[:4], refs[4:]
    result = forward_step(messages, layer_in, out_matrix, act, pre, inverse, layer_out)
    put_forward(message, result, flat(up_next))
    message[:, HID + 128 :] = jnp.dot(
        cots[...], flat(out_next), preferred_element_type=f32
    ).astype(bf16)


def backward_kernel(from_forward, *refs):
    messages, refs = refs[:4], refs[4:]
    total = summed(messages)
    if from_forward:
        grad_out, layer_in, up_matrix, out_next, back, grad_in, message = refs
        pre_value, act_value, inverse_value = take_forward(total)
        back[:, LEFT:] = act_value
        grad_act = total[:, HID + 128 :] * SCALE_OUT
    else:
        act, pre, inverse, grad_out, layer_in, up_matrix, out_next, back, grad_in, message = refs
        back[:, LEFT:] = act[...]
        pre_value = pre[...]
        inverse_value = inverse[:, 0:1]
        grad_act = total * SCALE_OUT
    pulled = (grad_act * gelu_slope(pre_value)).astype(bf16)
    back[:, 0:LOCAL] = layer_in[...]
    back[:, LOCAL : 2 * LOCAL] = grad_out[...]
    back[:, 2 * LOCAL : LEFT] = (pulled.astype(f32) * inverse_value).astype(bf16)
    correction = jnp.sum(pulled.astype(f32) * pre_value, axis=1, keepdims=True) * (1.0 / D)
    grad_norm = times_t(pulled, flat(up_matrix)) * SCALE_IN
    normed = layer_in[...].astype(f32) * inverse_value
    result = grad_out[...].astype(f32) + (grad_norm - normed * correction) * inverse_value
    result = result.astype(bf16)
    grad_in[...] = result
    message[...] = jnp.dot(result, flat(out_next), preferred_element_type=f32).astype(bf16)


def close_kernel(*refs):
    messages, (act, pre, inverse, grad_out, layer_in, back) = refs[:4], refs[4:]
    grad_act = summed(messages) * SCALE_OUT
    pulled = (grad_act * gelu_slope(pre[...])).astype(bf16)
    back[:, 0:LOCAL] = layer_in[...]
    back[:, LOCAL : 2 * LOCAL] = grad_out[...]
    back[:, 2 * LOCAL : LEFT] = (pulled.astype(f32) * inverse[:, 0:1]).astype(bf16)
    back[:, LEFT:] = act[...]


def all_of(message):
    return [message] + [shift_z(message, k) for k in (1, 3, 2)]


def products(core, mine, other, chosen, store):
    half = GROUPS // 2

    def product(left, right, scale, start):
        both = jnp.concatenate([mine[:, left], other[:, left]], axis=0)
        turned = both.astype(f32).T.astype(bf16)
        for g in range(half):
            columns = pl.ds(pl.multiple_of(right + (2 * g + core) * 128, 128), 128)
            chosen[0:TOK, g * 128 : (g + 1) * 128] = mine[:, columns]
            chosen[TOK:, g * 128 : (g + 1) * 128] = other[:, columns]
        result = jnp.dot(turned, chosen[...], preferred_element_type=f32) * scale
        for g in range(half):
            store(start + g, result[:, g * 128 : (g + 1) * 128].astype(bf16))

    product(slice(2 * LOCAL, LEFT), 0, SCALE_IN, 0)
    product(slice(LEFT, LEFT + HID), LOCAL, SCALE_OUT, half)
    for owner in range(2 * half, 16):
        store(owner, jnp.zeros((HID, 128), bf16))


def gradient_kernel(x_first, count, place, *refs):
    ins, outs, (chosen, table) = refs[: 2 * count], refs[2 * count : 2 * count + 4], refs[-2:]
    for n in range(count):

        def store(owner, value):
            table[owner, n] = value

        products(place[2], *ins[2 * n : 2 * n + 2], chosen, store)
    for k in range(4):
        for j in range(4):
            if x_first:
                owner = lax.rem(place[0] + k, 4) * 4 + j
            else:
                owner = j * 4 + lax.rem(place[1] + k, 4)
            outs[k][j] = table[owner]


def halve_kernel(x_first, counts, place, *refs):
    mine = place[1] if x_first else place[0]
    outs = refs[4 * len(counts) :]
    for k in range(4):
        chunk = lax.rem(mine + k, 4)
        start = 0
        for n, count in enumerate(counts):
            four = refs[4 * n : 4 * n + 4]
            total = sum([ref[chunk].astype(f32) for ref in four[1:]], four[0][chunk].astype(f32))
            outs[k][start : start + count] = total.astype(outs[k].dtype)
            start += count


def first_half(x_first, place, sections, after=()):
    count = len(sections)
    chunks = call(
        functools.partial(gradient_kernel, x_first, count),
        [struct((4, count, HID, 128), bf16)] * 4,
        [SMEM] + [VMEM] * (2 * count),
        [VMEM] * 4,
        [pltpu.VMEM((2 * TOK, LOCAL // 2), bf16), pltpu.VMEM((16, count, HID, 128), bf16)],
        after=after, us=3.3)(place, *[v for section in sections for v in section])
    step = (1, 0) if x_first else (0, 1)
    return [chunks[0]] + [shift_xy(chunks[k], k * step[0], k * step[1]) for k in (1, 2, 3)]


def second_half(x_first, place, parts, after):
    counts = [part[0].shape[1] for part in parts]
    count = sum(counts)
    kept, *sends = call(
        functools.partial(halve_kernel, x_first, counts),
        [struct((count, HID, 128), f32)] + [struct((count, HID, 128), bf16)] * 3,
        [SMEM] + [VMEM] * (4 * len(parts)),
        [VMEM] * 4,
        after=after, us=1.4)(place, *[v for part in parts for v in part])
    step = (0, 1) if x_first else (1, 0)
    return [kept] + [shift_xy(sends[k - 1], k * step[0], k * step[1]) for k in (1, 2, 3)]


def finish_kernel(places_in, place, *refs):
    groups, refs = refs[: 4 * len(places_in)], refs[4 * len(places_in) :]
    kept, sends, table = refs[0], refs[1:4], refs[4]
    for m, sections in enumerate(places_in):
        four = groups[4 * m : 4 * m + 4]
        for n, section in enumerate(sections):
            table[section] = sum([ref[n].astype(f32) for ref in four[1:]], four[0][n])
    for k in range(4):
        value = table[lax.rem(place[3] + k, 4)]
        if k == 0:
            kept[...] = value
        else:
            sends[k - 1][...] = value.astype(bf16)


def split_moments_kernel(place, first, second, *outs):
    for k in range(4):
        rows = pl.ds(pl.multiple_of(lax.rem(place[3] + k, 4) * PIECE, PIECE), PIECE)
        for a in range(OWN):
            outs[k][0, a] = first[a, rows, :].astype(bf16)
            outs[k][1, a] = second[a, rows, :].astype(bf16)


def order_kernel(place, source, places, relays, early, late, second, *refs):
    moments, outs, (table, came, sem) = refs[:4], refs[4:8], refs[8:]
    start = jnp.minimum(place[4], REAL_OWNERS - 1) * OWN
    for k in range(4):
        section = lax.rem(place[3] + k, 4)
        for i in range(OWN):
            held = places[section * NBLK + start + i]
            fetch(section, held, relays, (early, late), second, came.at[k, i], sem)
    for k in range(4):
        table[k] = moments[k][...]
    for k in range(4):
        section = lax.rem(place[3] + k, 4)
        for i in range(OWN):
            held = source[section * OWN + i]
            outs[k][1, i] = table[held // OWN, 0, lax.rem(held, OWN)]
            outs[k][2, i] = table[held // OWN, 1, lax.rem(held, OWN)]
    pltpu.make_async_copy(came, came, sem).wait()
    for k in range(4):
        outs[k][0] = came[k]


def adam_kernel(place, *refs):
    gradients, held = refs[:4], refs[4:8]
    weight_out, first_out, second_out = refs[8:]
    real = place[4] < REAL_OWNERS
    for k in range(4):
        q = lax.rem(place[3] + 4 - k, 4)
        rows = pl.ds(pl.multiple_of(q * PIECE, PIECE), PIECE)
        turned = jnp.where(real, gradients[k][...].astype(f32).T, 0.0)
        for i in range(OWN):
            gradient = turned[i * PIECE : (i + 1) * PIECE, :]
            weight = jnp.where(real, held[k][0, i].astype(f32), 0.0)
            first = beta_first * held[k][1, i].astype(f32) + (1.0 - beta_first) * gradient
            second = beta_second * held[k][2, i].astype(f32) + (
                (1.0 - beta_second) * gradient * gradient
            )
            first_out[i, rows, :] = first
            second_out[i, rows, :] = second
            weight_out[i, rows, :] = (
                weight - step_size * first / (jnp.sqrt(second) + adam_eps)
            ).astype(bf16)


def on_device(
    acts_in,
    cotangent,
    old_blocks,
    send_slot,
    send_dest,
    send_block,
    old_first,
    old_second,
    moment_dest,
):
    me_r = lax.axis_index("replica")
    me_z = lax.axis_index("section")
    place = jnp.stack([me_r // 8, (me_r // 2) % 4, me_r % 2, me_z, me_r]).astype(jnp.int32)

    split = call(
        split_moments_kernel,
        [struct((2, OWN, PIECE, HID), bf16)] * 4,
        [SMEM, VMEM, VMEM],
        [VMEM] * 4, us=1.3)(place, old_first[0], old_second[0])
    pieces = [split[0]] + [shift_z(split[k], k) for k in (1, 2, 3)]

    weights, labels, arrivals, layer_0, cots = route_blocks(
        place, acts_in, cotangent, old_blocks, send_slot, send_dest, send_block, moment_dest
    )
    table = lax.dynamic_slice_in_dim(labels, me_r * 4, 4, 0)[:, 9:13]
    distance = (me_z - jnp.arange(SECTIONS, dtype=jnp.int32)) % 4
    held = (distance[:, None] * OWN + jnp.arange(OWN, dtype=jnp.int32)[None, :]).reshape(-1)
    slots = jnp.arange(SECTIONS * OWN, dtype=jnp.int32)
    source = jnp.sum(jnp.where(table.reshape(1, -1) == slots[:, None], held[None, :], 0), axis=1)
    message = call(
        open_kernel, struct((TOK, HID + 128), bf16), [VMEM] * 2, VMEM, us=0.3)(layer_0, weights[0][0])
    layers = [layer_0]
    acts, pres, inverses = [], [], []
    wide = struct((TOK, LEFT + HID), bf16)
    short = struct((TOK, HID), bf16)
    narrow = struct((TOK, LOCAL), bf16)
    for s in range(SECTIONS - 1):
        messages = all_of(message)
        turn = s == SECTIONS - 2
        extra = (weights[s + 1][1], cots) if turn else ()
        act, pre, inverse, layer, message = call(
            turn_kernel if turn else forward_kernel,
            [
                short,
                struct((TOK, HID), f32),
                struct((TOK, 128), f32),
                narrow,
                struct((TOK, 2 * HID + 128 if turn else HID + 128), bf16),
            ],
            [VMEM] * (7 + len(extra)),
            [VMEM] * 5,
            after=() if s else pieces[1:],
        )(layers[s], weights[s][1], weights[s + 1][0], *extra, *messages)
        layers.append(layer)
        acts.append(act)
        pres.append(pre)
        inverses.append(inverse)

    ordered = call(
        order_kernel,
        [struct((3, OWN, PIECE, HID), bf16)] * 4,
        [SMEM] * 4 + [ANY] * 3 + [VMEM] * 4,
        [VMEM] * 4,
        [
            pltpu.VMEM((4, 2, OWN, PIECE, HID), bf16),
            pltpu.VMEM((4, OWN, PIECE, HID), bf16),
            pltpu.SemaphoreType.DMA,
        ], us=1.6)(place, source, *arrivals, *pieces)
    owned = [ordered[0]] + [shift_z(ordered[k], k) for k in (1, 2, 3)]

    grad = cots
    ready = [None] * SECTIONS
    after = []
    for s in reversed(range(SECTIONS)):
        messages = all_of(message)
        if s == SECTIONS - 1:
            back, grad, message = call(
                functools.partial(backward_kernel, True),
                [wide, narrow, short],
                [VMEM] * 8,
                [VMEM] * 3,
                after=after,
            )(*messages, grad, layers[s], weights[s][0], weights[s - 1][1])
        elif s > 0:
            back, grad, message = call(
                functools.partial(backward_kernel, False),
                [wide, narrow, short],
                [VMEM] * 11,
                [VMEM] * 3,
                after=after,
            )(
                *messages, acts[s], pres[s], inverses[s], grad, layers[s], weights[s][0],
                weights[s - 1][1]
            )
        else:
            back = call(close_kernel, wide, [VMEM] * 9, VMEM, after=after)(
                *messages, acts[0], pres[0], inverses[0], grad, layers[0]
            )
        ready[s] = (back, from_sibling(back))
        if s == 3:
            after = []
        elif s == 2:
            after = [ready[2][1], ready[3][1]]
        elif s == 1:
            odd = first_half(True, place, [ready[3], ready[1]])
            after = odd[:1]
        else:
            even = first_half(False, place, [ready[2], ready[0]])
            after = even[:1]
    across = second_half(True, place, [odd], after)
    along = second_half(False, place, [even], after)
    kept, *sends = call(
        functools.partial(finish_kernel, ((3, 1), (2, 0))),
        [struct((HID, 128), f32)] + [struct((HID, 128), bf16)] * 3,
        [SMEM] + [VMEM] * 8,
        [VMEM] * 4,
        [pltpu.VMEM((SECTIONS, HID, 128), f32)], us=0.7)(place, *across, *along)
    gradients = [kept] + [shift_z(sends[k - 1], k) for k in (1, 2, 3)]
    new_weight, new_first, new_second = call(
        adam_kernel,
        [
            struct((OWN, 128, HID), bf16),
            struct((OWN, 128, HID), f32),
            struct((OWN, 128, HID), f32),
        ],
        [SMEM] + [VMEM] * 8,
        [VMEM] * 3, us=2.1)(place, *gradients, *owned)
    return (new_weight[None], new_first[None], new_second[None])


def solution(mesh):
    in_specs = (
        P("replica", None),
        P("replica", None),
        P(("replica", "section"), None, None, None),
        P(("replica", "section"), None),
        P(("replica", "section"), None),
        P(("replica", "section"), None),
        P(("replica", "section"), None, None, None),
        P(("replica", "section"), None, None, None),
        P(("replica", "section"), None),
    )
    out_specs = (
        P("section", "replica", None, None),
        P("section", "replica", None, None),
        P("section", "replica", None, None),
    )
    return jax.shard_map(
        on_device, mesh=mesh, in_specs=in_specs, out_specs=out_specs, check_vma=False
    )
```

```python
import functools

import jax
import jax.numpy as jnp
from jax import lax
from jax.experimental import pallas as pl
from jax.experimental.pallas import tpu as pltpu
from jax.sharding import PartitionSpec as P


D = 7168
HID = 256
TOK = 128
NBLK = 112
HALF = 56
PIECE = 32
LOCAL = HALF * PIECE
GROUPS = LOCAL // 128
LEFT = 2 * LOCAL + HID
SECTIONS = 4
REPLICAS = 32
DEVICES = 128
OWN = 4
REAL_OWNERS = NBLK // OWN
BIG = 1e6
EXTRA = 2 * PIECE
EVERY = ("replica", "section")

rms_eps = 1e-05
beta_first = 0.9
beta_second = 0.95
step_size = 0.1
adam_eps = 1e-08
SCALE_IN = D ** (-0.5)
SCALE_OUT = HID ** (-0.5)

f32 = jnp.float32
bf16 = jnp.bfloat16
ANY = pl.BlockSpec(memory_space=pl.ANY)
HBM = pl.BlockSpec(memory_space=pltpu.HBM)
SMEM = pl.BlockSpec(memory_space=pltpu.SMEM)
VMEM = pl.BlockSpec(memory_space=pltpu.VMEM)
LIMIT = 12 * 1024 * 1024
BULK = 62 * 1024 * 1024
BYTES_PER_US = 3.4e6


def struct(shape, dtype):
    return jax.ShapeDtypeStruct(shape, dtype)


def call(kernel, out_shape, in_specs, out_specs, scratch=(), after=(), aliases=None, limit=LIMIT, us=1.0):
    waits = len(after)

    def body(*refs):
        kernel(*refs[waits:])

    run = pl.pallas_call(
        body,
        out_shape=out_shape,
        in_specs=[ANY] * waits + in_specs,
        out_specs=out_specs,
        scratch_shapes=list(scratch),
        input_output_aliases={waits + i: o for i, o in (aliases or {}).items()},
        compiler_params=pltpu.CompilerParams(vmem_limit_bytes=limit),
        cost_estimate=pl.CostEstimate(
            flops=0, bytes_accessed=int(us * BYTES_PER_US), transcendentals=0
        ),
    )
    return lambda *arrays: run(*after, *arrays)


def replica_at(x, y, core):
    return ((x % 4) * 4 + (y % 4)) * 2 + core


def shift_xy(block, step_x, step_y):
    route = [
        (replica_at(x, y, c), replica_at(x + step_x, y + step_y, c))
        for x in range(4)
        for y in range(4)
        for c in range(2)
    ]
    return lax.ppermute(block, "replica", route)


def shift_z(block, step):
    return lax.ppermute(block, "section", [(i, (i + step) % 4) for i in range(4)])


def spread(block, axis):
    if axis == "z":
        names = ("replica", "section")
        route = []
        for r in range(REPLICAS):
            step = 1 - 2 * (r % 2)
            route += [(r * 4 + i, r * 4 + (i + step) % 4) for i in range(4)]
        return lax.ppermute(block, names, route)
    route = []
    for x in range(4):
        for y in range(4):
            for c in range(2):
                step = 1 - 2 * c
                to = (x + step, y) if axis == "x" else (x, y + step)
                route.append((replica_at(x, y, c), replica_at(*to, c)))
    return lax.ppermute(block, "replica", route)


def from_sibling(block):
    return lax.ppermute(block, "replica", [(i, i ^ 1) for i in range(REPLICAS)])


def pack_kernel(which, sections, table, blocks, out, room, came, went):
    tall = len(sections) * PIECE
    for part in range(8):
        for n, s in enumerate(sections):

            def start(i, carry):
                r = part * 4 + i
                pltpu.make_async_copy(
                    blocks.at[table[which, r * 4 + s]],
                    room.at[r, :, pl.ds(n * PIECE, PIECE)],
                    came.at[part],
                ).start()
                return carry

            lax.fori_loop(0, 4, start, 0)

    def go(part):
        rows = pl.ds(part * 4, 4)
        into = out.at[rows, :, pl.ds(0, tall)]
        return pltpu.make_async_copy(room.at[rows], into, went.at[part])

    for part in range(8):
        rows = pl.ds(part * 4, 4)
        pltpu.make_async_copy(room.at[rows], room.at[rows], came.at[part]).wait()
        go(part).start()
    for part in range(8):
        go(part).wait()


def pack(which, sections, table, blocks, extra=0, after=()):
    tall = len(sections) * PIECE
    return call(
        functools.partial(pack_kernel, which, sections),
        struct((REPLICAS, 4, tall + extra, HID), bf16),
        [SMEM, ANY],
        HBM,
        [
            pltpu.VMEM((REPLICAS, 4, tall, HID), bf16),
            pltpu.SemaphoreType.DMA((8,)),
            pltpu.SemaphoreType.DMA((8,)),
        ],
        after=after,
        limit=BULK,
        us=1.85 * len(sections),
    )(table, blocks)


def pack_second_kernel(half, table, blocks, *refs):
    outs, (room, came, went) = refs[:-3], refs[-3:]

    @pl.when(table[2, 0] == 1)
    def _():
        for s in range(SECTIONS):

            def start(r, carry):
                rows = blocks.at[table[1, r * 4 + s], :, pl.ds(half * 16, 16)]
                pltpu.make_async_copy(rows, room.at[s, r], came.at[s]).start()
                return carry

            lax.fori_loop(0, REPLICAS, start, 0, unroll=4)

        def go(s):
            out = outs[0].at[s] if len(outs) == 1 else outs[s]
            return pltpu.make_async_copy(room.at[s], out, went.at[s])

        for s in range(SECTIONS):
            pltpu.make_async_copy(room.at[s], room.at[s], came.at[s]).wait()
            go(s).start()
        for s in range(SECTIONS):
            go(s).wait()


def pack_second(half, table, blocks, after=()):
    shape = (REPLICAS, 4, 16, HID)
    split = [struct(shape, bf16)] * SECTIONS
    whole = [struct((SECTIONS, *shape), bf16)]
    outs = whole if half else split
    return call(
        functools.partial(pack_second_kernel, half),
        outs,
        [SMEM, ANY],
        [HBM] * len(outs),
        [
            pltpu.VMEM((SECTIONS, *shape), bf16),
            pltpu.SemaphoreType.DMA((4,)),
            pltpu.SemaphoreType.DMA((4,)),
        ],
        after=after,
        limit=BULK, us=4.0)(table, blocks)


def take_over_kernel(table, got, in_0, in_1, in_2, in_3, out_0, out_1, out_2, out_3, room, came, went):
    outs = (out_0, out_1, out_2, out_3)

    @pl.when(table[2, 0] == 1)
    def _():
        def come(s):
            return pltpu.make_async_copy(got.at[s], room.at[s], came.at[s])

        def go(s):
            return pltpu.make_async_copy(room.at[s], outs[s], went.at[s])

        for s in range(SECTIONS):
            come(s).start()
        for s in range(SECTIONS):
            come(s).wait()
            go(s).start()
        for s in range(SECTIONS):
            go(s).wait()


def take_over(flag, got, own):
    return call(
        take_over_kernel,
        [struct((REPLICAS, 4, 16, HID), bf16)] * 4,
        [SMEM] + [HBM] * 5,
        [HBM] * 4,
        [
            pltpu.VMEM((SECTIONS, REPLICAS, 4, 16, HID), bf16),
            pltpu.SemaphoreType.DMA((4,)),
            pltpu.SemaphoreType.DMA((4,)),
        ],
        aliases={2: 0, 3: 1, 4: 2, 5: 3},
        limit=BULK, us=4.0)(flag, got, *own)


def relay_places(busy):
    x, y, core, z = busy // 32, (busy // 8) % 4, (busy // 4) % 2, busy % 4
    found = []
    for c in (core, 1 - core):
        step = 1 + 2 * c
        for dx, dy, dz in ((0, 0, 0), (1, 0, 0), (0, 1, 0), (0, 0, 1)):
            chip = (x + dx * step) % 4 * 4 + (y + dy * step) % 4
            found.append((chip * 2 + c) * 4 + (z + dz * step) % 4)
    return found


def add_relayed_kernel(got, place, in_0, in_1, in_2, in_3, buffer, out, room, sem):
    numbers = lax.broadcasted_iota(jnp.int32, (DEVICES, 16), 0)
    lanes = lax.broadcasted_iota(jnp.int32, (DEVICES, 16), 1)
    holds = (lanes == 8) & (got[...] == 1)
    busy = jnp.max(jnp.where(holds, numbers.astype(f32), 0.0)).astype(jnp.int32)
    places = relay_places(busy)
    me = place[4] * 4 + place[3]
    for k, ref in enumerate((in_0, in_1, in_2, in_3)):

        @pl.when((places[k] == me) | (places[4 + k] == me))
        def _():
            come = pltpu.make_async_copy(ref, room, sem.at[0])
            come.start()
            come.wait()
            go = pltpu.make_async_copy(room, out.at[:, :, pl.ds(EXTRA, 16)], sem.at[1])
            go.start()
            go.wait()


def add_relayed(got, place, relays, buffer):
    return call(
        add_relayed_kernel,
        struct((REPLICAS, 4, EXTRA + 16, HID), bf16),
        [VMEM, SMEM] + [HBM] * 5,
        HBM,
        [pltpu.VMEM((REPLICAS, 4, 16, HID), bf16), pltpu.SemaphoreType.DMA((2,))],
        aliases={6: 0},
        limit=BULK, us=2.2)(got, place, *relays, buffer)


def blank_kernel(flag, out):
    pass


def blank(flag):
    return call(blank_kernel, struct((DEVICES, SECTIONS * PIECE, HID), bf16), [SMEM], HBM)(flag)


def fetch(section, place, relays, firsts, second, out, sem):
    def copy(source, target):
        pltpu.make_async_copy(source, target, sem).start()

    def rows(start):
        if not isinstance(start, int):
            start = pl.multiple_of(start, PIECE)
        return pl.ds(start, PIECE)

    for half in range(2):
        here = section // 2 == half

        def direct():
            @pl.when(place < DEVICES)
            def _():
                copy(firsts[half].at[place, rows((section - 2 * half) * PIECE)], out)

        if not isinstance(section, int):
            pl.when(here)(direct)
        elif here:
            direct()

    @pl.when(place >= DEVICES)
    def _():
        @pl.when(place < 2 * DEVICES)
        def _():
            copy(second.at[place - DEVICES, rows(section * PIECE)], out)

        @pl.when(place == 2 * DEVICES)
        def _():
            extra = pl.ds(EXTRA, 16)
            copy(firsts[1].at[relays[section], extra], out.at[pl.ds(0, 16)])
            copy(firsts[1].at[relays[section + 4], extra], out.at[pl.ds(16, 16)])


def gather_kernel(section, begin, places, relays, early, late, second, out, sem):
    def start(b, carry):
        fetch(section, places[begin + b], relays, (early, late), second, out.at[b], sem)
        return carry

    lax.fori_loop(0, HALF, start, 0, unroll=8)
    pltpu.make_async_copy(out, out, sem).wait()


def gather(section, begin, places, relays, early, late, second):
    return call(
        functools.partial(gather_kernel, section, begin),
        struct((HALF, PIECE, HID), bf16),
        [SMEM, SMEM, ANY, ANY, ANY],
        ANY,
        [pltpu.SemaphoreType.DMA], us=1.9)(places, relays, early, late, second)


def tables_kernel(lists, table, labels):
    send_slot, send_dest, send_block = lists[0:1], lists[1:2], lists[2:3]
    code = (send_slot * 128 + send_block).astype(f32)
    lanes = lax.broadcasted_iota(jnp.int32, (DEVICES, 128), 1)
    rows = lax.broadcasted_iota(jnp.int32, (DEVICES, 128), 0)
    entries = (DEVICES, lists.shape[1])
    match = send_dest == lax.broadcasted_iota(jnp.int32, entries, 0)
    low = jnp.min(jnp.where(match, code, BIG), axis=1, keepdims=True)
    high = jnp.max(jnp.where(match, code, -1.0), axis=1, keepdims=True)
    first = jnp.where(low < BIG, low, -1.0)
    second = jnp.where(high > low, high, -1.0)
    any_second = jnp.max(second, axis=0, keepdims=True) >= 0.0
    flag = jnp.broadcast_to(jnp.where(any_second, 1.0, 0.0), (8, 128))
    spare_slot = jnp.where(lanes >= NBLK, lanes - NBLK, lanes).astype(f32)
    slots, named = [], []
    for codes in (first, second):
        along = jnp.broadcast_to(codes, (DEVICES, 128)).T
        slot = jnp.floor(along * (1.0 / 128))
        slots.append(jnp.where(along >= 0.0, slot, spare_slot)[0:8])
        block = jnp.where(along >= 0.0, along - 128.0 * slot + 1.0, 0.0)
        named.append(jnp.where(rows // 4 == lanes // 4, block, 0.0).astype(bf16))
    short = lax.broadcasted_iota(jnp.int32, (8, 128), 0)
    table[...] = jnp.where(
        short == 0, slots[0], jnp.where(short == 1, slots[1], flag)
    ).astype(jnp.int32)
    d = lax.broadcasted_iota(jnp.int32, (DEVICES, 16), 0)
    j = lax.broadcasted_iota(jnp.int32, (DEVICES, 16), 1)
    total = jnp.where(j == 8, jnp.broadcast_to(flag[0:1, 0:16], (DEVICES, 16)), 0.0)
    for n, names in enumerate(named):
        pick = jnp.where(d % 4 == j - 4 * n, 1.0, 0.0).astype(bf16)
        total = total + jnp.dot(names, pick, preferred_element_type=f32)
    result = total.astype(jnp.int32)
    for k in range(OWN):
        own = jnp.broadcast_to(lists[3:4, k : k + 1], (DEVICES, 16))
        result = jnp.where(j == 9 + k, own, result)
    labels[...] = result


def send_tables(moment_dest, send_slot, send_dest, send_block):
    moments = jnp.pad(moment_dest, ((0, 0), (0, send_dest.shape[1] - moment_dest.shape[1])))
    return call(
        tables_kernel,
        [struct((8, 128), jnp.int32), struct((DEVICES, 16), jnp.int32)],
        [VMEM],
        [VMEM] * 2,
        us=1.0,
    )(jnp.concatenate([send_slot, send_dest, send_block, moments], axis=0))


def route_blocks(
    place, acts_in, cotangent, old_blocks, send_slot, send_dest, send_block, moment_dest
):
    blocks = old_blocks.reshape(NBLK, 4, PIECE, HID)
    table, labels = send_tables(moment_dest, send_slot, send_dest, send_block)

    early = pack(0, (0, 1), table, blocks)
    early, table = lax.optimization_barrier((early, table))
    (other,) = pack_second(1, table, blocks)
    table_other = from_sibling(table)
    came = from_sibling(other)
    own = pack_second(0, table, blocks, after=[other])
    mine = take_over(table_other, came, own)
    buffer = pack(0, (2, 3), table, blocks, 16)
    early = lax.all_to_all(early.reshape(DEVICES, EXTRA, HID), EVERY, 0, 0, tiled=True)
    early, labels, buffer = lax.optimization_barrier((early, labels, buffer))
    relays = [mine[0], spread(mine[1], "x"), spread(mine[2], "y"), spread(mine[3], "z")]
    got = lax.all_to_all(labels, EVERY, 0, 0, tiled=True)
    buffer = add_relayed(got, place, relays, buffer)
    layer_0, cots = quarter(acts_in, cotangent, place[3])
    buffer, got = lax.optimization_barrier((buffer, got))
    holders = got[:, 8]
    alone = jnp.sum(holders) == 1
    numbers = jnp.arange(DEVICES, dtype=jnp.int32)
    busy = jnp.sum(jnp.where(holders > 0, numbers, 0))
    busy = jnp.where(alone, busy, 0)
    relayed_by = jnp.stack(relay_places(busy)).astype(jnp.int32)
    late = lax.all_to_all(buffer.reshape(DEVICES, EXTRA + 16, HID), EVERY, 0, 0, tiled=True)

    def second_round():
        again = pack(1, tuple(range(SECTIONS)), table, blocks)
        return lax.all_to_all(
            again.reshape(DEVICES, SECTIONS * PIECE, HID), EVERY, 0, 0, tiled=True
        )

    late, table, alone_now = lax.optimization_barrier((late, table, alone))
    spare = lax.cond(alone_now, lambda: blank(table), second_round)

    wanted = jnp.arange(1, NBLK + 1, dtype=jnp.int32)[None, None, :]
    in_first = got[:, 0:4, None] == wanted
    in_second = got[:, 4:8, None] == wanted
    senders = numbers[:, None, None]
    later = jnp.where(alone, 2 * DEVICES, senders + DEVICES)
    places = jnp.sum(jnp.where(in_first, senders, 0) + jnp.where(in_second, later, 0), axis=0)
    places = jnp.clip(places, 0, 2 * DEVICES)
    weights = [
        [gather(s, begin, places[s], relayed_by, early, late, spare) for begin in (0, HALF)]
        for s in range(SECTIONS)
    ]
    return weights, got, (places.reshape(-1), relayed_by, early, late, spare), layer_0, cots


def quarter_kernel(pick, acts, cots, acts_out, cots_out):
    chosen = pick[...]
    for j in range(GROUPS):
        wide = slice(j * 512, (j + 1) * 512)
        narrow = slice(j * 128, (j + 1) * 128)
        acts_out[:, narrow] = jnp.dot(
            acts[:, wide], chosen, preferred_element_type=f32
        ).astype(bf16)
        cots_out[:, narrow] = jnp.dot(
            cots[:, wide], chosen, preferred_element_type=f32
        ).astype(bf16)


def quarter(acts, cots, q):
    rows = jnp.arange(512, dtype=jnp.int32)[:, None]
    columns = jnp.arange(128, dtype=jnp.int32)[None, :]
    pick = (rows == (columns // 32) * 128 + q * 32 + columns % 32).astype(bf16)
    return call(
        quarter_kernel,
        [struct((TOK, LOCAL), bf16)] * 2,
        [VMEM] * 3,
        [VMEM] * 2, us=1.1)(pick, acts, cots)


def flat(weight):
    return weight[...].reshape(LOCAL, HID)


def put_forward(message, layer_in, up_matrix):
    wide = layer_in.astype(f32)
    squares = jnp.sum(wide * wide, axis=1, keepdims=True)
    high = squares.astype(bf16)
    low = (squares - high.astype(f32)).astype(bf16)
    lane = lax.broadcasted_iota(jnp.int32, (TOK, 128), 1)
    message[:, 0:HID] = jnp.dot(layer_in, up_matrix, preferred_element_type=f32).astype(bf16)
    message[:, HID : HID + 128] = jnp.where(
        lane == 0, high.astype(f32), jnp.where(lane == 1, low.astype(f32), 0.0)
    ).astype(bf16)


def take_forward(total):
    squares = total[:, HID : HID + 1] + total[:, HID + 1 : HID + 2]
    inverse = lax.rsqrt(squares * (1.0 / D) + rms_eps)
    pre = total[:, 0:HID] * inverse * SCALE_IN
    return pre, jax.nn.gelu(pre, approximate=True).astype(bf16), inverse


def gelu_slope(v):
    root = 0.7978845608028654
    t = jnp.tanh(root * (v + 0.044715 * v * v * v))
    return 0.5 * (1.0 + t) + 0.5 * v * (1.0 - t * t) * root * (1.0 + 0.134145 * v * v)


def times_t(a, b):
    return lax.dot_general(a, b, (((1,), (1,)), ((), ())), preferred_element_type=f32)


def summed(refs):
    return sum([ref[...].astype(f32) for ref in refs[1:]], refs[0][...].astype(f32))


def open_kernel(layer_in, weight, message):
    put_forward(message, layer_in[...], flat(weight))


def forward_kernel(layer_in, out_matrix, up_next, *refs):
    messages, (act, pre, inverse, layer_out, message) = refs[:4], refs[4:]
    result = forward_step(messages, layer_in, out_matrix, act, pre, inverse, layer_out)
    put_forward(message, result, flat(up_next))


def forward_step(messages, layer_in, out_matrix, act, pre, inverse, layer_out):
    pre_value, act_value, inverse_value = take_forward(summed(messages))
    act[...] = act_value
    pre[...] = pre_value
    inverse[...] = jnp.broadcast_to(inverse_value, (TOK, 128))
    branch = times_t(act_value, flat(out_matrix))
    result = (layer_in[...].astype(f32) + branch * SCALE_OUT).astype(bf16)
    layer_out[...] = result
    return result


def turn_kernel(layer_in, out_matrix, up_next, out_next, cots, *refs):
    messages, (act, pre, inverse, layer_out, message) = refs[:4], refs[4:]
    result = forward_step(messages, layer_in, out_matrix, act, pre, inverse, layer_out)
    put_forward(message, result, flat(up_next))
    message[:, HID + 128 :] = jnp.dot(
        cots[...], flat(out_next), preferred_element_type=f32
    ).astype(bf16)


def backward_kernel(from_forward, *refs):
    messages, refs = refs[:4], refs[4:]
    total = summed(messages)
    if from_forward:
        grad_out, layer_in, up_matrix, out_next, back, grad_in, message = refs
        pre_value, act_value, inverse_value = take_forward(total)
        back[:, LEFT:] = act_value
        grad_act = total[:, HID + 128 :] * SCALE_OUT
    else:
        act, pre, inverse, grad_out, layer_in, up_matrix, out_next, back, grad_in, message = refs
        back[:, LEFT:] = act[...]
        pre_value = pre[...]
        inverse_value = inverse[:, 0:1]
        grad_act = total * SCALE_OUT
    pulled = (grad_act * gelu_slope(pre_value)).astype(bf16)
    back[:, 0:LOCAL] = layer_in[...]
    back[:, LOCAL : 2 * LOCAL] = grad_out[...]
    back[:, 2 * LOCAL : LEFT] = (pulled.astype(f32) * inverse_value).astype(bf16)
    correction = jnp.sum(pulled.astype(f32) * pre_value, axis=1, keepdims=True) * (1.0 / D)
    grad_norm = times_t(pulled, flat(up_matrix)) * SCALE_IN
    normed = layer_in[...].astype(f32) * inverse_value
    result = grad_out[...].astype(f32) + (grad_norm - normed * correction) * inverse_value
    result = result.astype(bf16)
    grad_in[...] = result
    message[...] = jnp.dot(result, flat(out_next), preferred_element_type=f32).astype(bf16)


def close_kernel(*refs):
    messages, (act, pre, inverse, grad_out, layer_in, back) = refs[:4], refs[4:]
    grad_act = summed(messages) * SCALE_OUT
    pulled = (grad_act * gelu_slope(pre[...])).astype(bf16)
    back[:, 0:LOCAL] = layer_in[...]
    back[:, LOCAL : 2 * LOCAL] = grad_out[...]
    back[:, 2 * LOCAL : LEFT] = (pulled.astype(f32) * inverse[:, 0:1]).astype(bf16)
    back[:, LEFT:] = act[...]


def all_of(message):
    return [message] + [shift_z(message, k) for k in (1, 3, 2)]


def products(core, mine, other, small, small_sib, chosen, store):
    half = GROUPS // 2

    def product(n, right, scale, start):
        both = jnp.concatenate([small[n], small_sib[n]], axis=0)
        turned = both.astype(f32).T.astype(bf16)
        for g in range(half):
            columns = pl.ds(pl.multiple_of(right + (2 * g + core) * 128, 128), 128)
            chosen[0:TOK, g * 128 : (g + 1) * 128] = mine[:, columns]
            chosen[TOK:, g * 128 : (g + 1) * 128] = other[:, columns]
        result = jnp.dot(turned, chosen[...], preferred_element_type=f32) * scale
        for g in range(half):
            store(start + g, result[:, g * 128 : (g + 1) * 128].astype(bf16))

    product(0, 0, SCALE_IN, 0)
    product(1, LOCAL, SCALE_OUT, half)
    for owner in range(2 * half, 16):
        store(owner, jnp.zeros((HID, 128), bf16))


def deal(x_first, place, table, outs):
    for k in range(4):
        for j in range(4):
            if x_first:
                owner = lax.rem(place[0] + k, 4) * 4 + j
            else:
                owner = j * 4 + lax.rem(place[1] + k, 4)
            outs[k][j] = table[owner]


def gradient_kernel(x_first, count, place, *refs):
    ins, outs, (chosen, table) = refs[: 2 * count], refs[2 * count : 2 * count + 4], refs[-2:]
    for n in range(count):

        def store(owner, value):
            table[owner, n] = value

        mine, other = ins[2 * n : 2 * n + 2]
        small, small_sib = [
            [ref[:, 2 * LOCAL : LEFT], ref[:, LEFT:]] for ref in (mine, other)
        ]
        products(place[2], mine, other, small, small_sib, chosen, store)
    deal(x_first, place, table, outs)


def table_kernel(place, mine, other, table, chosen):
    def store(owner, value):
        table[owner] = value

    small, small_sib = [[ref[:, 2 * LOCAL : LEFT], ref[:, LEFT:]] for ref in (mine, other)]
    products(place[2], mine, other, small, small_sib, chosen, store)


def last_gradient_kernel(place, earlier, mine, other, *refs):
    outs, (chosen, table) = refs[:4], refs[4:]

    def store(owner, value):
        table[owner, 1] = value

    for owner in range(16):
        table[owner, 0] = earlier[owner]
    small, small_sib = [[ref[:, 2 * LOCAL : LEFT], ref[:, LEFT:]] for ref in (mine, other)]
    products(place[2], mine, other, small, small_sib, chosen, store)
    deal(False, place, table, outs)


def last_half(place, arrays):
    chunks = call(
        last_gradient_kernel,
        [struct((4, 2, HID, 128), bf16)] * 4,
        [SMEM] + [VMEM] * 3,
        [VMEM] * 4,
        [pltpu.VMEM((2 * TOK, LOCAL // 2), bf16), pltpu.VMEM((16, 2, HID, 128), bf16)],
        us=2.0,
    )(place, *arrays)
    return [chunks[0]] + [shift_xy(chunks[k], 0, k) for k in (1, 2, 3)]


def halve_kernel(x_first, counts, place, *refs):
    mine = place[1] if x_first else place[0]
    outs = refs[4 * len(counts) :]
    for k in range(4):
        chunk = lax.rem(mine + k, 4)
        start = 0
        for n, count in enumerate(counts):
            four = refs[4 * n : 4 * n + 4]
            total = sum([ref[chunk].astype(f32) for ref in four[1:]], four[0][chunk].astype(f32))
            outs[k][start : start + count] = total.astype(outs[k].dtype)
            start += count


def first_half(x_first, place, sections, after=()):
    count = len(sections)
    chunks = call(
        functools.partial(gradient_kernel, x_first, count),
        [struct((4, count, HID, 128), bf16)] * 4,
        [SMEM] + [VMEM] * (2 * count),
        [VMEM] * 4,
        [pltpu.VMEM((2 * TOK, LOCAL // 2), bf16), pltpu.VMEM((16, count, HID, 128), bf16)],
        after=after, us=3.3)(place, *[v for section in sections for v in section])
    step = (1, 0) if x_first else (0, 1)
    return [chunks[0]] + [shift_xy(chunks[k], k * step[0], k * step[1]) for k in (1, 2, 3)]


def second_half(x_first, place, parts, after):
    counts = [part[0].shape[1] for part in parts]
    count = sum(counts)
    kept, *sends = call(
        functools.partial(halve_kernel, x_first, counts),
        [struct((count, HID, 128), f32)] + [struct((count, HID, 128), bf16)] * 3,
        [SMEM] + [VMEM] * (4 * len(parts)),
        [VMEM] * 4,
        after=after, us=1.4)(place, *[v for part in parts for v in part])
    step = (0, 1) if x_first else (1, 0)
    return [kept] + [shift_xy(sends[k - 1], k * step[0], k * step[1]) for k in (1, 2, 3)]


def finish_kernel(places_in, place, *refs):
    groups, refs = refs[: 4 * len(places_in)], refs[4 * len(places_in) :]
    kept, sends, table = refs[0], refs[1:4], refs[4]
    for m, sections in enumerate(places_in):
        four = groups[4 * m : 4 * m + 4]
        for n, section in enumerate(sections):
            table[section] = sum([ref[n].astype(f32) for ref in four[1:]], four[0][n])
    for k in range(4):
        value = table[lax.rem(place[3] + k, 4)]
        if k == 0:
            kept[...] = value
        else:
            sends[k - 1][...] = value.astype(bf16)


def split_moments_kernel(place, first, second, *outs):
    for k in range(4):
        rows = pl.ds(pl.multiple_of(lax.rem(place[3] + k, 4) * PIECE, PIECE), PIECE)
        for a in range(OWN):
            outs[k][0, a] = first[a, rows, :].astype(bf16)
            outs[k][1, a] = second[a, rows, :].astype(bf16)


def order_kernel(place, source, places, relays, early, late, second, *refs):
    moments, outs, (table, came, sem) = refs[:4], refs[4:8], refs[8:]
    start = jnp.minimum(place[4], REAL_OWNERS - 1) * OWN
    for k in range(4):
        section = lax.rem(place[3] + k, 4)
        for i in range(OWN):
            held = places[section * NBLK + start + i]
            fetch(section, held, relays, (early, late), second, came.at[k, i], sem)
    for k in range(4):
        table[k] = moments[k][...]
    for k in range(4):
        section = lax.rem(place[3] + k, 4)
        for i in range(OWN):
            held = source[section * OWN + i]
            outs[k][1, i] = table[held // OWN, 0, lax.rem(held, OWN)]
            outs[k][2, i] = table[held // OWN, 1, lax.rem(held, OWN)]
    pltpu.make_async_copy(came, came, sem).wait()
    for k in range(4):
        outs[k][0] = came[k]


def adam_kernel(place, *refs):
    gradients, held = refs[:4], refs[4:8]
    weight_out, first_out, second_out = refs[8:]
    real = place[4] < REAL_OWNERS
    for k in range(4):
        q = lax.rem(place[3] + 4 - k, 4)
        rows = pl.ds(pl.multiple_of(q * PIECE, PIECE), PIECE)
        turned = jnp.where(real, gradients[k][...].astype(f32).T, 0.0)
        for i in range(OWN):
            gradient = turned[i * PIECE : (i + 1) * PIECE, :]
            weight = jnp.where(real, held[k][0, i].astype(f32), 0.0)
            first = beta_first * held[k][1, i].astype(f32) + (1.0 - beta_first) * gradient
            second = beta_second * held[k][2, i].astype(f32) + (
                (1.0 - beta_second) * gradient * gradient
            )
            first_out[i, rows, :] = first
            second_out[i, rows, :] = second
            weight_out[i, rows, :] = (
                weight - step_size * first / (jnp.sqrt(second) + adam_eps)
            ).astype(bf16)


def on_device(
    acts_in,
    cotangent,
    old_blocks,
    send_slot,
    send_dest,
    send_block,
    old_first,
    old_second,
    moment_dest,
):
    me_r = lax.axis_index("replica")
    me_z = lax.axis_index("section")
    place = jnp.stack([me_r // 8, (me_r // 2) % 4, me_r % 2, me_z, me_r]).astype(jnp.int32)

    split = call(
        split_moments_kernel,
        [struct((2, OWN, PIECE, HID), bf16)] * 4,
        [SMEM, VMEM, VMEM],
        [VMEM] * 4, us=1.3)(place, old_first[0], old_second[0])
    pieces = [split[0]] + [shift_z(split[k], k) for k in (1, 2, 3)]

    weights, labels, arrivals, layer_0, cots = route_blocks(
        place, acts_in, cotangent, old_blocks, send_slot, send_dest, send_block, moment_dest
    )
    table = lax.dynamic_slice_in_dim(labels, me_r * 4, 4, 0)[:, 9:13]
    distance = (me_z - jnp.arange(SECTIONS, dtype=jnp.int32)) % 4
    held = (distance[:, None] * OWN + jnp.arange(OWN, dtype=jnp.int32)[None, :]).reshape(-1)
    slots = jnp.arange(SECTIONS * OWN, dtype=jnp.int32)
    source = jnp.sum(jnp.where(table.reshape(1, -1) == slots[:, None], held[None, :], 0), axis=1)
    message = call(
        open_kernel, struct((TOK, HID + 128), bf16), [VMEM] * 2, VMEM, us=0.3)(layer_0, weights[0][0])
    layers = [layer_0]
    acts, pres, inverses = [], [], []
    wide = struct((TOK, LEFT + HID), bf16)
    short = struct((TOK, HID), bf16)
    narrow = struct((TOK, LOCAL), bf16)
    for s in range(SECTIONS - 1):
        messages = all_of(message)
        turn = s == SECTIONS - 2
        extra = (weights[s + 1][1], cots) if turn else ()
        act, pre, inverse, layer, message = call(
            turn_kernel if turn else forward_kernel,
            [
                short,
                struct((TOK, HID), f32),
                struct((TOK, 128), f32),
                narrow,
                struct((TOK, 2 * HID + 128 if turn else HID + 128), bf16),
            ],
            [VMEM] * (7 + len(extra)),
            [VMEM] * 5,
            after=() if s else pieces[1:],
        )(layers[s], weights[s][1], weights[s + 1][0], *extra, *messages)
        layers.append(layer)
        acts.append(act)
        pres.append(pre)
        inverses.append(inverse)

    ordered = call(
        order_kernel,
        [struct((3, OWN, PIECE, HID), bf16)] * 4,
        [SMEM] * 4 + [ANY] * 3 + [VMEM] * 4,
        [VMEM] * 4,
        [
            pltpu.VMEM((4, 2, OWN, PIECE, HID), bf16),
            pltpu.VMEM((4, OWN, PIECE, HID), bf16),
            pltpu.SemaphoreType.DMA,
        ], us=1.6)(place, source, *arrivals, *pieces)
    owned = [ordered[0]] + [shift_z(ordered[k], k) for k in (1, 2, 3)]

    grad = cots
    ready = [None] * SECTIONS
    after = []
    for s in reversed(range(SECTIONS)):
        messages = all_of(message)
        if s == SECTIONS - 1:
            back, grad, message = call(
                functools.partial(backward_kernel, True),
                [wide, narrow, short],
                [VMEM] * 8,
                [VMEM] * 3,
                after=after,
            )(*messages, grad, layers[s], weights[s][0], weights[s - 1][1])
        elif s > 0:
            back, grad, message = call(
                functools.partial(backward_kernel, False),
                [wide, narrow, short],
                [VMEM] * 11,
                [VMEM] * 3,
                after=after,
            )(
                *messages, acts[s], pres[s], inverses[s], grad, layers[s], weights[s][0],
                weights[s - 1][1]
            )
        else:
            back = call(close_kernel, wide, [VMEM] * 9, VMEM, after=after)(
                *messages, acts[0], pres[0], inverses[0], grad, layers[0]
            )
        ready[s] = (back, from_sibling(back))
        if s == 3:
            after = []
        elif s == 2:
            after = [ready[2][1], ready[3][1]]
        elif s == 1:
            odd = first_half(True, place, [ready[3], ready[1]])
            earlier = call(
                table_kernel,
                struct((16, HID, 128), bf16),
                [SMEM] + [VMEM] * 2,
                VMEM,
                [pltpu.VMEM((2 * TOK, LOCAL // 2), bf16)],
                us=1.6,
            )(place, *ready[2])
            after = [odd[0], earlier]
        else:
            even = last_half(place, (earlier, *ready[0]))
            after = even[:1]
    across = second_half(True, place, [odd], [*after, ordered[0]])
    along = second_half(False, place, [even], after)
    kept, *sends = call(
        functools.partial(finish_kernel, ((3, 1), (2, 0))),
        [struct((HID, 128), f32)] + [struct((HID, 128), bf16)] * 3,
        [SMEM] + [VMEM] * 8,
        [VMEM] * 4,
        [pltpu.VMEM((SECTIONS, HID, 128), f32)], us=0.7)(place, *across, *along)
    gradients = [kept] + [shift_z(sends[k - 1], k) for k in (1, 2, 3)]
    new_weight, new_first, new_second = call(
        adam_kernel,
        [
            struct((OWN, 128, HID), bf16),
            struct((OWN, 128, HID), f32),
            struct((OWN, 128, HID), f32),
        ],
        [SMEM] + [VMEM] * 8,
        [VMEM] * 3, us=2.1)(place, *gradients, *owned)
    return (new_weight[None], new_first[None], new_second[None])


def solution(mesh):
    in_specs = (
        P("replica", None),
        P("replica", None),
        P(("replica", "section"), None, None, None),
        P(("replica", "section"), None),
        P(("replica", "section"), None),
        P(("replica", "section"), None),
        P(("replica", "section"), None, None, None),
        P(("replica", "section"), None, None, None),
        P(("replica", "section"), None),
    )
    out_specs = (
        P("section", "replica", None, None),
        P("section", "replica", None, None),
        P("section", "replica", None, None),
    )
    return jax.shard_map(
        on_device, mesh=mesh, in_specs=in_specs, out_specs=out_specs, check_vma=False
    )
```

```python
import functools

import jax
import jax.numpy as jnp
from jax import lax
from jax.experimental import pallas as pl
from jax.experimental.pallas import tpu as pltpu
from jax.sharding import PartitionSpec as P


D = 7168
HID = 256
TOK = 128
NBLK = 112
HALF = 56
PIECE = 32
LOCAL = HALF * PIECE
GROUPS = LOCAL // 128
LEFT = 2 * LOCAL + HID
SECTIONS = 4
REPLICAS = 32
DEVICES = 128
OWN = 4
REAL_OWNERS = NBLK // OWN
BIG = 1e6
EXTRA = 2 * PIECE
EVERY = ("replica", "section")

rms_eps = 1e-05
beta_first = 0.9
beta_second = 0.95
step_size = 0.1
adam_eps = 1e-08
SCALE_IN = D ** (-0.5)
SCALE_OUT = HID ** (-0.5)

f32 = jnp.float32
bf16 = jnp.bfloat16
ANY = pl.BlockSpec(memory_space=pl.ANY)
HBM = pl.BlockSpec(memory_space=pltpu.HBM)
SMEM = pl.BlockSpec(memory_space=pltpu.SMEM)
VMEM = pl.BlockSpec(memory_space=pltpu.VMEM)
LIMIT = 12 * 1024 * 1024
BULK = 62 * 1024 * 1024
BYTES_PER_US = 3.4e6


def struct(shape, dtype):
    return jax.ShapeDtypeStruct(shape, dtype)


def call(kernel, out_shape, in_specs, out_specs, scratch=(), after=(), aliases=None, limit=LIMIT, us=1.0):
    waits = len(after)

    def body(*refs):
        kernel(*refs[waits:])

    run = pl.pallas_call(
        body,
        out_shape=out_shape,
        in_specs=[ANY] * waits + in_specs,
        out_specs=out_specs,
        scratch_shapes=list(scratch),
        input_output_aliases={waits + i: o for i, o in (aliases or {}).items()},
        compiler_params=pltpu.CompilerParams(vmem_limit_bytes=limit),
        cost_estimate=pl.CostEstimate(
            flops=0, bytes_accessed=int(us * BYTES_PER_US), transcendentals=0
        ),
    )
    return lambda *arrays: run(*after, *arrays)


def replica_at(x, y, core):
    return ((x % 4) * 4 + (y % 4)) * 2 + core


def shift_xy(block, step_x, step_y):
    route = [
        (replica_at(x, y, c), replica_at(x + step_x, y + step_y, c))
        for x in range(4)
        for y in range(4)
        for c in range(2)
    ]
    return lax.ppermute(block, "replica", route)


def shift_z(block, step):
    return lax.ppermute(block, "section", [(i, (i + step) % 4) for i in range(4)])


def spread(block, axis):
    if axis == "z":
        names = ("replica", "section")
        route = []
        for r in range(REPLICAS):
            step = 1 - 2 * (r % 2)
            route += [(r * 4 + i, r * 4 + (i + step) % 4) for i in range(4)]
        return lax.ppermute(block, names, route)
    route = []
    for x in range(4):
        for y in range(4):
            for c in range(2):
                step = 1 - 2 * c
                to = (x + step, y) if axis == "x" else (x, y + step)
                route.append((replica_at(x, y, c), replica_at(*to, c)))
    return lax.ppermute(block, "replica", route)


def from_sibling(block):
    return lax.ppermute(block, "replica", [(i, i ^ 1) for i in range(REPLICAS)])


def pack_kernel(which, sections, table, blocks, out, room, came, went):
    tall = len(sections) * PIECE
    for part in range(8):
        for n, s in enumerate(sections):

            def start(i, carry):
                r = part * 4 + i
                pltpu.make_async_copy(
                    blocks.at[table[which, r * 4 + s]],
                    room.at[r, :, pl.ds(n * PIECE, PIECE)],
                    came.at[part],
                ).start()
                return carry

            lax.fori_loop(0, 4, start, 0)

    def go(part):
        rows = pl.ds(part * 4, 4)
        into = out.at[rows, :, pl.ds(0, tall)]
        return pltpu.make_async_copy(room.at[rows], into, went.at[part])

    for part in range(8):
        rows = pl.ds(part * 4, 4)
        pltpu.make_async_copy(room.at[rows], room.at[rows], came.at[part]).wait()
        go(part).start()
    for part in range(8):
        go(part).wait()


def pack(which, sections, table, blocks, extra=0, after=()):
    tall = len(sections) * PIECE
    return call(
        functools.partial(pack_kernel, which, sections),
        struct((REPLICAS, 4, tall + extra, HID), bf16),
        [SMEM, ANY],
        HBM,
        [
            pltpu.VMEM((REPLICAS, 4, tall, HID), bf16),
            pltpu.SemaphoreType.DMA((8,)),
            pltpu.SemaphoreType.DMA((8,)),
        ],
        after=after,
        limit=BULK,
        us=1.85 * len(sections),
    )(table, blocks)


def pack_second_kernel(half, table, blocks, *refs):
    outs, (room, came, went) = refs[:-3], refs[-3:]

    @pl.when(table[2, 0] == 1)
    def _():
        for s in range(SECTIONS):

            def start(r, carry):
                rows = blocks.at[table[1, r * 4 + s], :, pl.ds(half * 16, 16)]
                pltpu.make_async_copy(rows, room.at[s, r], came.at[s]).start()
                return carry

            lax.fori_loop(0, REPLICAS, start, 0, unroll=4)

        def go(s):
            out = outs[0].at[s] if len(outs) == 1 else outs[s]
            return pltpu.make_async_copy(room.at[s], out, went.at[s])

        for s in range(SECTIONS):
            pltpu.make_async_copy(room.at[s], room.at[s], came.at[s]).wait()
            go(s).start()
        for s in range(SECTIONS):
            go(s).wait()


def pack_second(half, table, blocks, after=()):
    shape = (REPLICAS, 4, 16, HID)
    split = [struct(shape, bf16)] * SECTIONS
    whole = [struct((SECTIONS, *shape), bf16)]
    outs = whole if half else split
    return call(
        functools.partial(pack_second_kernel, half),
        outs,
        [SMEM, ANY],
        [HBM] * len(outs),
        [
            pltpu.VMEM((SECTIONS, *shape), bf16),
            pltpu.SemaphoreType.DMA((4,)),
            pltpu.SemaphoreType.DMA((4,)),
        ],
        after=after,
        limit=BULK, us=4.0)(table, blocks)


def take_over_kernel(table, got, in_0, in_1, in_2, in_3, out_0, out_1, out_2, out_3, room, came, went):
    outs = (out_0, out_1, out_2, out_3)

    @pl.when(table[2, 0] == 1)
    def _():
        def come(s):
            return pltpu.make_async_copy(got.at[s], room.at[s], came.at[s])

        def go(s):
            return pltpu.make_async_copy(room.at[s], outs[s], went.at[s])

        for s in range(SECTIONS):
            come(s).start()
        for s in range(SECTIONS):
            come(s).wait()
            go(s).start()
        for s in range(SECTIONS):
            go(s).wait()


def take_over(flag, got, own):
    return call(
        take_over_kernel,
        [struct((REPLICAS, 4, 16, HID), bf16)] * 4,
        [SMEM] + [HBM] * 5,
        [HBM] * 4,
        [
            pltpu.VMEM((SECTIONS, REPLICAS, 4, 16, HID), bf16),
            pltpu.SemaphoreType.DMA((4,)),
            pltpu.SemaphoreType.DMA((4,)),
        ],
        aliases={2: 0, 3: 1, 4: 2, 5: 3},
        limit=BULK, us=4.0)(flag, got, *own)


def relay_places(busy):
    x, y, core, z = busy // 32, (busy // 8) % 4, (busy // 4) % 2, busy % 4
    found = []
    for c in (core, 1 - core):
        step = 1 + 2 * c
        for dx, dy, dz in ((0, 0, 0), (1, 0, 0), (0, 1, 0), (0, 0, 1)):
            chip = (x + dx * step) % 4 * 4 + (y + dy * step) % 4
            found.append((chip * 2 + c) * 4 + (z + dz * step) % 4)
    return found


def add_relayed_kernel(got, place, in_0, in_1, in_2, in_3, buffer, out, room, sem):
    numbers = lax.broadcasted_iota(jnp.int32, (DEVICES, 16), 0)
    lanes = lax.broadcasted_iota(jnp.int32, (DEVICES, 16), 1)
    holds = (lanes == 8) & (got[...] == 1)
    busy = jnp.max(jnp.where(holds, numbers.astype(f32), 0.0)).astype(jnp.int32)
    places = relay_places(busy)
    me = place[4] * 4 + place[3]
    for k, ref in enumerate((in_0, in_1, in_2, in_3)):

        @pl.when((places[k] == me) | (places[4 + k] == me))
        def _():
            come = pltpu.make_async_copy(ref, room, sem.at[0])
            come.start()
            come.wait()
            go = pltpu.make_async_copy(room, out.at[:, :, pl.ds(EXTRA, 16)], sem.at[1])
            go.start()
            go.wait()


def add_relayed(got, place, relays, buffer):
    return call(
        add_relayed_kernel,
        struct((REPLICAS, 4, EXTRA + 16, HID), bf16),
        [VMEM, SMEM] + [HBM] * 5,
        HBM,
        [pltpu.VMEM((REPLICAS, 4, 16, HID), bf16), pltpu.SemaphoreType.DMA((2,))],
        aliases={6: 0},
        limit=BULK, us=2.2)(got, place, *relays, buffer)


def blank_kernel(flag, out):
    pass


def blank(flag):
    return call(blank_kernel, struct((DEVICES, SECTIONS * PIECE, HID), bf16), [SMEM], HBM)(flag)


def fetch(section, place, relays, firsts, second, out, sem):
    def copy(source, target):
        pltpu.make_async_copy(source, target, sem).start()

    def rows(start):
        if not isinstance(start, int):
            start = pl.multiple_of(start, PIECE)
        return pl.ds(start, PIECE)

    for half in range(2):
        here = section // 2 == half

        def direct():
            @pl.when(place < DEVICES)
            def _():
                copy(firsts[half].at[place, rows((section - 2 * half) * PIECE)], out)

        if not isinstance(section, int):
            pl.when(here)(direct)
        elif here:
            direct()

    @pl.when(place >= DEVICES)
    def _():
        @pl.when(place < 2 * DEVICES)
        def _():
            copy(second.at[place - DEVICES, rows(section * PIECE)], out)

        @pl.when(place == 2 * DEVICES)
        def _():
            extra = pl.ds(EXTRA, 16)
            copy(firsts[1].at[relays[section], extra], out.at[pl.ds(0, 16)])
            copy(firsts[1].at[relays[section + 4], extra], out.at[pl.ds(16, 16)])


def gather_kernel(section, begin, places, relays, early, late, second, out, sem):
    def start(b, carry):
        fetch(section, places[begin + b], relays, (early, late), second, out.at[b], sem)
        return carry

    lax.fori_loop(0, HALF, start, 0, unroll=8)
    pltpu.make_async_copy(out, out, sem).wait()


def gather(section, begin, places, relays, early, late, second):
    return call(
        functools.partial(gather_kernel, section, begin),
        struct((HALF, PIECE, HID), bf16),
        [SMEM, SMEM, ANY, ANY, ANY],
        ANY,
        [pltpu.SemaphoreType.DMA], us=1.9)(places, relays, early, late, second)


def tables_kernel(lists, table, labels):
    send_slot, send_dest, send_block = lists[0:1], lists[1:2], lists[2:3]
    code = (send_slot * 128 + send_block).astype(f32)
    lanes = lax.broadcasted_iota(jnp.int32, (DEVICES, 128), 1)
    rows = lax.broadcasted_iota(jnp.int32, (DEVICES, 128), 0)
    entries = (DEVICES, lists.shape[1])
    match = send_dest == lax.broadcasted_iota(jnp.int32, entries, 0)
    low = jnp.min(jnp.where(match, code, BIG), axis=1, keepdims=True)
    high = jnp.max(jnp.where(match, code, -1.0), axis=1, keepdims=True)
    first = jnp.where(low < BIG, low, -1.0)
    second = jnp.where(high > low, high, -1.0)
    any_second = jnp.max(second, axis=0, keepdims=True) >= 0.0
    flag = jnp.broadcast_to(jnp.where(any_second, 1.0, 0.0), (8, 128))
    spare_slot = jnp.where(lanes >= NBLK, lanes - NBLK, lanes).astype(f32)
    slots, named = [], []
    for codes in (first, second):
        along = jnp.broadcast_to(codes, (DEVICES, 128)).T
        slot = jnp.floor(along * (1.0 / 128))
        slots.append(jnp.where(along >= 0.0, slot, spare_slot)[0:8])
        block = jnp.where(along >= 0.0, along - 128.0 * slot + 1.0, 0.0)
        named.append(jnp.where(rows // 4 == lanes // 4, block, 0.0).astype(bf16))
    short = lax.broadcasted_iota(jnp.int32, (8, 128), 0)
    table[...] = jnp.where(
        short == 0, slots[0], jnp.where(short == 1, slots[1], flag)
    ).astype(jnp.int32)
    d = lax.broadcasted_iota(jnp.int32, (DEVICES, 16), 0)
    j = lax.broadcasted_iota(jnp.int32, (DEVICES, 16), 1)
    total = jnp.where(j == 8, jnp.broadcast_to(flag[0:1, 0:16], (DEVICES, 16)), 0.0)
    for n, names in enumerate(named):
        pick = jnp.where(d % 4 == j - 4 * n, 1.0, 0.0).astype(bf16)
        total = total + jnp.dot(names, pick, preferred_element_type=f32)
    result = total.astype(jnp.int32)
    for k in range(OWN):
        own = jnp.broadcast_to(lists[3:4, k : k + 1], (DEVICES, 16))
        result = jnp.where(j == 9 + k, own, result)
    labels[...] = result


def send_tables(moment_dest, send_slot, send_dest, send_block):
    moments = jnp.pad(moment_dest, ((0, 0), (0, send_dest.shape[1] - moment_dest.shape[1])))
    return call(
        tables_kernel,
        [struct((8, 128), jnp.int32), struct((DEVICES, 16), jnp.int32)],
        [VMEM],
        [VMEM] * 2,
        us=1.0,
    )(jnp.concatenate([send_slot, send_dest, send_block, moments], axis=0))


def route_blocks(
    place, acts_in, cotangent, old_blocks, send_slot, send_dest, send_block, moment_dest
):
    blocks = old_blocks.reshape(NBLK, 4, PIECE, HID)
    table, labels = send_tables(moment_dest, send_slot, send_dest, send_block)

    early = pack(0, (0, 1), table, blocks)
    early, table = lax.optimization_barrier((early, table))
    (other,) = pack_second(1, table, blocks)
    table_other = from_sibling(table)
    came = from_sibling(other)
    own = pack_second(0, table, blocks, after=[other])
    mine = take_over(table_other, came, own)
    buffer = pack(0, (2, 3), table, blocks, 16)
    early = lax.all_to_all(early.reshape(DEVICES, EXTRA, HID), EVERY, 0, 0, tiled=True)
    early, labels, buffer = lax.optimization_barrier((early, labels, buffer))
    relays = [mine[0], spread(mine[1], "x"), spread(mine[2], "y"), spread(mine[3], "z")]
    got = lax.all_to_all(labels, EVERY, 0, 0, tiled=True)
    buffer = add_relayed(got, place, relays, buffer)
    layer_0, cots = quarter(acts_in, cotangent, place[3])
    buffer, got = lax.optimization_barrier((buffer, got))
    holders = got[:, 8]
    alone = jnp.sum(holders) == 1
    numbers = jnp.arange(DEVICES, dtype=jnp.int32)
    busy = jnp.sum(jnp.where(holders > 0, numbers, 0))
    busy = jnp.where(alone, busy, 0)
    relayed_by = jnp.stack(relay_places(busy)).astype(jnp.int32)
    late = lax.all_to_all(buffer.reshape(DEVICES, EXTRA + 16, HID), EVERY, 0, 0, tiled=True)

    def second_round():
        again = pack(1, tuple(range(SECTIONS)), table, blocks)
        return lax.all_to_all(
            again.reshape(DEVICES, SECTIONS * PIECE, HID), EVERY, 0, 0, tiled=True
        )

    late, table, alone_now = lax.optimization_barrier((late, table, alone))
    spare = lax.cond(alone_now, lambda: blank(table), second_round)

    wanted = jnp.arange(1, NBLK + 1, dtype=jnp.int32)[None, None, :]
    in_first = got[:, 0:4, None] == wanted
    in_second = got[:, 4:8, None] == wanted
    senders = numbers[:, None, None]
    later = jnp.where(alone, 2 * DEVICES, senders + DEVICES)
    places = jnp.sum(jnp.where(in_first, senders, 0) + jnp.where(in_second, later, 0), axis=0)
    places = jnp.clip(places, 0, 2 * DEVICES)
    weights = [
        [gather(s, begin, places[s], relayed_by, early, late, spare) for begin in (0, HALF)]
        for s in range(SECTIONS)
    ]
    return weights, got, (places.reshape(-1), relayed_by, early, late, spare), layer_0, cots


def quarter_kernel(pick, acts, cots, acts_out, cots_out):
    chosen = pick[...]
    for j in range(GROUPS):
        wide = slice(j * 512, (j + 1) * 512)
        narrow = slice(j * 128, (j + 1) * 128)
        acts_out[:, narrow] = jnp.dot(
            acts[:, wide], chosen, preferred_element_type=f32
        ).astype(bf16)
        cots_out[:, narrow] = jnp.dot(
            cots[:, wide], chosen, preferred_element_type=f32
        ).astype(bf16)


def quarter(acts, cots, q):
    rows = jnp.arange(512, dtype=jnp.int32)[:, None]
    columns = jnp.arange(128, dtype=jnp.int32)[None, :]
    pick = (rows == (columns // 32) * 128 + q * 32 + columns % 32).astype(bf16)
    return call(
        quarter_kernel,
        [struct((TOK, LOCAL), bf16)] * 2,
        [VMEM] * 3,
        [VMEM] * 2, us=1.1)(pick, acts, cots)


def flat(weight):
    return weight[...].reshape(LOCAL, HID)


def put_forward(message, layer_in, up_matrix):
    wide = layer_in.astype(f32)
    squares = jnp.sum(wide * wide, axis=1, keepdims=True)
    along = jnp.broadcast_to(squares, (TOK, 128)).T[0:16]
    high = along.astype(bf16)
    low = (along - high.astype(f32)).astype(bf16)
    row = lax.broadcasted_iota(jnp.int32, (16, 128), 0)
    both = jnp.where(row == 0, high.astype(f32), jnp.where(row == 1, low.astype(f32), 0.0))
    message[0:TOK, 0:HID] = jnp.dot(layer_in, up_matrix, preferred_element_type=f32).astype(bf16)
    message[TOK:, 0:128] = both.astype(bf16)
    message[TOK:, 128:] = jnp.zeros((16, message.shape[1] - 128), bf16)


def take_forward(total):
    along = total[TOK : TOK + 1, 0:128] + total[TOK + 1 : TOK + 2, 0:128]
    squares = jnp.broadcast_to(along, (128, 128)).T[:, 0:1]
    inverse = lax.rsqrt(squares * (1.0 / D) + rms_eps)
    pre = total[0:TOK, 0:HID] * inverse * SCALE_IN
    return pre, jax.nn.gelu(pre, approximate=True).astype(bf16), inverse


def gelu_slope(v):
    root = 0.7978845608028654
    t = jnp.tanh(root * (v + 0.044715 * v * v * v))
    return 0.5 * (1.0 + t) + 0.5 * v * (1.0 - t * t) * root * (1.0 + 0.134145 * v * v)


def times_t(a, b):
    return lax.dot_general(a, b, (((1,), (1,)), ((), ())), preferred_element_type=f32)


def summed(refs):
    return sum([ref[...].astype(f32) for ref in refs[1:]], refs[0][...].astype(f32))


def open_kernel(layer_in, weight, message):
    put_forward(message, layer_in[...], flat(weight))


def forward_kernel(layer_in, out_matrix, up_next, *refs):
    messages, (act, pre, inverse, layer_out, message) = refs[:4], refs[4:]
    result = forward_step(messages, layer_in, out_matrix, act, pre, inverse, layer_out)
    put_forward(message, result, flat(up_next))


def forward_step(messages, layer_in, out_matrix, act, pre, inverse, layer_out):
    pre_value, act_value, inverse_value = take_forward(summed(messages))
    act[...] = act_value
    pre[...] = pre_value
    inverse[...] = jnp.broadcast_to(inverse_value, (TOK, 128))
    branch = times_t(act_value, flat(out_matrix))
    result = (layer_in[...].astype(f32) + branch * SCALE_OUT).astype(bf16)
    layer_out[...] = result
    return result


def turn_kernel(layer_in, out_matrix, up_next, out_next, cots, *refs):
    messages, (act, pre, inverse, layer_out, message) = refs[:4], refs[4:]
    result = forward_step(messages, layer_in, out_matrix, act, pre, inverse, layer_out)
    put_forward(message, result, flat(up_next))
    message[0:TOK, HID:] = jnp.dot(
        cots[...], flat(out_next), preferred_element_type=f32
    ).astype(bf16)


def backward_kernel(from_forward, *refs):
    messages, refs = refs[:4], refs[4:]
    total = summed(messages)
    if from_forward:
        grad_out, layer_in, up_matrix, out_next, back, grad_in, message = refs
        pre_value, act_value, inverse_value = take_forward(total)
        back[:, LEFT:] = act_value
        grad_act = total[0:TOK, HID:] * SCALE_OUT
    else:
        act, pre, inverse, grad_out, layer_in, up_matrix, out_next, back, grad_in, message = refs
        back[:, LEFT:] = act[...]
        pre_value = pre[...]
        inverse_value = inverse[:, 0:1]
        grad_act = total * SCALE_OUT
    pulled = (grad_act * gelu_slope(pre_value)).astype(bf16)
    back[:, 0:LOCAL] = layer_in[...]
    back[:, LOCAL : 2 * LOCAL] = grad_out[...]
    back[:, 2 * LOCAL : LEFT] = (pulled.astype(f32) * inverse_value).astype(bf16)
    correction = jnp.sum(pulled.astype(f32) * pre_value, axis=1, keepdims=True) * (1.0 / D)
    grad_norm = times_t(pulled, flat(up_matrix)) * SCALE_IN
    normed = layer_in[...].astype(f32) * inverse_value
    result = grad_out[...].astype(f32) + (grad_norm - normed * correction) * inverse_value
    result = result.astype(bf16)
    grad_in[...] = result
    message[...] = jnp.dot(result, flat(out_next), preferred_element_type=f32).astype(bf16)


def close_kernel(*refs):
    messages, (act, pre, inverse, grad_out, layer_in, back) = refs[:4], refs[4:]
    grad_act = summed(messages) * SCALE_OUT
    pulled = (grad_act * gelu_slope(pre[...])).astype(bf16)
    back[:, 0:LOCAL] = layer_in[...]
    back[:, LOCAL : 2 * LOCAL] = grad_out[...]
    back[:, 2 * LOCAL : LEFT] = (pulled.astype(f32) * inverse[:, 0:1]).astype(bf16)
    back[:, LEFT:] = act[...]


def all_of(message):
    return [message] + [shift_z(message, k) for k in (1, 3, 2)]


def products(core, mine, other, small, small_sib, chosen, store):
    half = GROUPS // 2

    def product(n, right, scale, start):
        both = jnp.concatenate([small[n], small_sib[n]], axis=0)
        turned = both.astype(f32).T.astype(bf16)
        for g in range(half):
            columns = pl.ds(pl.multiple_of(right + (2 * g + core) * 128, 128), 128)
            chosen[0:TOK, g * 128 : (g + 1) * 128] = mine[:, columns]
            chosen[TOK:, g * 128 : (g + 1) * 128] = other[:, columns]
        result = jnp.dot(turned, chosen[...], preferred_element_type=f32) * scale
        for g in range(half):
            store(start + g, result[:, g * 128 : (g + 1) * 128].astype(bf16))

    product(0, 0, SCALE_IN, 0)
    product(1, LOCAL, SCALE_OUT, half)
    for owner in range(2 * half, 16):
        store(owner, jnp.zeros((HID, 128), bf16))


def deal(x_first, place, table, outs):
    for k in range(4):
        for j in range(4):
            if x_first:
                owner = lax.rem(place[0] + k, 4) * 4 + j
            else:
                owner = j * 4 + lax.rem(place[1] + k, 4)
            outs[k][j] = table[owner]


def gradient_kernel(x_first, count, place, *refs):
    ins, outs, (chosen, table) = refs[: 2 * count], refs[2 * count : 2 * count + 4], refs[-2:]
    for n in range(count):

        def store(owner, value):
            table[owner, n] = value

        mine, other = ins[2 * n : 2 * n + 2]
        small, small_sib = [
            [ref[:, 2 * LOCAL : LEFT], ref[:, LEFT:]] for ref in (mine, other)
        ]
        products(place[2], mine, other, small, small_sib, chosen, store)
    deal(x_first, place, table, outs)


def table_kernel(place, mine, other, table, chosen):
    def store(owner, value):
        table[owner] = value

    small, small_sib = [[ref[:, 2 * LOCAL : LEFT], ref[:, LEFT:]] for ref in (mine, other)]
    products(place[2], mine, other, small, small_sib, chosen, store)


def last_gradient_kernel(place, earlier, mine, other, *refs):
    outs, (chosen, table) = refs[:4], refs[4:]

    def store(owner, value):
        table[owner, 1] = value

    for owner in range(16):
        table[owner, 0] = earlier[owner]
    small, small_sib = [[ref[:, 2 * LOCAL : LEFT], ref[:, LEFT:]] for ref in (mine, other)]
    products(place[2], mine, other, small, small_sib, chosen, store)
    deal(False, place, table, outs)


def last_half(place, arrays):
    chunks = call(
        last_gradient_kernel,
        [struct((4, 2, HID, 128), bf16)] * 4,
        [SMEM] + [VMEM] * 3,
        [VMEM] * 4,
        [pltpu.VMEM((2 * TOK, LOCAL // 2), bf16), pltpu.VMEM((16, 2, HID, 128), bf16)],
        us=2.0,
    )(place, *arrays)
    return [chunks[0]] + [shift_xy(chunks[k], 0, k) for k in (1, 2, 3)]


def halve_kernel(x_first, counts, place, *refs):
    mine = place[1] if x_first else place[0]
    outs = refs[4 * len(counts) :]
    for k in range(4):
        chunk = lax.rem(mine + k, 4)
        start = 0
        for n, count in enumerate(counts):
            four = refs[4 * n : 4 * n + 4]
            total = sum([ref[chunk].astype(f32) for ref in four[1:]], four[0][chunk].astype(f32))
            outs[k][start : start + count] = total.astype(outs[k].dtype)
            start += count


def first_half(x_first, place, sections, after=()):
    count = len(sections)
    chunks = call(
        functools.partial(gradient_kernel, x_first, count),
        [struct((4, count, HID, 128), bf16)] * 4,
        [SMEM] + [VMEM] * (2 * count),
        [VMEM] * 4,
        [pltpu.VMEM((2 * TOK, LOCAL // 2), bf16), pltpu.VMEM((16, count, HID, 128), bf16)],
        after=after, us=3.3)(place, *[v for section in sections for v in section])
    step = (1, 0) if x_first else (0, 1)
    return [chunks[0]] + [shift_xy(chunks[k], k * step[0], k * step[1]) for k in (1, 2, 3)]


def second_half(x_first, place, parts, after):
    counts = [part[0].shape[1] for part in parts]
    count = sum(counts)
    kept, *sends = call(
        functools.partial(halve_kernel, x_first, counts),
        [struct((count, HID, 128), f32)] + [struct((count, HID, 128), bf16)] * 3,
        [SMEM] + [VMEM] * (4 * len(parts)),
        [VMEM] * 4,
        after=after, us=1.4)(place, *[v for part in parts for v in part])
    step = (0, 1) if x_first else (1, 0)
    return [kept] + [shift_xy(sends[k - 1], k * step[0], k * step[1]) for k in (1, 2, 3)]


def finish_kernel(places_in, place, *refs):
    groups, refs = refs[: 4 * len(places_in)], refs[4 * len(places_in) :]
    kept, sends, table = refs[0], refs[1:4], refs[4]
    for m, sections in enumerate(places_in):
        four = groups[4 * m : 4 * m + 4]
        for n, section in enumerate(sections):
            table[section] = sum([ref[n].astype(f32) for ref in four[1:]], four[0][n])
    for k in range(4):
        value = table[lax.rem(place[3] + k, 4)]
        if k == 0:
            kept[...] = value
        else:
            sends[k - 1][...] = value.astype(bf16)


def split_moments_kernel(place, first, second, *outs):
    for k in range(4):
        rows = pl.ds(pl.multiple_of(lax.rem(place[3] + k, 4) * PIECE, PIECE), PIECE)
        for a in range(OWN):
            outs[k][0, a] = first[a, rows, :].astype(bf16)
            outs[k][1, a] = second[a, rows, :].astype(bf16)


def order_kernel(place, source, places, relays, early, late, second, *refs):
    moments, outs, (table, came, sem) = refs[:4], refs[4:8], refs[8:]
    start = jnp.minimum(place[4], REAL_OWNERS - 1) * OWN
    for k in range(4):
        section = lax.rem(place[3] + k, 4)
        for i in range(OWN):
            held = places[section * NBLK + start + i]
            fetch(section, held, relays, (early, late), second, came.at[k, i], sem)
    for k in range(4):
        table[k] = moments[k][...]
    for k in range(4):
        section = lax.rem(place[3] + k, 4)
        for i in range(OWN):
            held = source[section * OWN + i]
            outs[k][1, i] = table[held // OWN, 0, lax.rem(held, OWN)]
            outs[k][2, i] = table[held // OWN, 1, lax.rem(held, OWN)]
    pltpu.make_async_copy(came, came, sem).wait()
    for k in range(4):
        outs[k][0] = came[k]


def adam_kernel(place, *refs):
    gradients, held = refs[:4], refs[4:8]
    weight_out, first_out, second_out = refs[8:]
    real = place[4] < REAL_OWNERS
    for k in range(4):
        q = lax.rem(place[3] + 4 - k, 4)
        rows = pl.ds(pl.multiple_of(q * PIECE, PIECE), PIECE)
        turned = jnp.where(real, gradients[k][...].astype(f32).T, 0.0)
        for i in range(OWN):
            gradient = turned[i * PIECE : (i + 1) * PIECE, :]
            weight = jnp.where(real, held[k][0, i].astype(f32), 0.0)
            first = beta_first * held[k][1, i].astype(f32) + (1.0 - beta_first) * gradient
            second = beta_second * held[k][2, i].astype(f32) + (
                (1.0 - beta_second) * gradient * gradient
            )
            first_out[i, rows, :] = first
            second_out[i, rows, :] = second
            weight_out[i, rows, :] = (
                weight - step_size * first / (jnp.sqrt(second) + adam_eps)
            ).astype(bf16)


def on_device(
    acts_in,
    cotangent,
    old_blocks,
    send_slot,
    send_dest,
    send_block,
    old_first,
    old_second,
    moment_dest,
):
    me_r = lax.axis_index("replica")
    me_z = lax.axis_index("section")
    place = jnp.stack([me_r // 8, (me_r // 2) % 4, me_r % 2, me_z, me_r]).astype(jnp.int32)

    split = call(
        split_moments_kernel,
        [struct((2, OWN, PIECE, HID), bf16)] * 4,
        [SMEM, VMEM, VMEM],
        [VMEM] * 4, us=1.3)(place, old_first[0], old_second[0])
    pieces = [split[0]] + [shift_z(split[k], k) for k in (1, 2, 3)]

    weights, labels, arrivals, layer_0, cots = route_blocks(
        place, acts_in, cotangent, old_blocks, send_slot, send_dest, send_block, moment_dest
    )
    table = lax.dynamic_slice_in_dim(labels, me_r * 4, 4, 0)[:, 9:13]
    distance = (me_z - jnp.arange(SECTIONS, dtype=jnp.int32)) % 4
    held = (distance[:, None] * OWN + jnp.arange(OWN, dtype=jnp.int32)[None, :]).reshape(-1)
    slots = jnp.arange(SECTIONS * OWN, dtype=jnp.int32)
    source = jnp.sum(jnp.where(table.reshape(1, -1) == slots[:, None], held[None, :], 0), axis=1)
    message = call(
        open_kernel, struct((TOK + 16, HID), bf16), [VMEM] * 2, VMEM, us=0.3)(layer_0, weights[0][0])
    layers = [layer_0]
    acts, pres, inverses = [], [], []
    wide = struct((TOK, LEFT + HID), bf16)
    short = struct((TOK, HID), bf16)
    narrow = struct((TOK, LOCAL), bf16)
    for s in range(SECTIONS - 1):
        messages = all_of(message)
        turn = s == SECTIONS - 2
        extra = (weights[s + 1][1], cots) if turn else ()
        act, pre, inverse, layer, message = call(
            turn_kernel if turn else forward_kernel,
            [
                short,
                struct((TOK, HID), f32),
                struct((TOK, 128), f32),
                narrow,
                struct((TOK + 16, 2 * HID if turn else HID), bf16),
            ],
            [VMEM] * (7 + len(extra)),
            [VMEM] * 5,
            after=() if s else pieces[1:],
        )(layers[s], weights[s][1], weights[s + 1][0], *extra, *messages)
        layers.append(layer)
        acts.append(act)
        pres.append(pre)
        inverses.append(inverse)

    ordered = call(
        order_kernel,
        [struct((3, OWN, PIECE, HID), bf16)] * 4,
        [SMEM] * 4 + [ANY] * 3 + [VMEM] * 4,
        [VMEM] * 4,
        [
            pltpu.VMEM((4, 2, OWN, PIECE, HID), bf16),
            pltpu.VMEM((4, OWN, PIECE, HID), bf16),
            pltpu.SemaphoreType.DMA,
        ], us=1.6)(place, source, *arrivals, *pieces)
    owned = [ordered[0]] + [shift_z(ordered[k], k) for k in (1, 2, 3)]

    grad = cots
    ready = [None] * SECTIONS
    after = []
    for s in reversed(range(SECTIONS)):
        messages = all_of(message)
        if s == SECTIONS - 1:
            back, grad, message = call(
                functools.partial(backward_kernel, True),
                [wide, narrow, short],
                [VMEM] * 8,
                [VMEM] * 3,
                after=after,
            )(*messages, grad, layers[s], weights[s][0], weights[s - 1][1])
        elif s > 0:
            back, grad, message = call(
                functools.partial(backward_kernel, False),
                [wide, narrow, short],
                [VMEM] * 11,
                [VMEM] * 3,
                after=after,
            )(
                *messages, acts[s], pres[s], inverses[s], grad, layers[s], weights[s][0],
                weights[s - 1][1]
            )
        else:
            back = call(close_kernel, wide, [VMEM] * 9, VMEM, after=after)(
                *messages, acts[0], pres[0], inverses[0], grad, layers[0]
            )
        ready[s] = (back, from_sibling(back))
        if s == 3:
            after = []
        elif s == 2:
            after = [ready[2][1], ready[3][1]]
        elif s == 1:
            odd = first_half(True, place, [ready[3], ready[1]])
            earlier = call(
                table_kernel,
                struct((16, HID, 128), bf16),
                [SMEM] + [VMEM] * 2,
                VMEM,
                [pltpu.VMEM((2 * TOK, LOCAL // 2), bf16)],
                us=1.6,
            )(place, *ready[2])
            after = [odd[0], earlier]
        else:
            even = last_half(place, (earlier, *ready[0]))
            after = even[:1]
    across = second_half(True, place, [odd], [*after, ordered[0]])
    along = second_half(False, place, [even], after)
    kept, *sends = call(
        functools.partial(finish_kernel, ((3, 1), (2, 0))),
        [struct((HID, 128), f32)] + [struct((HID, 128), bf16)] * 3,
        [SMEM] + [VMEM] * 8,
        [VMEM] * 4,
        [pltpu.VMEM((SECTIONS, HID, 128), f32)], us=0.7)(place, *across, *along)
    gradients = [kept] + [shift_z(sends[k - 1], k) for k in (1, 2, 3)]
    new_weight, new_first, new_second = call(
        adam_kernel,
        [
            struct((OWN, 128, HID), bf16),
            struct((OWN, 128, HID), f32),
            struct((OWN, 128, HID), f32),
        ],
        [SMEM] + [VMEM] * 8,
        [VMEM] * 3, us=2.1)(place, *gradients, *owned)
    return (new_weight[None], new_first[None], new_second[None])


def solution(mesh):
    in_specs = (
        P("replica", None),
        P("replica", None),
        P(("replica", "section"), None, None, None),
        P(("replica", "section"), None),
        P(("replica", "section"), None),
        P(("replica", "section"), None),
        P(("replica", "section"), None, None, None),
        P(("replica", "section"), None, None, None),
        P(("replica", "section"), None),
    )
    out_specs = (
        P("section", "replica", None, None),
        P("section", "replica", None, None),
        P("section", "replica", None, None),
    )
    return jax.shard_map(
        on_device, mesh=mesh, in_specs=in_specs, out_specs=out_specs, check_vma=False
    )
```
